128 devices in a mesh: section: 2 (over z_lo), dp: 16 (over x, y), tensor: 4 (over z_hi, core).
Axes of the slice: x: 4, y: 4, z: 4 (z_hi: 2, z_lo: 2; z = z_hi * 2 + z_lo), core: 2. Of those that a mesh axis runs over, the one named last changes fastest.
Arguments:
- tokens: bfloat16 [8192, 1024], P('dp'), may hold values from -6 to 6
- lengths: int32 [32, 4], P('dp'), may hold values from 1 to 170, 256 in all within a row
- cotangent: bfloat16 [8192, 1024], P('dp'), may hold values from -6 to 6
- qkv_weight: bfloat16 [2, 1024, 3, 1024], P('section', None, None, 'tensor'), may hold values from -0.1875 to 0.1875
- out_weight: bfloat16 [2, 1024, 1024], P('section', 'tensor'), may hold values from -1.5 to 1.5
- up_weight: bfloat16 [2, 1024, 4096], P('section', None, 'tensor'), may hold values from -0.1875 to 0.1875
- down_weight: bfloat16 [2, 4096, 1024], P('section', 'tensor'), may hold values from -0.09375 to 0.09375
- norm_gains: float32 [2, 2, 1024], P('section'), may hold values from 0.1 to 1.9
- feat_weights: float32 [2, 16, 64], P('section', 'tensor'), may hold values from 0.25 to 4
Outputs:
- acts: bfloat16 [2, 8192, 1024], P('section', 'dp')
- in_grads: float32 [2, 8192, 1024], P('section', 'dp')
- qkv_grad: float32 [2, 1024, 3, 1024], P('section', None, None, 'tensor')
- out_grad: float32 [2, 1024, 1024], P('section', 'tensor')
- up_grad: float32 [2, 1024, 4096], P('section', None, 'tensor')
- down_grad: float32 [2, 4096, 1024], P('section', 'tensor')
- gain_grad: float32 [2, 2, 1024], P('section')
- feat_grad: float32 [2, 16, 64], P('section', 'tensor')
The draws below stay inside these ranges and needn't reach their ends.
Inputs may be any that keep to these rules, and one draw needn't show every extreme that they name: `lengths`: row r describes micro-batch r % 2 of index r // 2 of dp: the 4 sequences packed one after another into its 256 tokens, which they fill exactly.
All inputs are finite; a program needn't handle non-finite values.
Results may differ from the reference program's by a relative error of at most 0.033.
Values may be sent and summed in bfloat16 or wider, within the bound.
A program may use at most 192 MiB of HBM per device.

```python
import math
import jax
import jax.numpy as jnp
import numpy as np
from jax import lax

D = 1024
HEADS = 16
HEAD_DIM = 64
ROT = 16
FF = 4096
FEATS = 64
BLK = 64
MICROS = 2
SEQS = 4
MICRO_TOK = 256
SEQ_MOST = 170
LAYERS = 2
TOKENS = 8192
N_DP = 16
N_TENSOR = 4


def steps_of(key, extent, cuts, least, largest):
    level, own = 1.0, jax.random.fold_in(key, 6)
    for dim, shards_of in cuts:
        steps = jnp.exp(jax.random.uniform(jax.random.fold_in(own, dim), (shards_of,), jnp.float32, least / len(cuts), largest / len(cuts)))
        level = level * jnp.repeat(steps, extent[dim] // shards_of).reshape([-1 if axis == dim else 1 for axis in range(len(extent))])
    return level


def length_profile(count, total, bound, slope):
    portions = [(1 << 20) // math.isqrt(rank ** slope) + 1 for rank in range(2, count + 1)]
    surplus, given = total - bound - (count - 1), [1] * (count - 1)
    while surplus > 0:
        candidates = [i for i in range(count - 1) if given[i] < bound]
        whole, left = sum([portions[i] for i in candidates]), surplus
        for i in candidates:
            more = min(bound - given[i], max(1, left * portions[i] // whole), surplus)
            given[i] = given[i] + more
            surplus = surplus - more
    return np.array([bound] + given)


def ragged_sizes(rng, number_of, total, most, skew):
    if number_of == 2:
        one = jax.random.randint(rng, (), max(1, total - most), min(most, total - 1) + 1)
        return jnp.stack([one, total - one])
    tallies = jnp.asarray(length_profile(number_of, total, most, skew), jnp.int32)
    twos = (number_of - 1) // 2
    donor, receiver = tallies[1:1 + 2 * twos:2], tallies[2:2 + 2 * twos:2]
    room = jnp.minimum(donor - 1, most - receiver)
    moved = jax.random.randint(jax.random.fold_in(rng, 1), (twos,), 0, 1 << 20) % (room + 1)
    tallies = tallies.at[1:1 + 2 * twos:2].set(donor - moved).at[2:2 + 2 * twos:2].set(receiver + moved)
    return tallies[jax.random.permutation(jax.random.fold_in(rng, 2), number_of)]


def gaussian(stream_key, extent, deviation, limit, cuts=(), kind=jnp.bfloat16):
    result = deviation * jax.random.normal(stream_key, extent, jnp.float32)
    if cuts:
        result = result * steps_of(stream_key, extent, cuts, -0.22, 0.18)
    return jnp.clip(result, -limit, limit).astype(kind)


def setup_inputs(seed: int = 0) -> dict:
    key_list = jax.random.split(jax.random.key(seed), 10)
    tokens = gaussian(key_list[0], (TOKENS, D), 1.0, 6.0, ((0, 16),))
    lengths = jax.vmap(lambda own: ragged_sizes(own, SEQS, MICRO_TOK, SEQ_MOST, 2))(jax.random.split(key_list[1], (N_DP * MICROS))).reshape((N_DP * MICROS, SEQS)).astype(jnp.int32)
    cotangent = gaussian(key_list[2], (TOKENS, D), 1.0, 6.0, ((0, 16),))
    qkv_weight = gaussian(key_list[3], (LAYERS, D, 3, D), D ** -0.5, 0.1875, ((0, 2), (3, 4)))
    out_weight = gaussian(key_list[4], (LAYERS, D, D), (max(D // 64, 1)) ** -0.5, 1.5, ((0, 2), (1, 4)))
    up_weight = gaussian(key_list[5], (LAYERS, D, FF), D ** -0.5, 0.1875, ((0, 2), (2, 4)))
    down_weight = gaussian(key_list[6], (LAYERS, FF, D), FF ** -0.5, 0.09375, ((0, 2), (1, 4)))
    norm_gains = jnp.clip(1.0 + 0.18 * jax.random.normal(key_list[7], (LAYERS, 2, D), jnp.float32), 0.1, 1.9)
    feat_weights = jnp.clip(jnp.exp(math.log(4.0) - 2.7725887 * jax.random.uniform(key_list[8], (LAYERS, HEADS, FEATS), jnp.float32) ** steps_of(key_list[8], (LAYERS, HEADS, FEATS), ((0, 2), (1, 4)), -0.2, 0.2)), 0.25, 4.0)
    return dict(tokens=tokens, lengths=lengths, cotangent=cotangent, qkv_weight=qkv_weight, out_weight=out_weight, up_weight=up_weight, down_weight=down_weight, norm_gains=norm_gains, feat_weights=feat_weights)


@jax.custom_vjp
def low(v):
    return lax.optimization_barrier(v.astype(jnp.bfloat16)).astype(jnp.float32)

@jax.custom_vjp
def low_back(v):
    return v

def low_keep(v):
    return (low(v), None)

def low_pass(kept, grad):
    return (grad,)

def back_keep(v):
    return (v, None)

def back_low(kept, grad):
    return (low(grad),)
low.defvjp(low_keep, low_pass)
low_back.defvjp(back_keep, back_low)
HIGHEST = lax.Precision.HIGHEST
norm_eps = 1e-05

def feature_table(head_dim, feat_count):
    golden = 0.6180339887498949
    row_grid = np.arange(feat_count)[:, None] + 0.5
    columns = np.arange(head_dim)[None, :] * 1.0
    points = np.mod(row_grid * (2.0 * columns + 1.0) / feat_count + golden * columns, 1.0)
    radius = np.sqrt(-2.0 * np.log(points[:, 0::2]))
    turning = 2.0 * np.pi * points[:, 1::2]
    omega_rows = np.stack([radius * np.cos(turning), radius * np.sin(turning)], axis=2).reshape(feat_count, head_dim)
    frequency = np.arange(head_dim)[:, None] * 1.0
    cosine_basis = np.sqrt(2.0 / head_dim) * np.cos(np.pi * (2.0 * columns + 1.0) * frequency / (2.0 * head_dim))
    cosine_basis = np.where(frequency == 0, np.sqrt(0.5), 1.0) * cosine_basis
    return np.sum(omega_rows[:, :, None] * cosine_basis[None, :, :], axis=1)

def documents(length_row, token_count):
    seq_ends = jnp.cumsum(length_row, dtype=jnp.int32)
    starts = seq_ends - length_row
    places = jnp.arange(token_count, dtype=jnp.int32)
    doc_index = lax.optimization_barrier(jnp.sum((places[:, None] >= seq_ends[None, :]).astype(jnp.int32), axis=1, dtype=jnp.int32))
    belongs = doc_index[:, None] == jnp.arange(length_row.shape[0], dtype=jnp.int32)[None, :]
    positions = places - lax.optimization_barrier(jnp.sum(jnp.where(belongs, starts[None, :], 0), axis=1, dtype=jnp.int32))
    return (doc_index, positions)

def rotation(positions, rot_dims):
    half_rot = rot_dims // 2
    inverse = 10000.0 ** (-2.0 * jnp.arange(half_rot, dtype=jnp.float32) / rot_dims)
    angles = positions.astype(jnp.float32)[:, None] * inverse[None, :]
    return (jnp.cos(angles), jnp.sin(angles))

def rotate(vectors, cosine, sine_part, rot_dims):
    half_rot = rot_dims // 2
    leading = vectors[..., :half_rot]
    trailing = vectors[..., half_rot:rot_dims]
    cosine = cosine[:, None, :]
    sine_part = sine_part[:, None, :]
    return jnp.concatenate([leading * cosine - trailing * sine_part, trailing * cosine + leading * sine_part, vectors[..., rot_dims:]], axis=-1)

def feature_maps(turned, feat_table, feat_scale):
    head_dim = turned.shape[-1]
    projections = jnp.einsum('thd,md->thm', turned, feat_table, precision=HIGHEST)
    squares = lax.optimization_barrier(jnp.sum(turned * turned, axis=-1, keepdims=True))
    return feat_scale[None] * jnp.exp(projections / math.sqrt(head_dim) - squares / (2.0 * head_dim))

def causal_blocks(query_feats, key_feats, value_low, doc_index, rounder):
    token_count, head_count, feat_count = query_feats.shape
    head_dim = value_low.shape[-1]
    block_count = token_count // BLK
    query_blocks = query_feats.reshape(block_count, BLK, head_count, feat_count)
    key_blocks = key_feats.reshape(block_count, BLK, head_count, feat_count)
    value_blocks = value_low.reshape(block_count, BLK, head_count, head_dim)
    doc_blocks = doc_index.reshape(block_count, BLK)
    offsets_in_block = jnp.arange(BLK, dtype=jnp.int32)
    within = (doc_blocks[:, :, None] == doc_blocks[:, None, :]) & (offsets_in_block[:, None] >= offsets_in_block[None, :])[None]
    scores = jnp.einsum('cihm,cjhm->chij', query_blocks, key_blocks, precision=HIGHEST) * within[:, None].astype(jnp.float32)
    near_weighted = jnp.einsum('chij,cjhv->cihv', rounder(scores), value_blocks, precision=HIGHEST)
    near_norm = jnp.transpose(lax.optimization_barrier(jnp.sum(scores, axis=-1)), (0, 2, 1))
    lead_doc = doc_blocks[:, 0]
    next_doc = jnp.concatenate([lead_doc[1:], jnp.full((1,), -1, jnp.int32)])

    def carry_step(carried, pieces):
        state_sum, key_total = carried
        keys_blk, vals_blk, docs_blk, lead_one, next_one = pieces
        chosen = (docs_blk == next_one).astype(jnp.float32)[:, None, None]
        keep_flag = (lead_one == next_one).astype(jnp.float32)
        new_state = keep_flag * state_sum + jnp.einsum('jhm,jhv->hmv', keys_blk * chosen, vals_blk, precision=HIGHEST)
        new_total = keep_flag * key_total + lax.optimization_barrier(jnp.sum(keys_blk * chosen, axis=0))
        return ((new_state, new_total), (state_sum, key_total))
    initial = (jnp.zeros((head_count, feat_count, head_dim), jnp.float32), jnp.zeros((head_count, feat_count), jnp.float32))
    _, (states, totals) = lax.scan(jax.checkpoint(carry_step), initial, (key_blocks, value_blocks, doc_blocks, lead_doc, next_doc))
    live_rows = (doc_blocks == lead_doc[:, None]).astype(jnp.float32)
    far_weighted = jnp.einsum('cihm,chmv->cihv', query_blocks, states, precision=HIGHEST)
    far_norm = jnp.einsum('cihm,chm->cih', query_blocks, totals, precision=HIGHEST)
    numerator = near_weighted + live_rows[:, :, None, None] * far_weighted
    denominator = near_norm + live_rows[:, :, None] * far_norm
    return (numerator / denominator[..., None]).reshape(token_count, head_count, head_dim)

def attend(projected, feat_scale, doc_index, cosine, sine_part, feat_table, rounder):
    token_count = projected.shape[0]
    head_count = feat_scale.shape[0]
    head_split = projected.reshape(token_count, 3, head_count, -1)
    queries = rotate(head_split[:, 0], cosine, sine_part, ROT)
    keys_turned = rotate(head_split[:, 1], cosine, sine_part, ROT)
    query_feats = rounder(feature_maps(queries, feat_table, feat_scale))
    key_feats = rounder(feature_maps(keys_turned, feat_table, feat_scale))
    value_low = rounder(head_split[:, 2])
    return causal_blocks(query_feats, key_feats, value_low, doc_index, rounder).reshape(token_count, -1)

def layer_apply(inputs, weights, layer_number, context):
    qkv_matrix = weights[0][layer_number]
    out_matrix = weights[1][layer_number]
    up_matrix = weights[2][layer_number]
    down_matrix = weights[3][layer_number]
    norm_gain = weights[4][layer_number]
    feat_scale = weights[5][layer_number]
    doc_index, cosine, sine_part, feat_table = context
    mean_row = lax.optimization_barrier(jnp.mean(inputs, axis=-1, keepdims=True))
    centered = inputs - mean_row
    normed = centered * lax.rsqrt(lax.optimization_barrier(jnp.mean(centered * centered, axis=-1, keepdims=True)) + norm_eps)
    attn_in = low(normed * norm_gain[0])
    mlp_in = low(normed * norm_gain[1])
    projected = low_back(jnp.einsum('td,dsk->tsk', attn_in, qkv_matrix, precision=HIGHEST))
    attended = attend(projected, feat_scale, doc_index, cosine, sine_part, feat_table, low)
    mixed_heads = low_back(low(attended))
    hidden_pre = low_back(jnp.dot(mlp_in, up_matrix, precision=HIGHEST))
    hidden = low(jax.nn.gelu(hidden_pre, approximate=False))
    row_count = inputs.shape[0]
    model_width = inputs.shape[1]
    mixed_groups = mixed_heads.reshape(row_count, N_TENSOR, -1)
    out_groups = out_matrix.reshape(N_TENSOR, -1, model_width)
    hidden_groups = hidden.reshape(row_count, N_TENSOR, -1)
    down_groups = down_matrix.reshape(N_TENSOR, -1, model_width)
    partials = jnp.einsum('tgk,gkd->gtd', mixed_groups, out_groups, precision=HIGHEST)
    partials = partials + jnp.einsum('tgf,gfd->gtd', hidden_groups, down_groups, precision=HIGHEST)
    branch = low_back(lax.optimization_barrier(jnp.sum(low(partials), axis=0)))
    return inputs + branch

def reference(tokens, lengths, cotangent, qkv_weight, out_weight, up_weight, down_weight, norm_gains, feat_weights):
    feat_table = jnp.asarray(feature_table(HEAD_DIM, FEATS), jnp.float32)
    parameters = (qkv_weight.astype(jnp.float32), out_weight.astype(jnp.float32), up_weight.astype(jnp.float32), down_weight.astype(jnp.float32), norm_gains.astype(jnp.float32), feat_weights.astype(jnp.float32))
    pack_count = N_DP * MICROS
    token_packs = tokens.astype(jnp.float32).reshape(pack_count, MICRO_TOK, D)
    cot_packs = cotangent.astype(jnp.float32).reshape(pack_count, MICRO_TOK, D)

    def pack_step(totals, pieces):
        token_pack, cot_pack, length_row = pieces
        doc_index, positions = documents(length_row, MICRO_TOK)
        cosine, sine_part = rotation(positions, ROT)
        context = (doc_index, cosine, sine_part, feat_table)

        def forward(first_in, offset, weights):
            first_out = layer_apply(first_in, weights, 0, context)
            second_in = low_back(low(first_out)) + offset
            second_out = layer_apply(second_in, weights, 1, context)
            return (first_out, second_out)
        (first_out, second_out), pullback = jax.vjp(forward, token_pack, jnp.zeros_like(token_pack), parameters)
        grad_first, grad_offset, grad_params = pullback((jnp.zeros_like(first_out), cot_pack))
        totals = jax.tree.map(jnp.add, totals, grad_params)
        return (totals, (first_out.astype(jnp.bfloat16), second_out.astype(jnp.bfloat16), grad_first, grad_offset))
    zero_totals = jax.tree.map(jnp.zeros_like, parameters)
    totals, (firsts, seconds, grads_first, grads_second) = lax.scan(pack_step, zero_totals, (token_packs, cot_packs, lengths))
    acts = jnp.stack([firsts.reshape(TOKENS, D), seconds.reshape(TOKENS, D)])
    in_grads = jnp.stack([grads_first.reshape(TOKENS, D), grads_second.reshape(TOKENS, D)])
    return (acts, in_grads, totals[0], totals[1], totals[2], totals[3], totals[4], totals[5])
```

```python
import functools
import math

import jax
import jax.numpy as jnp
import numpy as np
from jax import lax
from jax.experimental import pallas as pl
from jax.experimental.pallas import tpu as pltpu
from jax.sharding import PartitionSpec as P

F32 = jnp.float32
BF16 = jnp.bfloat16
MESH = pl.DeviceIdType.MESH
EPS = 1e-05
ROWS = 256
HALF = 128
WIDTH = 1024
LOCAL = 256
HEADS = 4
DIM = 64
ROT = 16
MICROS = 2
ALL_ROWS = MICROS * ROWS


def feature_table(head_dim, feat_count):
    golden = 0.6180339887498949
    row_grid = np.arange(feat_count)[:, None] + 0.5
    columns = np.arange(head_dim)[None, :] * 1.0
    points = np.mod(row_grid * (2.0 * columns + 1.0) / feat_count + golden * columns, 1.0)
    radius = np.sqrt(-2.0 * np.log(points[:, 0::2]))
    turning = 2.0 * np.pi * points[:, 1::2]
    omega_rows = np.stack([radius * np.cos(turning), radius * np.sin(turning)], axis=2).reshape(
        feat_count, head_dim
    )
    frequency = np.arange(head_dim)[:, None] * 1.0
    cosine_basis = np.sqrt(2.0 / head_dim) * np.cos(
        np.pi * (2.0 * columns + 1.0) * frequency / (2.0 * head_dim)
    )
    cosine_basis = np.where(frequency == 0, np.sqrt(0.5), 1.0) * cosine_basis
    return np.sum(omega_rows[:, :, None] * cosine_basis[None, :, :], axis=1)


def low_pieces(values):
    high = values.astype(BF16)
    rest = (values - high.astype(values.dtype)).astype(BF16)
    return high, rest


def constants():
    table = feature_table(DIM, DIM).astype(np.float32)
    eye = np.eye(HEADS, dtype=np.float32)
    blocks = np.kron(eye, table.T / math.sqrt(DIM)).astype(np.float32)
    ones = np.kron(eye, np.ones((DIM, DIM), np.float32))
    high, rest = low_pieces(blocks)
    scaled = (ones * (-1.0 / (2.0 * DIM))).astype(BF16)
    forward = np.concatenate([high, high, rest, scaled, scaled], axis=0)
    backward = np.concatenate([blocks.T.astype(BF16), (ones / DIM).astype(BF16)], axis=1)
    half_rot = ROT // 2
    inverse = (10000.0 ** (-2.0 * np.arange(half_rot) / ROT)).astype(np.float32)
    angles = np.arange(ROWS, dtype=np.float32)[:, None] * inverse[None, :]
    cosine = np.ones((ROWS, DIM), np.float32)
    sine = np.zeros((ROWS, DIM), np.float32)
    for start in (0, half_rot):
        cosine[:, start : start + half_rot] = np.cos(angles.astype(np.float64))
        sine[:, start : start + half_rot] = np.sin(angles.astype(np.float64))
    cosine = np.tile(cosine, (1, HEADS))
    sine = np.tile(sine, (1, HEADS))
    turns = np.concatenate([*low_pieces(cosine), *low_pieces(sine)], axis=1)
    return forward, backward, ones.astype(BF16), turns


def dot_nn(a, b):
    return lax.dot_general(a, b, (((1,), (0,)), ((), ())), preferred_element_type=F32)


def dot_nt(a, b):
    return lax.dot_general(a, b, (((1,), (1,)), ((), ())), preferred_element_type=F32)


def dot_tn(a, b):
    return lax.dot_general(a, b, (((0,), (0,)), ((), ())), preferred_element_type=F32)


def ln_rows(x):
    mean = jnp.mean(x, axis=-1, keepdims=True)
    centered = x - mean
    inv = lax.rsqrt(jnp.mean(centered * centered, axis=-1, keepdims=True) + EPS)
    return centered * inv, inv


def ln_back(combined, normed, inv):
    mean_c = jnp.mean(combined, axis=-1, keepdims=True)
    mean_p = jnp.mean(combined * normed, axis=-1, keepdims=True)
    return inv * (combined - mean_c - normed * mean_p)


def relay_kernel(
    lens, tok, cot, wqkv, wout, wup, wdown, gains, fw, cfwd, cbwd, cones, cturn,
    acts, in_grads, grads, small,
    mask, rot, xin, glow, nrm, attn_in, mlp_in, tq, tk, pq, pk, qf, kf, vf, sb, den, att,
    mixed, hidden, gp, gh, gm, gproj, gpre,
    fpart, frx, fcs, fin, bpart, brx, bcs, bin_, xrx, srx,
    frx_s, fin_s, facts_s, brx_s, bin_s, bout_s, x_s, xsib_s, small_s,
):
    s = lax.axis_index("section")
    t = lax.axis_index("tensor")
    zh = t // 2
    c = lax.rem(t, 2)
    sibling = {"tensor": zh * 2 + 1 - c}
    partner = {"tensor": lax.rem(t + 2, 4)}
    across = [{"section": 1 - s, "tensor": z * 2 + c} for z in range(2)]

    barrier = pltpu.get_barrier_semaphore()
    for target in (sibling, partner, *across):
        pl.semaphore_signal(barrier, inc=1, device_id=target, device_id_type=MESH)
    pl.semaphore_wait(barrier, 4)

    def remote(src, dst, sems, index, target):
        return pltpu.make_async_remote_copy(
            src_ref=src, dst_ref=dst, send_sem=sems.at[(0, *index)],
            recv_sem=sems.at[(1, *index)], device_id=target, device_id_type=MESH,
        )

    def micro_rows(m):
        return pl.ds(pl.multiple_of(m * ROWS, ROWS), ROWS)

    def half_rows(m):
        return pl.ds(pl.multiple_of(m * ROWS + c * HALF, HALF), HALF)

    keep_rows = pl.ds(pl.multiple_of(c * HALF, HALF), HALF)
    give_rows = pl.ds(pl.multiple_of((1 - c) * HALF, HALF), HALF)

    def cols(n):
        return pl.ds(pl.multiple_of(n * 256, 256), 256)

    def f_swap(m):
        return remote(fpart.at[m, give_rows], frx.at[m], frx_s, (m,), sibling)

    def f_spread(m):
        return remote(fcs.at[m], fin.at[m], fin_s, (m,), partner)

    def f_share(m):
        return remote(acts.at[half_rows(m)], acts.at[half_rows(m)], facts_s, (m,), sibling)

    def b_swap(m):
        return remote(bpart.at[m, give_rows], brx.at[m], brx_s, (m,), sibling)

    def b_spread(m):
        return remote(bcs.at[m], bin_.at[m], bin_s, (m,), partner)

    def b_share(m):
        return remote(in_grads.at[half_rows(m)], in_grads.at[half_rows(m)], bout_s, (m,), sibling)

    def cross(src, m, z):
        return pltpu.make_async_remote_copy(
            src_ref=src.at[m], dst_ref=xrx.at[m, zh], send_sem=x_s.at[0, m, z],
            recv_sem=x_s.at[1, m, zh], device_id=across[z], device_id_type=MESH,
        )

    def cross_arrived(src, m, z):
        return pltpu.make_async_remote_copy(
            src_ref=src.at[m], dst_ref=xrx.at[m, z], send_sem=x_s.at[0, m, z],
            recv_sem=x_s.at[1, m, z], device_id=across[z], device_id_type=MESH,
        )

    def x_share(buf, m):
        return remote(buf.at[half_rows(m)], buf.at[half_rows(m)], xsib_s, (m,), sibling)

    def chip_sum(part, rx, cs, m):
        cs[m] = (part[m, keep_rows].astype(F32) + rx[m].astype(F32)).astype(BF16)

    def context(m):
        first_end = lens[m, 0]
        second_end = first_end + lens[m, 1]
        third_end = second_end + lens[m, 2]
        i = lax.broadcasted_iota(jnp.int32, (ROWS, ROWS), 0)
        j = lax.broadcasted_iota(jnp.int32, (ROWS, ROWS), 1)
        start = jnp.where(i >= first_end, first_end, 0)
        start = jnp.where(i >= second_end, second_end, start)
        start = jnp.where(i >= third_end, third_end, start)
        mask[m] = ((j <= i) & (j >= start)).astype(F32)
        hot = ((i - start) == j).astype(F32).astype(BF16)
        turns = dot_nn(hot, cturn[...])
        cosine = turns[:, :256] + turns[:, 256:512]
        sine = turns[:, 512:768] + turns[:, 768:]
        place = lax.rem(j, DIM)
        rot[m, 0] = cosine
        rot[m, 1] = jnp.where(place < ROT // 2, -sine, 0.0)
        rot[m, 2] = jnp.where(place >= ROT // 2, sine, 0.0)

    def norm_in(src, m):
        def body(k, carry):
            rows = pl.ds(pl.multiple_of(m * ROWS + k * 64, 64), 64)
            normed, _ = ln_rows(src[rows, :].astype(F32))
            nrm[rows, :] = normed
            attn_in[rows, :] = (normed * gains[0:1, :]).astype(BF16)
            mlp_in[rows, :] = (normed * gains[1:2, :]).astype(BF16)
            return carry

        lax.fori_loop(0, ROWS // 64, body, 0)

    def features(projected, m, turned_ref, phi_ref, low_ref):
        turned = (
            projected * rot[m, 0]
            + pltpu.roll(projected, LOCAL - ROT // 2, 1) * rot[m, 1]
            + pltpu.roll(projected, ROT // 2, 1) * rot[m, 2]
        )
        turned_ref[m] = turned
        high, rest = low_pieces(turned)
        square_high, square_rest = low_pieces(turned * turned)
        pieces = jnp.concatenate([high, rest, high, square_high, square_rest], axis=1)
        phi = fw[...] * jnp.exp(dot_nn(pieces, cfwd[...]))
        phi_ref[m] = phi
        low_ref[m] = phi.astype(BF16)

    def head_row(h):
        return cones[h * DIM : h * DIM + 1, :]

    def attend(m):
        queries, keys, values = qf[m], kf[m], vf[m]
        kept = mask[m] > 0.5
        total = jnp.zeros((ROWS, 2 * LOCAL), F32)
        for h in range(HEADS):
            row = head_row(h)
            scores = jnp.where(kept, dot_nt(queries * row, keys), 0.0).astype(BF16)
            sb[m, h] = scores
            right = jnp.concatenate(
                [values * row, jnp.broadcast_to(row, (ROWS, LOCAL))], axis=1
            )
            total = total + dot_nn(scores, right)
        norm = total[:, LOCAL:]
        attended = total[:, :LOCAL] / norm
        den[m] = norm
        att[m] = attended
        mixed[micro_rows(m), :] = attended.astype(BF16)

    def front(m):
        rows = micro_rows(m)
        normed_low = attn_in[rows, :]
        features(dot_nn(normed_low, wqkv[:, 0:256]), m, tq, pq, qf)
        features(dot_nn(normed_low, wqkv[:, 256:512]), m, tk, pk, kf)
        vf[m] = dot_nn(normed_low, wqkv[:, 512:768]).astype(BF16)
        attend(m)

        def up(n, carry):
            pre = dot_nn(mlp_in[rows, :], wup[:, cols(n)])
            cdf = 0.5 * (1.0 + lax.erf(pre * math.sqrt(0.5)))
            hidden[rows, cols(n)] = (pre * cdf).astype(BF16)
            density = jnp.exp(-0.5 * pre * pre) * (1.0 / math.sqrt(2.0 * math.pi))
            gp[rows, cols(n)] = cdf + pre * density
            return carry

        lax.fori_loop(0, 4, up, 0)

    def back_out(m):
        rows = micro_rows(m)

        def body(n, carry):
            tile = dot_nn(mixed[rows, :], wout[:, cols(n)])
            tile = tile + dot_nn(hidden[rows, :], wdown[:, cols(n)])
            fpart[m, :, cols(n)] = tile.astype(BF16)
            return carry

        lax.fori_loop(0, 4, body, 0)

    def grad_heads(src, m):
        rows = micro_rows(m)
        gm[rows, :] = dot_nt(src[rows, :], wout[...]).astype(BF16)

        def body(n, carry):
            gh[rows, cols(n)] = dot_nt(src[rows, :], wdown[cols(n), :])
            return carry

        lax.fori_loop(0, 4, body, 0)

    def feature_back(grad_phi, m, turned_ref, phi_ref):
        grad_s = grad_phi * phi_ref[m]
        small[2:3, 0:LOCAL] = small[2:3, 0:LOCAL] + jnp.sum(grad_s, axis=0, keepdims=True)
        both = dot_nn(grad_s.astype(BF16), cbwd[...])
        grad = both[:, :LOCAL] - turned_ref[m] * both[:, LOCAL:]
        return (
            grad * rot[m, 0]
            - pltpu.roll(grad, LOCAL - ROT // 2, 1) * rot[m, 1]
            - pltpu.roll(grad, ROT // 2, 1) * rot[m, 2]
        )

    def attend_back(m):
        rows = micro_rows(m)
        grad_att = gm[rows, :].astype(F32)
        grad_num = grad_att / den[m]
        grad_low = grad_num.astype(BF16)
        high, rest = low_pieces(grad_low.astype(F32) * att[m])
        grad_den = -(dot_nn(high, cones[...]) + dot_nn(rest, cones[...]))
        grad_low = grad_num.astype(BF16)
        kept = mask[m] > 0.5
        queries, keys, values = qf[m], kf[m], vf[m]
        grad_q = jnp.zeros((ROWS, LOCAL), F32)
        grad_k = jnp.zeros((ROWS, LOCAL), F32)
        grad_v = jnp.zeros((ROWS, LOCAL), F32)
        for h in range(HEADS):
            row = head_row(h)
            given = grad_low * row
            grad_scores = dot_nt(given, values) + grad_den[:, h * DIM : h * DIM + 1]
            grad_scores = jnp.where(kept, grad_scores, 0.0).astype(BF16)
            grad_q = grad_q + dot_nn(grad_scores, keys * row)
            grad_k = grad_k + dot_tn(grad_scores, queries * row)
            grad_v = grad_v + dot_tn(sb[m, h], given)
        gproj[rows, 0:256] = feature_back(grad_q, m, tq, pq).astype(BF16)
        gproj[rows, 256:512] = feature_back(grad_k, m, tk, pk).astype(BF16)
        gproj[rows, 512:768] = grad_v.astype(BF16)

    def back(m):
        rows = micro_rows(m)
        attend_back(m)

        def pre_body(n, carry):
            gpre[rows, cols(n)] = (gh[rows, cols(n)] * gp[rows, cols(n)]).astype(BF16)
            return carry

        lax.fori_loop(0, 4, pre_body, 0)

        def body(n, carry):
            grad_a = dot_nt(gproj[rows, :], wqkv[cols(n), :])
            grad_m = dot_nt(gpre[rows, :], wup[cols(n), :])
            here = cols(n)
            tile = gains[0:1, here] * grad_a + gains[1:2, here] * grad_m
            bpart[m, :, here] = tile.astype(BF16)
            normed = nrm[rows, here]
            small[0:1, here] = small[0:1, here] + jnp.sum(normed * grad_a, axis=0, keepdims=True)
            small[1:2, here] = small[1:2, here] + jnp.sum(normed * grad_m, axis=0, keepdims=True)
            return carry

        lax.fori_loop(0, 4, body, 0)

    def weight_grads(src):
        def body(n, carry):
            here = cols(n)
            at = pl.multiple_of(n * 256, 256)
            grads[pl.ds(at, 256), :] = dot_tn(hidden[:, here], src[...]).astype(BF16)
            grads[pl.ds(at + 1024, 256), :] = dot_tn(mlp_in[:, here], gpre[...]).astype(BF16)
            grads[pl.ds(at + 2048, 256), 0:768] = dot_tn(attn_in[:, here], gproj[...]).astype(BF16)
            grads[pl.ds(at + 2048, 256), 768:1024] = dot_tn(mixed[...], src[:, here]).astype(BF16)
            return carry

        lax.fori_loop(0, 4, body, 0)

    def finish_forward(src, m):
        f_spread(m).wait_recv()
        total = fcs[m].astype(F32) + fin[m].astype(F32)
        acts[half_rows(m), :] = (src[half_rows(m), :].astype(F32) + total).astype(BF16)
        f_share(m).start()

    def finish_backward(src, g_src, m):
        b_spread(m).wait_recv()
        total = bcs[m].astype(F32) + bin_[m].astype(F32)
        normed, inv = ln_rows(src[half_rows(m), :].astype(F32))
        in_grads[half_rows(m), :] = g_src[half_rows(m), :].astype(F32) + ln_back(total, normed, inv)
        b_share(m).start()

    def small_sums():
        for step, target in enumerate((sibling, partner)):
            copy = remote(small, srx.at[step], small_s, (step,), target)
            copy.start()
            copy.wait()
            small[0:2, :] = small[0:2, :] + srx[step, 0:2, :]
        small[2:3, 0:LOCAL] = small[2:3, 0:LOCAL] / fw[...]

    small[...] = jnp.zeros((8, WIDTH), F32)

    @pl.when(s == 0)
    def _():
        def forward(m, carry):
            context(m)
            norm_in(tok, m)
            front(m)
            back_out(m)
            f_swap(m).start()
            f_swap(m).wait_recv()
            chip_sum(fpart, frx, fcs, m)
            for z in range(2):
                cross(fcs, m, z).start()
            f_spread(m).start()
            return carry

        lax.fori_loop(0, MICROS, forward, 0)

        def finish(m, carry):
            finish_forward(tok, m)
            return carry

        lax.fori_loop(0, MICROS, finish, 0)

        def backward(m, carry):
            for z in range(2):
                cross_arrived(bcs, m, z).wait_recv()
            total = xrx[m, 0].astype(F32) + xrx[m, 1].astype(F32)
            normed, inv = ln_rows(acts[half_rows(m), :].astype(F32))
            grad = cot[half_rows(m), :].astype(F32) + ln_back(total, normed, inv)
            glow[half_rows(m), :] = grad.astype(BF16)
            x_share(glow, m).start()
            x_share(glow, m).wait_recv()
            grad_heads(glow, m)
            back(m)
            b_swap(m).start()
            b_swap(m).wait_recv()
            chip_sum(bpart, brx, bcs, m)
            b_spread(m).start()
            return carry

        lax.fori_loop(0, MICROS, backward, 0)
        weight_grads(glow)

        def finish_b(m, carry):
            finish_backward(tok, glow, m)
            return carry

        lax.fori_loop(0, MICROS, finish_b, 0)
        for m in range(MICROS):
            for z in range(2):
                cross(fcs, m, z).wait_send()
            x_share(glow, m).wait_send()

    @pl.when(s == 1)
    def _():
        def ahead(m, carry):
            context(m)
            grad_heads(cot, m)
            return carry

        lax.fori_loop(0, MICROS, ahead, 0)

        def both(m, carry):
            for z in range(2):
                cross_arrived(fcs, m, z).wait_recv()
            total = xrx[m, 0].astype(F32) + xrx[m, 1].astype(F32)
            layer_in = tok[half_rows(m), :].astype(F32) + total
            xin[half_rows(m), :] = layer_in.astype(BF16)
            x_share(xin, m).start()
            x_share(xin, m).wait_recv()
            norm_in(xin, m)
            front(m)
            back(m)
            b_swap(m).start()
            b_swap(m).wait_recv()
            chip_sum(bpart, brx, bcs, m)
            for z in range(2):
                cross(bcs, m, z).start()
            b_spread(m).start()
            return carry

        lax.fori_loop(0, MICROS, both, 0)
        weight_grads(cot)

        def out(m, carry):
            back_out(m)
            f_swap(m).start()
            f_swap(m).wait_recv()
            chip_sum(fpart, frx, fcs, m)
            f_spread(m).start()
            finish_backward(xin, cot, m)
            return carry

        lax.fori_loop(0, MICROS, out, 0)

        def finish(m, carry):
            finish_forward(xin, m)
            return carry

        lax.fori_loop(0, MICROS, finish, 0)
        for m in range(MICROS):
            for z in range(2):
                cross(bcs, m, z).wait_send()
            x_share(xin, m).wait_send()

    small_sums()
    for m in range(MICROS):
        f_share(m).wait_recv()
        b_share(m).wait_recv()
        for copy in (f_swap(m), f_spread(m), f_share(m), b_swap(m), b_spread(m), b_share(m)):
            copy.wait_send()


def relay(lengths, tok, cot, wqkv, wout, wup, wdown, gains, fw):
    vm = pl.BlockSpec(memory_space=pltpu.VMEM)

    def scratch(dtype, *shape):
        return pltpu.VMEM(shape, dtype)

    full = (MICROS, ROWS, WIDTH)
    half = (MICROS, HALF, WIDTH)
    sems = pltpu.SemaphoreType.DMA
    return pl.pallas_call(
        relay_kernel,
        out_shape=(
            jax.ShapeDtypeStruct((ALL_ROWS, WIDTH), BF16),
            jax.ShapeDtypeStruct((ALL_ROWS, WIDTH), F32),
            jax.ShapeDtypeStruct((3 * WIDTH, WIDTH), BF16),
            jax.ShapeDtypeStruct((8, WIDTH), F32),
        ),
        in_specs=[pl.BlockSpec(memory_space=pltpu.SMEM)] + [vm] * 12,
        out_specs=(vm, vm, vm, vm),
        scratch_shapes=[
            scratch(F32, MICROS, ROWS, ROWS),
            scratch(F32, MICROS, 3, ROWS, LOCAL),
            scratch(BF16, ALL_ROWS, WIDTH),
            scratch(BF16, ALL_ROWS, WIDTH),
            scratch(F32, ALL_ROWS, WIDTH),
            scratch(BF16, ALL_ROWS, WIDTH),
            scratch(BF16, ALL_ROWS, WIDTH),
            scratch(F32, MICROS, ROWS, LOCAL),
            scratch(F32, MICROS, ROWS, LOCAL),
            scratch(F32, MICROS, ROWS, LOCAL),
            scratch(F32, MICROS, ROWS, LOCAL),
            scratch(BF16, MICROS, ROWS, LOCAL),
            scratch(BF16, MICROS, ROWS, LOCAL),
            scratch(BF16, MICROS, ROWS, LOCAL),
            scratch(BF16, MICROS, HEADS, ROWS, ROWS),
            scratch(F32, MICROS, ROWS, LOCAL),
            scratch(F32, MICROS, ROWS, LOCAL),
            scratch(BF16, ALL_ROWS, LOCAL),
            scratch(BF16, ALL_ROWS, WIDTH),
            scratch(F32, ALL_ROWS, WIDTH),
            scratch(F32, ALL_ROWS, WIDTH),
            scratch(BF16, ALL_ROWS, LOCAL),
            scratch(BF16, ALL_ROWS, 3 * LOCAL),
            scratch(BF16, ALL_ROWS, WIDTH),
            scratch(BF16, *full),
            scratch(BF16, *half),
            scratch(BF16, *half),
            scratch(BF16, *half),
            scratch(BF16, *full),
            scratch(BF16, *half),
            scratch(BF16, *half),
            scratch(BF16, *half),
            scratch(BF16, MICROS, 2, HALF, WIDTH),
            scratch(F32, 2, 8, WIDTH),
            sems((2, MICROS)),
            sems((2, MICROS)),
            sems((2, MICROS)),
            sems((2, MICROS)),
            sems((2, MICROS)),
            sems((2, MICROS)),
            sems((2, MICROS, 2)),
            sems((2, MICROS)),
            sems((2, 2)),
        ],
        compiler_params=pltpu.CompilerParams(
            collective_id=0, has_side_effects=True, vmem_limit_bytes=60 * 2**20
        ),
        name="relay",
    )(lengths, tok, cot, wqkv, wout, wup, wdown, gains, fw, *map(jnp.asarray, constants()))


STREAMS = (("x", 1, "y", 1), ("x", -1, "y", -1), ("y", 1, "x", 1), ("y", -1, "x", -1))
CHUNKS = 3


def wrap(v):
    return lax.rem(v + 8, 4)


class Chain:
    def __init__(self, own, g, row0, stream, near, far, sent, got, place, at):
        self.own, self.g, self.row0 = own, g, row0
        self.axis1, self.d1, self.axis2, self.d2 = stream
        self.near, self.far, self.sent, self.got = near, far, sent, got
        self.p1, self.p2 = place[self.axis1], place[self.axis2]
        self.to1, self.to2 = at(self.axis1, self.d1), at(self.axis2, self.d2)
        self.copies = []

    def block(self, b):
        return pl.ds(pl.multiple_of(self.row0 + b * 64, 64), 64)

    def piece(self, b, k):
        return pl.ds(pl.multiple_of(self.row0 + b * 64 + k * 16, 16), 16)

    def send(self, step, src, dst, target):
        copy = pltpu.make_async_remote_copy(
            src_ref=src, dst_ref=dst, send_sem=self.sent.at[step], recv_sem=self.got.at[step],
            device_id=target, device_id_type=MESH,
        )
        copy.start()
        self.copies.append(copy)

    def step(self, t):
        g = self.g
        if t > 0:
            self.copies[-1].wait_recv()
        own1 = wrap(self.p1 + self.d1)
        own2 = wrap(self.p2 + self.d2)
        if t < 3:
            block = self.block(wrap(self.p1 - self.d1 * t))
            src = self.own.at[block]
            if t > 0:
                self.near[t - 1] = self.near[t - 1] + self.own[block]
                src = self.near.at[t - 1]
            self.send(t, src, self.near.at[t], self.to1)
        elif t < 6:
            k = t - 3
            if k == 0:
                self.near[2] = self.near[2] + self.own[self.block(own1)]
            rows = pl.ds(pl.multiple_of(wrap(self.p2 - self.d2 * k) * 16, 16), 16)
            src = self.near.at[2, rows]
            if k > 0:
                self.far[k - 1] = self.far[k - 1] + self.near[2, rows]
                src = self.far.at[k - 1]
            self.send(t, src, self.far.at[k], self.to2)
        elif t < 9:
            k = t - 6
            if k == 0:
                rows = pl.ds(pl.multiple_of(own2 * 16, 16), 16)
                g[self.piece(own1, own2)] = self.far[2] + self.near[2, rows]
            piece = self.piece(own1, wrap(own2 - self.d2 * k))
            self.send(t, g.at[piece], g.at[piece], self.to2)
        elif t < 12:
            block = self.block(wrap(own1 - self.d1 * (t - 9)))
            self.send(t, g.at[block], g.at[block], self.to1)
        else:
            for copy in self.copies:
                copy.wait_send()


def sum_kernel(gin, g, near, far, sent, got):
    dp = lax.axis_index("dp")
    place = {"x": dp // 4, "y": lax.rem(dp, 4)}

    def at(axis, d):
        there = dict(place)
        there[axis] = lax.rem(place[axis] + d + 4, 4)
        return {"dp": there["x"] * 4 + there["y"]}

    barrier = pltpu.get_barrier_semaphore()
    for axis in ("x", "y"):
        for d in (1, 3):
            pl.semaphore_signal(barrier, inc=1, device_id=at(axis, d), device_id_type=MESH)
    pl.semaphore_wait(barrier, 4)

    chains = [
        [
            Chain(
                gin, g, j * 1024 + q * 256, STREAMS[q], near.at[j * 4 + q], far.at[j * 4 + q],
                sent.at[j * 4 + q], got.at[j * 4 + q], place, at,
            )
            for q in range(4)
        ]
        for j in range(CHUNKS)
    ]
    for t in range(13):
        for row in chains:
            for chain in row:
                chain.step(t)


def total_over_dp(grads):
    n = 4 * CHUNKS
    vm = pl.BlockSpec(memory_space=pltpu.VMEM)
    sems = pltpu.SemaphoreType.DMA
    return pl.pallas_call(
        sum_kernel,
        out_shape=jax.ShapeDtypeStruct(grads.shape, BF16),
        in_specs=[vm],
        out_specs=vm,
        scratch_shapes=[
            pltpu.VMEM((n, 3, 64, WIDTH), BF16),
            pltpu.VMEM((n, 3, 16, WIDTH), BF16),
            sems((n, 12)),
            sems((n, 12)),
        ],
        compiler_params=pltpu.CompilerParams(
            collective_id=1, has_side_effects=True, vmem_limit_bytes=56 * 2**20
        ),
        name="total_over_dp",
    )(grads)


def per_device(
    tokens, lengths, cotangent, qkv_weight, out_weight, up_weight, down_weight, norm_gains,
    feat_weights, reduce=True,
):
    acts, in_grads, grads, small = relay(
        lengths, tokens, cotangent, qkv_weight[0].reshape(WIDTH, 3 * LOCAL), out_weight[0],
        up_weight[0], down_weight[0], norm_gains[0], feat_weights[0].reshape(1, LOCAL),
    )
    if reduce:
        grads = total_over_dp(grads)
        small = lax.psum(small, "dp")
    wide = grads[2 * WIDTH :]
    qkv = wide[:, : 3 * LOCAL].reshape(1, WIDTH, 3, LOCAL).astype(F32)
    out = wide[:, 3 * LOCAL :].reshape(4, LOCAL, LOCAL).transpose(1, 0, 2).reshape(1, LOCAL, WIDTH)
    return (
        acts[None],
        in_grads[None],
        qkv,
        out.astype(F32),
        grads[WIDTH : 2 * WIDTH].astype(F32)[None],
        grads[:WIDTH].astype(F32)[None],
        small[0:2][None],
        small[2, :LOCAL].reshape(1, HEADS, DIM),
    )


PLACED = (
    P("dp", None),
    P("dp", None),
    P("dp", None),
    P("section", None, None, "tensor"),
    P("section", "tensor", None),
    P("section", None, "tensor"),
    P("section", "tensor", None),
    P("section", None, None),
    P("section", "tensor", None),
)
GIVEN = (
    P("section", "dp", None),
    P("section", "dp", None),
    P("section", None, None, "tensor"),
    P("section", "tensor", None),
    P("section", None, "tensor"),
    P("section", "tensor", None),
    P("section", None, None),
    P("section", "tensor", None),
)


def solution(mesh):
    return jax.shard_map(
        per_device, mesh=mesh, in_specs=PLACED, out_specs=GIVEN, check_vma=False
    )
```

```python
import functools
import math

import jax
import jax.numpy as jnp
import numpy as np
from jax import lax
from jax.experimental import pallas as pl
from jax.experimental.pallas import tpu as pltpu
from jax.sharding import PartitionSpec as P

F32 = jnp.float32
BF16 = jnp.bfloat16
MESH = pl.DeviceIdType.MESH
EPS = 1e-05
ROWS = 256
HALF = 128
WIDTH = 1024
LOCAL = 256
HEADS = 4
DIM = 64
ROT = 16
MICROS = 2
ALL_ROWS = MICROS * ROWS


def feature_table(head_dim, feat_count):
    golden = 0.6180339887498949
    row_grid = np.arange(feat_count)[:, None] + 0.5
    columns = np.arange(head_dim)[None, :] * 1.0
    points = np.mod(row_grid * (2.0 * columns + 1.0) / feat_count + golden * columns, 1.0)
    radius = np.sqrt(-2.0 * np.log(points[:, 0::2]))
    turning = 2.0 * np.pi * points[:, 1::2]
    omega_rows = np.stack([radius * np.cos(turning), radius * np.sin(turning)], axis=2).reshape(
        feat_count, head_dim
    )
    frequency = np.arange(head_dim)[:, None] * 1.0
    cosine_basis = np.sqrt(2.0 / head_dim) * np.cos(
        np.pi * (2.0 * columns + 1.0) * frequency / (2.0 * head_dim)
    )
    cosine_basis = np.where(frequency == 0, np.sqrt(0.5), 1.0) * cosine_basis
    return np.sum(omega_rows[:, :, None] * cosine_basis[None, :, :], axis=1)


def low_pieces(values):
    high = values.astype(BF16)
    rest = (values - high.astype(values.dtype)).astype(BF16)
    return high, rest


def constants():
    table = feature_table(DIM, DIM).astype(np.float32)
    eye = np.eye(HEADS, dtype=np.float32)
    blocks = np.kron(eye, table.T / math.sqrt(DIM)).astype(np.float32)
    ones = np.kron(eye, np.ones((DIM, DIM), np.float32))
    high, rest = low_pieces(blocks)
    scaled = (ones * (-1.0 / (2.0 * DIM))).astype(BF16)
    forward = np.concatenate([high, high, rest, scaled, scaled], axis=0)
    backward = np.concatenate([blocks.T.astype(BF16), (ones / DIM).astype(BF16)], axis=1)
    half_rot = ROT // 2
    inverse = (10000.0 ** (-2.0 * np.arange(half_rot) / ROT)).astype(np.float32)
    angles = np.arange(ROWS, dtype=np.float32)[:, None] * inverse[None, :]
    cosine = np.ones((ROWS, DIM), np.float32)
    sine = np.zeros((ROWS, DIM), np.float32)
    for start in (0, half_rot):
        cosine[:, start : start + half_rot] = np.cos(angles.astype(np.float64))
        sine[:, start : start + half_rot] = np.sin(angles.astype(np.float64))
    cosine = np.tile(cosine, (1, HEADS))
    sine = np.tile(sine, (1, HEADS))
    turns = np.concatenate([*low_pieces(cosine), *low_pieces(sine)], axis=1)
    spread = np.tile(np.eye(DIM, dtype=np.float32), (1, HEADS))
    return forward, backward, ones.astype(BF16), turns, spread


def dot_nn(a, b):
    return lax.dot_general(a, b, (((1,), (0,)), ((), ())), preferred_element_type=F32)


def dot_nt(a, b):
    return lax.dot_general(a, b, (((1,), (1,)), ((), ())), preferred_element_type=F32)


def dot_tn(a, b):
    return lax.dot_general(a, b, (((0,), (0,)), ((), ())), preferred_element_type=F32)


def ln_rows(x):
    mean = jnp.mean(x, axis=-1, keepdims=True)
    centered = x - mean
    inv = lax.rsqrt(jnp.mean(centered * centered, axis=-1, keepdims=True) + EPS)
    return centered * inv, inv


def ln_back(combined, normed, inv):
    mean_c = jnp.mean(combined, axis=-1, keepdims=True)
    mean_p = jnp.mean(combined * normed, axis=-1, keepdims=True)
    return inv * (combined - mean_c - normed * mean_p)


STREAMS = (("x", 1, "y", 1), ("x", -1, "y", -1), ("y", 1, "x", 1), ("y", -1, "x", -1))
PARTS = 3
CHAINS = 4 * PARTS


def wrap(v):
    return lax.rem(v + 8, 4)


class Chain:
    def __init__(self, own, g, out, row0, stream, near, far, sems, place, at):
        self.own, self.g, self.out, self.row0 = own, g, out, row0
        self.axis1, self.d1, self.axis2, self.d2 = stream
        self.near, self.far = near, far
        self.sent, self.got, self.saved = sems
        self.p1, self.p2 = place[self.axis1], place[self.axis2]
        self.to1, self.to2 = at(self.axis1, self.d1), at(self.axis2, self.d2)
        self.own1, self.own2 = wrap(self.p1 + self.d1), wrap(self.p2 + self.d2)

    def block(self, b):
        return pl.ds(pl.multiple_of(self.row0 + b * 64, 64), 64)

    def piece(self, b, k):
        return pl.ds(pl.multiple_of(self.row0 + b * 64 + k * 16, 16), 16)

    def copy(self, t):
        k = t % 3
        if t < 3:
            src = self.near.at[k - 1] if k else self.own.at[self.block(self.p1)]
            dst = self.near.at[k]
        elif t < 6:
            rows = pl.ds(pl.multiple_of(self.p2 * 16, 16), 16)
            src = self.far.at[k - 1] if k else self.near.at[2, rows]
            dst = self.far.at[k]
        elif t < 9:
            src = dst = self.g.at[self.piece(self.own1, wrap(self.own2 - self.d2 * k))]
        else:
            src = dst = self.g.at[self.block(wrap(self.own1 - self.d1 * k))]
        return pltpu.make_async_remote_copy(
            src_ref=src, dst_ref=dst, send_sem=self.sent.at[t], recv_sem=self.got.at[t],
            device_id=self.to1 if t < 3 or t > 8 else self.to2, device_id_type=MESH,
        )

    def save(self, k):
        rows = self.block(wrap(self.own1 - self.d1 * k))
        return pltpu.make_async_copy(self.g.at[rows], self.out.at[rows], self.saved.at[k])

    def step(self, t):
        if t > 0:
            self.copy(t - 1).wait_recv()
        k = t % 3
        if 0 < t < 3:
            block = self.block(wrap(self.p1 - self.d1 * t))
            self.near[k - 1] = self.near[k - 1] + self.own[block, :]
        elif t == 3:
            self.near[2] = self.near[2] + self.own[self.block(self.own1), :]
        elif 3 < t < 6:
            rows = pl.ds(pl.multiple_of(wrap(self.p2 - self.d2 * k) * 16, 16), 16)
            self.far[k - 1] = self.far[k - 1] + self.near[2, rows]
        elif t == 6:
            rows = pl.ds(pl.multiple_of(self.own2 * 16, 16), 16)
            self.g[self.piece(self.own1, self.own2), :] = self.far[2] + self.near[2, rows]
        if t < 12:
            self.copy(t).start()
        if t > 8:
            self.save(t - 9).start()

    def finish(self):
        for t in range(12):
            self.copy(t).wait_send()
        for k in range(4):
            self.save(k).wait()


def layers_kernel(
    lens, tok_h, cot_h, wqkv_h, wout_h, wup_h, wdown_h, gains, feats, cfwd, cbwd, cones, cturn, cspread,
    acts_h, in_grads_h, grads_h, gain_out, feat_out,
    xin, glow, aux, wqkv, wout, wup, wdown, acts, in_grads, gbuf, gsum, near, far,
    fw, mask, rot, nrm, attn_in, mlp_in, tq, tk, pq, pk, qf, kf, vf, sb, den, att,
    mixed, hidden, ghp, gm, gproj, gpre, nx, inv_x,
    fpart, frx, fcs, fin, bpart, brx, bcs, bin_, xrx, small, srx, sall,
    load_s, frx_s, fin_s, facts_s, brx_s, bin_s, bout_s, x_s, xsib_s, small_s, all_s,
    sent_s, got_s, saved_s, out_s,
):
    s = lax.axis_index("section")
    t = lax.axis_index("tensor")
    dp = lax.axis_index("dp")
    zh = t // 2
    c = lax.rem(t, 2)
    sibling = {"tensor": zh * 2 + 1 - c}
    partner = {"tensor": lax.rem(t + 2, 4)}
    across = [{"section": 1 - s, "tensor": z * 2 + c} for z in range(2)]
    place = {"x": dp // 4, "y": lax.rem(dp, 4)}

    def at(axis, d):
        there = dict(place)
        there[axis] = lax.rem(place[axis] + d + 4, 4)
        return {"dp": there["x"] * 4 + there["y"]}

    def load(src, dst, k):
        return pltpu.make_async_copy(src, dst, load_s.at[k])

    load_qkv = [load(wqkv_h.at[k], wqkv.at[k], 2 + k) for k in range(3)]
    load_up = load(wup_h, wup, 5)
    load_out = load(wout_h, wout, 6)
    load_down = load(wdown_h, wdown, 7)

    @pl.when(s == 0)
    def _():
        load(tok_h, xin, 0).start()
        for one in (*load_qkv, load_up, load_out, load_down):
            one.start()
        load(cot_h, aux, 1).start()

    @pl.when(s == 1)
    def _():
        load(cot_h, glow, 0).start()
        for one in (load_out, load_down, *load_qkv, load_up):
            one.start()
        load(tok_h, aux, 1).start()

    barrier = pltpu.get_barrier_semaphore()
    peers = [sibling, partner, *across] + [at(axis, d) for axis in ("x", "y") for d in (1, 2, 3)]
    for target in peers:
        pl.semaphore_signal(barrier, inc=1, device_id=target, device_id_type=MESH)

    def remote(src, dst, sems, index, target):
        return pltpu.make_async_remote_copy(
            src_ref=src, dst_ref=dst, send_sem=sems.at[(0, *index)],
            recv_sem=sems.at[(1, *index)], device_id=target, device_id_type=MESH,
        )

    def micro_rows(m):
        if isinstance(m, int):
            return slice(m * ROWS, (m + 1) * ROWS)
        return pl.ds(pl.multiple_of(m * ROWS, ROWS), ROWS)

    def half_rows(m):
        return pl.ds(pl.multiple_of(m * ROWS + c * HALF, HALF), HALF)

    def part_rows(m, core, k):
        return pl.ds(pl.multiple_of(m * ROWS + core * HALF + k * 64, 64), 64)

    keep_rows = pl.ds(pl.multiple_of(c * HALF, HALF), HALF)
    give_rows = pl.ds(pl.multiple_of((1 - c) * HALF, HALF), HALF)

    def cols(n):
        return slice(n * 256, (n + 1) * 256)

    def f_swap(m):
        return remote(fpart.at[m, give_rows], frx.at[m], frx_s, (m,), sibling)

    def f_spread(m):
        return remote(fcs.at[m], fin.at[m], fin_s, (m,), partner)

    def f_share(m):
        return remote(acts.at[half_rows(m)], acts.at[half_rows(m)], facts_s, (m,), sibling)

    def b_swap(m):
        return remote(bpart.at[m, give_rows], brx.at[m], brx_s, (m,), sibling)

    def b_spread(m):
        return remote(bcs.at[m], bin_.at[m], bin_s, (m,), partner)

    def b_share(m):
        return remote(in_grads.at[half_rows(m)], in_grads.at[half_rows(m)], bout_s, (m,), sibling)

    def cross(src, m, z, k, arrival=False):
        here = z if arrival else zh
        rows = slice(k * 64, (k + 1) * 64)
        return pltpu.make_async_remote_copy(
            src_ref=src.at[m, rows], dst_ref=xrx.at[m, here, rows], send_sem=x_s.at[0, m, z, k],
            recv_sem=x_s.at[1, m, here, k], device_id=across[z], device_id_type=MESH,
        )

    def x_share(buf, m, k):
        rows = part_rows(m, c, k)
        return remote(buf.at[rows], buf.at[rows], xsib_s, (m, k), sibling)

    def chip_sum(part, rx, cs, m):
        cs[m] = (part[m, keep_rows].astype(F32) + rx[m].astype(F32)).astype(BF16)

    def send_across(cs, m):
        for k in range(2):
            for z in range(2):
                cross(cs, m, z, k).start()

    def arrived(src, m, k):
        for z in range(2):
            cross(src, m, z, k, arrival=True).wait_recv()
        rows = slice(k * 64, (k + 1) * 64)
        return xrx[m, 0, rows].astype(F32) + xrx[m, 1, rows].astype(F32)

    def context(m):
        first_end = lens[m, 0]
        second_end = first_end + lens[m, 1]
        third_end = second_end + lens[m, 2]
        i = lax.broadcasted_iota(jnp.int32, (ROWS, ROWS), 0)
        j = lax.broadcasted_iota(jnp.int32, (ROWS, ROWS), 1)
        start = jnp.where(i >= first_end, first_end, 0)
        start = jnp.where(i >= second_end, second_end, start)
        start = jnp.where(i >= third_end, third_end, start)
        mask[m] = ((j <= i) & (j >= start)).astype(F32)
        hot = ((i - start) == j).astype(F32).astype(BF16)
        turns = dot_nn(hot, cturn[...])
        cosine = turns[:, :256] + turns[:, 256:512]
        sine = turns[:, 512:768] + turns[:, 768:]
        column = lax.rem(j, DIM)
        rot[m, 0] = cosine
        rot[m, 1] = jnp.where(column < ROT // 2, -sine, 0.0)
        rot[m, 2] = jnp.where(column >= ROT // 2, sine, 0.0)

    def norm_rows(rows):
        normed, _ = ln_rows(xin[rows, :].astype(F32))
        nrm[rows, :] = normed
        attn_in[rows, :] = (normed * gains[0:1, :]).astype(BF16)
        mlp_in[rows, :] = (normed * gains[1:2, :]).astype(BF16)

    def features(projected, m, turned_ref, phi_ref, low_ref):
        turned = (
            projected * rot[m, 0]
            + pltpu.roll(projected, LOCAL - ROT // 2, 1) * rot[m, 1]
            + pltpu.roll(projected, ROT // 2, 1) * rot[m, 2]
        )
        turned_ref[m] = turned
        high, rest = low_pieces(turned)
        square_high, square_rest = low_pieces(turned * turned)
        pieces = jnp.concatenate([high, rest, high, square_high, square_rest], axis=1)
        phi = fw[...] * jnp.exp(dot_nn(pieces, cfwd[...]))
        phi_ref[m] = phi
        low_ref[m] = phi.astype(BF16)

    def head_row(h):
        return cones[h * DIM : h * DIM + 1, :]

    def attend(m):
        queries, keys, values = qf[m], kf[m], vf[m]
        kept = mask[m] > 0.5
        total = jnp.zeros((ROWS, 2 * LOCAL), F32)
        for h in range(HEADS):
            row = head_row(h)
            scores = jnp.where(kept, dot_nt(queries * row, keys), 0.0).astype(BF16)
            sb[m, h] = scores
            right = jnp.concatenate(
                [values * row, jnp.broadcast_to(row, (ROWS, LOCAL))], axis=1
            )
            total = total + dot_nn(scores, right)
        norm = total[:, LOCAL:]
        attended = total[:, :LOCAL] / norm
        den[m] = norm
        att[m] = attended
        mixed[micro_rows(m), :] = attended.astype(BF16)

    def front(m, gradient):
        rows = micro_rows(m)
        normed_low = attn_in[rows, :]
        features(dot_nn(normed_low, wqkv[0]), m, tq, pq, qf)
        features(dot_nn(normed_low, wqkv[1]), m, tk, pk, kf)
        vf[m] = dot_nn(normed_low, wqkv[2]).astype(BF16)
        attend(m)
        for n in range(4):
            pre = dot_nn(mlp_in[rows, :], wup[:, cols(n)])
            cdf = 0.5 * (1.0 + lax.erf(pre * math.sqrt(0.5)))
            hidden[rows, cols(n)] = (pre * cdf).astype(BF16)
            density = jnp.exp(-0.5 * pre * pre) * (1.0 / math.sqrt(2.0 * math.pi))
            slope = cdf + pre * density
            if gradient:
                gpre[rows, cols(n)] = (ghp[rows, cols(n)] * slope).astype(BF16)
            else:
                ghp[rows, cols(n)] = slope

    def back_out(m):
        rows = micro_rows(m)
        for n in range(4):
            tile = dot_nn(mixed[rows, :], wout[:, cols(n)])
            tile = tile + dot_nn(hidden[rows, :], wdown[:, cols(n)])
            fpart[m, :, cols(n)] = tile.astype(BF16)

    def grad_hidden(m, known):
        rows = micro_rows(m)
        for n in range(4):
            grad = dot_nt(glow[rows, :], wdown[cols(n), :])
            if known:
                gpre[rows, cols(n)] = (grad * ghp[rows, cols(n)]).astype(BF16)
            else:
                ghp[rows, cols(n)] = grad

    def grad_mixed(m):
        rows = micro_rows(m)
        gm[rows, :] = dot_nt(glow[rows, :], wout[...]).astype(BF16)

    def feature_back(grad_phi, m, turned_ref, phi_ref):
        grad_s = grad_phi * phi_ref[m]
        small[0, 2:3, 0:LOCAL] = small[0, 2:3, 0:LOCAL] + jnp.sum(grad_s, axis=0, keepdims=True)
        both = dot_nn(grad_s.astype(BF16), cbwd[...])
        grad = both[:, :LOCAL] - turned_ref[m] * both[:, LOCAL:]
        return (
            grad * rot[m, 0]
            - pltpu.roll(grad, LOCAL - ROT // 2, 1) * rot[m, 1]
            - pltpu.roll(grad, ROT // 2, 1) * rot[m, 2]
        )

    def attend_back(m):
        rows = micro_rows(m)
        grad_num = gm[rows, :].astype(F32) / den[m]
        grad_low = grad_num.astype(BF16)
        high, rest = low_pieces(grad_low.astype(F32) * att[m])
        grad_den = -(dot_nn(high, cones[...]) + dot_nn(rest, cones[...]))
        kept = mask[m] > 0.5
        queries, keys, values = qf[m], kf[m], vf[m]
        grad_q = jnp.zeros((ROWS, LOCAL), F32)
        grad_k = jnp.zeros((ROWS, LOCAL), F32)
        grad_v = jnp.zeros((ROWS, LOCAL), F32)
        for h in range(HEADS):
            row = head_row(h)
            given = grad_low * row
            grad_scores = dot_nt(given, values) + grad_den[:, h * DIM : h * DIM + 1]
            grad_scores = jnp.where(kept, grad_scores, 0.0).astype(BF16)
            grad_q = grad_q + dot_nn(grad_scores, keys * row)
            grad_k = grad_k + dot_tn(grad_scores, queries * row)
            grad_v = grad_v + dot_tn(sb[m, h], given)
        gproj[0, rows, :] = feature_back(grad_q, m, tq, pq).astype(BF16)
        gproj[1, rows, :] = feature_back(grad_k, m, tk, pk).astype(BF16)
        gproj[2, rows, :] = grad_v.astype(BF16)

    def back_in(m):
        rows = micro_rows(m)
        for n in range(4):
            here = cols(n)
            grad_a = dot_nt(gproj[0, rows, :], wqkv[0, here, :])
            grad_a = grad_a + dot_nt(gproj[1, rows, :], wqkv[1, here, :])
            grad_a = grad_a + dot_nt(gproj[2, rows, :], wqkv[2, here, :])
            grad_m = dot_nt(gpre[rows, :], wup[here, :])
            tile = gains[0:1, here] * grad_a + gains[1:2, here] * grad_m
            bpart[m, :, here] = tile.astype(BF16)
            normed = nrm[rows, here]
            for k, grad in enumerate((grad_a, grad_m)):
                line = jnp.sum(normed * grad, axis=0, keepdims=True)
                small[0, k : k + 1, here] = small[0, k : k + 1, here] + line

    def grads_down():
        for n in range(4):
            gbuf[cols(n), :] = dot_tn(hidden[:, cols(n)], glow[...]).astype(BF16)

    def grads_up():
        for n in range(4):
            rows = slice(1024 + n * 256, 1280 + n * 256)
            gbuf[rows, :] = dot_tn(mlp_in[:, cols(n)], gpre[...]).astype(BF16)

    def grads_attn():
        for n in range(4):
            rows = slice(2048 + n * 256, 2304 + n * 256)
            for k in range(3):
                gbuf[rows, cols(k)] = dot_tn(attn_in[:, cols(n)], gproj[k]).astype(BF16)
            gbuf[rows, cols(3)] = dot_tn(mixed[...], glow[:, cols(n)]).astype(BF16)

    def finish_forward(m):
        f_spread(m).wait_recv()
        total = fcs[m].astype(F32) + fin[m].astype(F32)
        acts[half_rows(m), :] = (xin[half_rows(m), :].astype(F32) + total).astype(BF16)
        f_share(m).start()

    def finish_backward(m):
        b_spread(m).wait_recv()
        total = bcs[m].astype(F32) + bin_[m].astype(F32)
        normed, inv = ln_rows(xin[half_rows(m), :].astype(F32))
        in_grads[half_rows(m), :] = glow[half_rows(m), :].astype(F32) + ln_back(total, normed, inv)
        b_share(m).start()

    chains = [
        [
            Chain(
                gbuf, gsum, grads_h, j * 1024 + q * 256, STREAMS[q], near.at[j * 4 + q],
                far.at[j * 4 + q],
                (sent_s.at[j * 4 + q], got_s.at[j * 4 + q], saved_s.at[j * 4 + q]), place, at,
            )
            for q in range(4)
        ]
        for j in range(PARTS)
    ]

    def hop(j, step):
        for chain in chains[j]:
            chain.step(step)

    def small_step(k):
        def copy(k):
            if k < 2:
                return [remote(small.at[k], srx.at[k], small_s, (k,), (sibling, partner)[k])]
            axis = "xy"[k - 2]
            return [
                pltpu.make_async_remote_copy(
                    src_ref=small.at[k], dst_ref=sall.at[k - 2, place[axis]],
                    send_sem=all_s.at[0, k - 2, d], recv_sem=all_s.at[1, k - 2, d],
                    device_id=at(axis, d), device_id_type=MESH,
                )
                for d in (1, 2, 3)
            ]

        if k == -1:
            return [one for j in range(4) for one in copy(j)]
        if k > 0:
            for one in copy(k - 1):
                one.wait_recv()
        if k in (1, 2):
            line = lax.broadcasted_iota(jnp.int32, (8, WIDTH), 0)
            small[k] = small[k - 1] + jnp.where(line < 2, srx[k - 1], 0.0)
        if k in (3, 4):
            parts = sall[k - 3]
            small[k] = (parts[0] + parts[1]) + (parts[2] + parts[3])
        if k in (2, 3):
            sall[k - 2, place["xy"[k - 2]]] = small[k]
        if k < 4:
            for one in copy(k):
                one.start()
        return None

    small[...] = jnp.zeros(small.shape, F32)
    exact = lax.dot_general(
        feats[...], cspread[...], (((1,), (0,)), ((), ())), preferred_element_type=F32,
        precision=lax.Precision.HIGHEST,
    )
    heads_of = jnp.concatenate([head_row(h) for h in range(HEADS)], axis=0).astype(F32)
    fw[...] = jnp.sum(exact * heads_of, axis=0, keepdims=True)

    @pl.when(s == 0)
    def _():
        def forward(m, carry):
            context(m)

            @pl.when(m == 0)
            def _():
                load(tok_h, xin, 0).wait()

            for k in range(4):
                norm_rows(pl.ds(pl.multiple_of(m * ROWS + k * 64, 64), 64))

            @pl.when(m == 0)
            def _():
                for one in (*load_qkv, load_up, load_out, load_down):
                    one.wait()

            front(m, False)
            back_out(m)

            @pl.when(m == 0)
            def _():
                pl.semaphore_wait(barrier, len(peers))

            f_swap(m).start()
            f_swap(m).wait_recv()
            chip_sum(fpart, frx, fcs, m)
            send_across(fcs, m)
            return carry

        lax.fori_loop(0, MICROS, forward, 0)
        load(cot_h, aux, 1).wait()
        for m in range(MICROS):
            for z in range(2):
                for k in range(2):
                    cross(fcs, m, z, k).wait_send()
            f_spread(m).start()
        for m in range(MICROS):
            finish_forward(m)
            normed, inv = ln_rows(acts[half_rows(m), :].astype(F32))
            nx[m] = normed
            inv_x[m] = jnp.broadcast_to(inv, (HALF, 128))

        def gradient_in(m):
            for k in range(2):
                total = arrived(bcs, m, k)
                rows = slice(k * 64, (k + 1) * 64)
                back = ln_back(total, nx[m, rows], inv_x[m, rows, 0:1])
                grad = aux[part_rows(m, c, k), :].astype(F32) + back
                glow[part_rows(m, c, k), :] = grad.astype(BF16)
                x_share(glow, m, k).start()
            for k in range(2):
                x_share(glow, m, k).wait_recv()

        gradient_in(0)
        grad_mixed(0)
        grad_hidden(0, True)
        attend_back(0)
        back_in(0)
        b_swap(0).start()
        b_swap(0).wait_recv()
        chip_sum(bpart, brx, bcs, 0)
        b_spread(0).start()
        gradient_in(1)
        grads_down()
        hop(0, 0)
        grad_hidden(1, True)
        grads_up()
        hop(1, 0)
        grad_mixed(1)
        attend_back(1)
        grads_attn()
        hop(2, 0)
        hop(0, 1)
        back_in(1)
        hop(1, 1)
        b_swap(1).start()
        b_swap(1).wait_recv()
        chip_sum(bpart, brx, bcs, 1)
        b_spread(1).start()
        finish_backward(0)
        finish_backward(1)
        hop(2, 1)
        for m in range(MICROS):
            for k in range(2):
                x_share(glow, m, k).wait_send()

    @pl.when(s == 1)
    def _():
        load(cot_h, glow, 0).wait()
        load_out.wait()
        load_down.wait()
        for m in range(MICROS):
            context(m)
            grad_hidden(m, False)
            grad_mixed(m)
        for one in (*load_qkv, load_up, load(tok_h, aux, 1)):
            one.wait()
        pl.semaphore_wait(barrier, len(peers))

        def both(m, carry):
            for k in range(2):
                total = arrived(fcs, m, k)
                own = part_rows(m, c, k)
                xin[own, :] = (aux[own, :].astype(F32) + total).astype(BF16)
                x_share(xin, m, k).start()
                x_share(xin, m, k).wait_recv()
                norm_rows(own)
                norm_rows(part_rows(m, 1 - c, k))
            front(m, True)
            attend_back(m)
            back_in(m)
            b_swap(m).start()
            b_swap(m).wait_recv()
            chip_sum(bpart, brx, bcs, m)
            send_across(bcs, m)
            return carry

        lax.fori_loop(0, MICROS, both, 0)
        grads_down()
        hop(0, 0)
        grads_up()
        hop(1, 0)
        grads_attn()
        hop(2, 0)
        hop(0, 1)
        for m in range(MICROS):
            back_out(m)
            f_swap(m).start()
        hop(1, 1)
        for m in range(MICROS):
            f_swap(m).wait_recv()
            chip_sum(fpart, frx, fcs, m)
            f_spread(m).start()
            for z in range(2):
                for k in range(2):
                    cross(bcs, m, z, k).wait_send()
            b_spread(m).start()
        hop(2, 1)
        for m in range(MICROS):
            finish_forward(m)
            finish_backward(m)
        for m in range(MICROS):
            for k in range(2):
                x_share(xin, m, k).wait_send()

    def store(m):
        rows = micro_rows(m)
        return [
            pltpu.make_async_copy(acts.at[rows], acts_h.at[rows], out_s.at[0, m]),
            pltpu.make_async_copy(in_grads.at[rows], in_grads_h.at[rows], out_s.at[1, m]),
        ]

    for step in range(2, 13):
        for j in range(PARTS):
            hop(j, step)
        if step < 7:
            small_step(step - 2)
        if step == 7:
            for m in range(MICROS):
                f_share(m).wait_recv()
                b_share(m).wait_recv()
                for one in store(m):
                    one.start()
            gain_out[...] = small[4, 0:2, :]
            line = jnp.broadcast_to(small[4, 2:3, 0:LOCAL] / fw[...], (HEADS, LOCAL)) * heads_of
            feat_out[...] = lax.dot_general(
                line, cspread[...], (((1,), (1,)), ((), ())), preferred_element_type=F32,
                precision=lax.Precision.HIGHEST,
            )
    for row in chains:
        for chain in row:
            chain.finish()
    for m in range(MICROS):
        for one in (f_swap(m), f_spread(m), f_share(m), b_swap(m), b_spread(m), b_share(m)):
            one.wait_send()
        for one in store(m):
            one.wait()
    for one in small_step(-1):
        one.wait_send()


def layers(lengths, tok, cot, wqkv, wout, wup, wdown, gains, feats):
    vm = pl.BlockSpec(memory_space=pltpu.VMEM)
    far_off = pl.BlockSpec(memory_space=pl.ANY)

    def low(*shape):
        return pltpu.VMEM(shape, BF16)

    def wide(*shape):
        return pltpu.VMEM(shape, F32)

    full = (MICROS, ROWS, WIDTH)
    half = (MICROS, HALF, WIDTH)
    square = (MICROS, ROWS, LOCAL)
    rows = (ALL_ROWS, WIDTH)
    sems = pltpu.SemaphoreType.DMA
    return pl.pallas_call(
        layers_kernel,
        out_shape=(
            jax.ShapeDtypeStruct(rows, BF16),
            jax.ShapeDtypeStruct(rows, F32),
            jax.ShapeDtypeStruct((PARTS * WIDTH, WIDTH), BF16),
            jax.ShapeDtypeStruct((2, WIDTH), F32),
            jax.ShapeDtypeStruct((HEADS, DIM), F32),
        ),
        in_specs=[pl.BlockSpec(memory_space=pltpu.SMEM)] + [far_off] * 6 + [vm] * 7,
        out_specs=(far_off, far_off, far_off, vm, vm),
        scratch_shapes=[
            low(*rows), low(*rows), low(*rows),
            low(3, WIDTH, LOCAL), low(LOCAL, WIDTH), low(WIDTH, WIDTH), low(WIDTH, WIDTH),
            low(*rows), wide(*rows),
            low(PARTS * WIDTH, WIDTH), low(PARTS * WIDTH, WIDTH),
            low(CHAINS, 3, 64, WIDTH), low(CHAINS, 3, 16, WIDTH),
            wide(1, LOCAL), wide(*square), wide(MICROS, 3, ROWS, LOCAL),
            wide(*rows), low(*rows), low(*rows),
            wide(*square), wide(*square), wide(*square), wide(*square),
            low(*square), low(*square), low(*square),
            low(MICROS, HEADS, ROWS, ROWS), wide(*square), wide(*square),
            low(ALL_ROWS, LOCAL), low(*rows), wide(*rows), low(ALL_ROWS, LOCAL),
            low(3, ALL_ROWS, LOCAL), low(*rows), wide(*half), wide(MICROS, HALF, 128),
            low(*full), low(*half), low(*half), low(*half),
            low(*full), low(*half), low(*half), low(*half),
            low(MICROS, 2, HALF, WIDTH), wide(5, 8, WIDTH), wide(2, 8, WIDTH), wide(2, 4, 8, WIDTH),
            sems((8,)),
            sems((2, MICROS)), sems((2, MICROS)), sems((2, MICROS)),
            sems((2, MICROS)), sems((2, MICROS)), sems((2, MICROS)),
            sems((2, MICROS, 2, 2)), sems((2, MICROS, 2)), sems((2, 2)), sems((2, 2, 4)),
            sems((CHAINS, 12)), sems((CHAINS, 12)), sems((CHAINS, 4)), sems((2, MICROS)),
        ],
        compiler_params=pltpu.CompilerParams(
            collective_id=0, has_side_effects=True, vmem_limit_bytes=63 * 2**20
        ),
        name="layers",
    )(lengths, tok, cot, wqkv, wout, wup, wdown, gains, feats, *map(jnp.asarray, constants()))


STEPS = 8


def widen_kernel(down, up, attn, acts, in_grads, gains, feats, o_down, o_up, o_qkv, o_out, o_acts, o_in, o_gains, o_feats):
    o_down[...] = down[...].astype(F32)
    o_up[...] = up[...].astype(F32)
    for k in range(3):
        o_qkv[k] = attn[:, k * 256 : (k + 1) * 256].astype(F32)
    o_out[...] = attn[:, 768:].astype(F32)
    o_acts[...] = acts[...]
    o_in[...] = in_grads[...]
    o_gains[...] = gains[...]
    o_feats[...] = feats[...]


def widen(grads, acts, in_grads, gains, feats):
    tall = WIDTH // STEPS
    few = ALL_ROWS // STEPS

    def part(j):
        return pl.BlockSpec((tall, WIDTH), lambda i: (i + j * STEPS, 0))

    one = pl.BlockSpec((tall, WIDTH), lambda i: (i, 0))
    row = pl.BlockSpec((few, WIDTH), lambda i: (i, 0))
    gain = pl.BlockSpec((2, WIDTH), lambda i: (0, 0))
    feat = pl.BlockSpec((HEADS, DIM), lambda i: (0, 0))

    def like(*shape):
        return jax.ShapeDtypeStruct(shape, F32)

    return pl.pallas_call(
        widen_kernel,
        grid=(STEPS,),
        in_specs=[part(0), part(1), part(2), row, row, gain, feat],
        out_specs=[
            one, one, pl.BlockSpec((3, tall, LOCAL), lambda i: (0, i, 0)),
            pl.BlockSpec((tall, LOCAL), lambda i: (lax.rem(i, 2), i // 2)),
            row, row, gain, feat,
        ],
        out_shape=(
            like(WIDTH, WIDTH), like(WIDTH, WIDTH), like(3, WIDTH, LOCAL), like(LOCAL, WIDTH),
            jax.ShapeDtypeStruct((ALL_ROWS, WIDTH), BF16), like(ALL_ROWS, WIDTH),
            like(2, WIDTH), like(HEADS, DIM),
        ),
        compiler_params=pltpu.CompilerParams(vmem_limit_bytes=48 * 2**20),
        name="widen",
    )(grads, grads, grads, acts, in_grads, gains, feats)


def per_device(
    tokens, lengths, cotangent, qkv_weight, out_weight, up_weight, down_weight, norm_gains,
    feat_weights,
):
    acts, in_grads, grads, gains, feats = layers(
        lengths, tokens, cotangent, jnp.transpose(qkv_weight[0], (1, 0, 2)), out_weight[0],
        up_weight[0], down_weight[0], norm_gains[0], feat_weights[0],
    )
    down, up, qkv, out, acts, in_grads, gains, feats = widen(grads, acts, in_grads, gains, feats)
    qkv = jnp.transpose(qkv, (1, 0, 2))
    return tuple(one[None] for one in (acts, in_grads, qkv, out, up, down, gains, feats))


PLACED = (
    P("dp", None),
    P("dp", None),
    P("dp", None),
    P("section", None, None, "tensor"),
    P("section", "tensor", None),
    P("section", None, "tensor"),
    P("section", "tensor", None),
    P("section", None, None),
    P("section", "tensor", None),
)
GIVEN = (
    P("section", "dp", None),
    P("section", "dp", None),
    P("section", None, None, "tensor"),
    P("section", "tensor", None),
    P("section", None, "tensor"),
    P("section", "tensor", None),
    P("section", None, None),
    P("section", "tensor", None),
)


def solution(mesh):
    return jax.shard_map(
        per_device, mesh=mesh, in_specs=PLACED, out_specs=GIVEN, check_vma=False
    )
```

```python
import functools
import math

import jax
import jax.numpy as jnp
import numpy as np
from jax import lax
from jax.experimental import pallas as pl
from jax.experimental.pallas import tpu as pltpu
from jax.sharding import PartitionSpec as P

F32 = jnp.float32
BF16 = jnp.bfloat16
MESH = pl.DeviceIdType.MESH
EPS = 1e-05
ROWS = 256
HALF = 128
WIDTH = 1024
LOCAL = 256
HEADS = 4
DIM = 64
ROT = 16
MICROS = 2
ALL_ROWS = MICROS * ROWS


def feature_table(head_dim, feat_count):
    golden = 0.6180339887498949
    row_grid = np.arange(feat_count)[:, None] + 0.5
    columns = np.arange(head_dim)[None, :] * 1.0
    points = np.mod(row_grid * (2.0 * columns + 1.0) / feat_count + golden * columns, 1.0)
    radius = np.sqrt(-2.0 * np.log(points[:, 0::2]))
    turning = 2.0 * np.pi * points[:, 1::2]
    omega_rows = np.stack([radius * np.cos(turning), radius * np.sin(turning)], axis=2).reshape(
        feat_count, head_dim
    )
    frequency = np.arange(head_dim)[:, None] * 1.0
    cosine_basis = np.sqrt(2.0 / head_dim) * np.cos(
        np.pi * (2.0 * columns + 1.0) * frequency / (2.0 * head_dim)
    )
    cosine_basis = np.where(frequency == 0, np.sqrt(0.5), 1.0) * cosine_basis
    return np.sum(omega_rows[:, :, None] * cosine_basis[None, :, :], axis=1)


def low_pieces(values):
    high = values.astype(BF16)
    rest = (values - high.astype(values.dtype)).astype(BF16)
    return high, rest


def constants():
    table = feature_table(DIM, DIM).astype(np.float32)
    eye = np.eye(HEADS, dtype=np.float32)
    blocks = np.kron(eye, table.T / math.sqrt(DIM)).astype(np.float32)
    ones = np.kron(eye, np.ones((DIM, DIM), np.float32))
    high, rest = low_pieces(blocks)
    scaled = (ones * (-1.0 / (2.0 * DIM))).astype(BF16)
    forward = np.concatenate([high, high, rest, scaled, scaled], axis=0)
    backward = np.concatenate([blocks.T.astype(BF16), (ones / DIM).astype(BF16)], axis=1)
    half_rot = ROT // 2
    inverse = (10000.0 ** (-2.0 * np.arange(half_rot) / ROT)).astype(np.float32)
    angles = np.arange(ROWS, dtype=np.float32)[:, None] * inverse[None, :]
    cosine = np.ones((ROWS, DIM), np.float32)
    sine = np.zeros((ROWS, DIM), np.float32)
    for start in (0, half_rot):
        cosine[:, start : start + half_rot] = np.cos(angles.astype(np.float64))
        sine[:, start : start + half_rot] = np.sin(angles.astype(np.float64))
    cosine = np.tile(cosine, (1, HEADS))
    sine = np.tile(sine, (1, HEADS))
    turns = np.concatenate([*low_pieces(cosine), *low_pieces(sine)], axis=1)
    spread = np.tile(np.eye(DIM, dtype=np.float32), (1, HEADS))
    return np.concatenate(
        [
            *np.split(turns, 4, axis=1), forward, *np.split(backward, 2, axis=1), ones.astype(BF16),
            spread.astype(BF16),
        ],
        axis=0,
    )


def dot_nn(a, b):
    return lax.dot_general(a, b, (((1,), (0,)), ((), ())), preferred_element_type=F32)


def dot_nt(a, b):
    return lax.dot_general(a, b, (((1,), (1,)), ((), ())), preferred_element_type=F32)


def dot_exact(a, b, side):
    return lax.dot_general(
        a, b, (((1,), (side,)), ((), ())), preferred_element_type=F32,
        precision=lax.Precision.HIGHEST,
    )


def dot_tn(a, b):
    return lax.dot_general(a, b, (((0,), (0,)), ((), ())), preferred_element_type=F32)


def ln_rows(x):
    mean = jnp.mean(x, axis=-1, keepdims=True)
    centered = x - mean
    inv = lax.rsqrt(jnp.mean(centered * centered, axis=-1, keepdims=True) + EPS)
    return centered * inv, inv


def ln_back(combined, normed, inv):
    mean_c = jnp.mean(combined, axis=-1, keepdims=True)
    mean_p = jnp.mean(combined * normed, axis=-1, keepdims=True)
    return inv * (combined - mean_c - normed * mean_p)


STREAMS = (("x", 1, "y"), ("x", -1, "y"), ("y", 1, "x"), ("y", -1, "x"))
PARTS = 3
CHAINS = 4 * PARTS


def wrap(v):
    return lax.rem(v + 8, 4)


class Chain:
    LAST = 8

    def __init__(self, own, g, row0, stream, near, far, sems, place, at):
        self.own, self.g, self.row0, self.at = own, g, row0, at
        self.axis1, self.d1, self.axis2 = stream
        self.near, self.far = near, far
        self.sent, self.got = sems
        self.p1, self.p2 = place[self.axis1], place[self.axis2]
        self.own1 = wrap(self.p1 + self.d1)

    def block(self, b):
        return pl.ds(pl.multiple_of(self.row0 + b * 64, 64), 64)

    def piece(self, k):
        return pl.ds(pl.multiple_of(self.row0 + self.own1 * 64 + k * 16, 16), 16)

    def copy(self, i):
        k = i % 3
        ring = i < 3 or i > 8
        if i < 3:
            src = self.near.at[k - 1] if k else self.own.at[self.block(self.p1)]
            dst = self.near.at[k]
        elif i < 6:
            rows = pl.ds(pl.multiple_of(wrap(self.p2 + k + 1) * 16, 16), 16)
            src, dst = self.near.at[2, rows], self.far.at[k]
        elif i < 9:
            src = dst = self.g.at[self.piece(self.p2)]
        else:
            src = dst = self.g.at[self.block(wrap(self.own1 - self.d1 * k))]
        return pltpu.make_async_remote_copy(
            src_ref=src, dst_ref=dst, send_sem=self.sent.at[i], recv_sem=self.got.at[i],
            device_id=self.at(self.axis1, self.d1) if ring else self.at(self.axis2, k + 1),
            device_id_type=MESH,
        )

    def copies(self, t):
        if t < 3:
            return [self.copy(t)]
        if t < 5:
            return [self.copy(3 * t - 6 + k) for k in range(3)]
        return [self.copy(t + 4)] if t < self.LAST else []

    def step(self, t):
        if t > 0:
            for one in self.copies(t - 1):
                one.wait_recv()
        if 0 < t < 3:
            block = self.block(wrap(self.p1 - self.d1 * t))
            self.near[t - 1] = self.near[t - 1] + self.own[block, :]
        elif t == 3:
            self.near[2] = self.near[2] + self.own[self.block(self.own1), :]
        elif t == 4:
            rows = pl.ds(pl.multiple_of(self.p2 * 16, 16), 16)
            total = self.near[2, rows].astype(F32) + self.far[0].astype(F32)
            total = total + (self.far[1].astype(F32) + self.far[2].astype(F32))
            self.g[self.piece(self.p2), :] = total.astype(BF16)
        for one in self.copies(t):
            one.start()
        if t >= 3:
            for one in self.copies(t - 3):
                one.wait_send()

    def finish(self):
        for t in (6, 7):
            for one in self.copies(t):
                one.wait_send()


def layers_kernel(
    lens, tok_h, cot_h, wqkv_h, wout_h, wup_h, wdown_h, gains_h, feats_h, cst_h,
    acts, in_grads, gsum, gain_out, feat_out,
    xin, glow, aux, wqkv, wout, wup, wdown, gains, feats, cst, gbuf, near, far,
    fw, mask, rot, nrm, attn_in, mlp_in, tq, tk, pq, pk, qf, kf, vf, sb, den, att,
    mixed, hidden, ghp, gm, gproj, gpre, nx, inv_x,
    fpart, frx, fcs, fin, bpart, brx, bcs, bin_, xrx, small, srx, sall,
    load_s, frx_s, fin_s, facts_s, brx_s, bin_s, bout_s, x_s, xsib_s, ret_s, small_s, all_s,
    sent_s, got_s,
):
    s = lax.axis_index("section")
    t = lax.axis_index("tensor")
    dp = lax.axis_index("dp")
    zh = t // 2
    c = lax.rem(t, 2)
    sibling = {"tensor": zh * 2 + 1 - c}
    partner = {"tensor": lax.rem(t + 2, 4)}
    across = [{"section": 1 - s, "tensor": z * 2 + c} for z in range(2)]
    place = {"x": dp // 4, "y": lax.rem(dp, 4)}

    def at(axis, d):
        there = dict(place)
        there[axis] = lax.rem(place[axis] + d + 4, 4)
        return {"dp": there["x"] * 4 + there["y"]}

    def load(src, dst, k):
        return pltpu.make_async_copy(src, dst, load_s.at[k])

    first, second = slice(0, ROWS), slice(ROWS, ALL_ROWS)
    load_gains = load(gains_h, gains, 0)
    load_feats = load(feats_h, feats, 1)
    load_cst = load(cst_h, cst, 2)
    load_qkv = [load(wqkv_h.at[k], wqkv.at[k], 3 + k) for k in range(3)]
    load_up = load(wup_h, wup, 6)
    load_out = load(wout_h, wout, 7)
    load_down = load(wdown_h, wdown, 8)

    @pl.when(s == 0)
    def _():
        load(tok_h.at[first], xin.at[first], 9).start()
        for one in (load_gains, load_feats, load_cst, *load_qkv):
            one.start()

    @pl.when(s == 1)
    def _():
        load(cot_h, glow, 9).start()
        for one in (load_down, load_out, load_cst, load_gains, load_feats, *load_qkv, load_up):
            one.start()
        load(tok_h, aux, 11).start()

    barrier = pltpu.get_barrier_semaphore()
    peers = [sibling, partner, *across] + [at(axis, d) for axis in ("x", "y") for d in (1, 2, 3)]
    for target in peers:
        pl.semaphore_signal(barrier, inc=1, device_id=target, device_id_type=MESH)

    def remote(src, dst, sems, index, target):
        return pltpu.make_async_remote_copy(
            src_ref=src, dst_ref=dst, send_sem=sems.at[(0, *index)],
            recv_sem=sems.at[(1, *index)], device_id=target, device_id_type=MESH,
        )

    def micro_rows(m):
        if isinstance(m, int):
            return slice(m * ROWS, (m + 1) * ROWS)
        return pl.ds(pl.multiple_of(m * ROWS, ROWS), ROWS)

    def half_rows(m):
        return pl.ds(pl.multiple_of(m * ROWS + c * HALF, HALF), HALF)

    def part_rows(m, core, k):
        return pl.ds(pl.multiple_of(m * ROWS + core * HALF + k * 64, 64), 64)

    keep_rows = pl.ds(pl.multiple_of(c * HALF, HALF), HALF)
    give_rows = pl.ds(pl.multiple_of((1 - c) * HALF, HALF), HALF)

    def cols(n):
        return slice(n * 256, (n + 1) * 256)

    def f_swap(m):
        return remote(fpart.at[m, give_rows], frx.at[m], frx_s, (m,), sibling)

    def f_spread(m):
        return remote(fcs.at[m], fin.at[m], fin_s, (m,), partner)

    def f_share(m):
        return remote(acts.at[half_rows(m)], acts.at[half_rows(m)], facts_s, (m,), sibling)

    def b_swap(m):
        return remote(bpart.at[m, give_rows], brx.at[m], brx_s, (m,), sibling)

    def b_spread(m):
        return remote(bcs.at[m], bin_.at[m], bin_s, (m,), partner)

    def b_share(m):
        return remote(in_grads.at[half_rows(m)], in_grads.at[half_rows(m)], bout_s, (m,), sibling)

    def cross(src, m, z, k, arrival=False):
        here = z if arrival else zh
        rows = slice(k * 64, (k + 1) * 64)
        return pltpu.make_async_remote_copy(
            src_ref=src.at[m, rows], dst_ref=xrx.at[m, here, rows], send_sem=x_s.at[0, m, z, k],
            recv_sem=x_s.at[1, m, here, k], device_id=across[z], device_id_type=MESH,
        )

    def send_back(m, z, arrival=False):
        rows = part_rows(m, c, z if arrival else zh)
        return pltpu.make_async_remote_copy(
            src_ref=xin.at[rows], dst_ref=acts.at[rows], send_sem=ret_s.at[0, m, z],
            recv_sem=ret_s.at[1, m, z if arrival else zh], device_id=across[z], device_id_type=MESH,
        )

    def x_share(buf, m, k):
        rows = part_rows(m, c, k)
        return remote(buf.at[rows], buf.at[rows], xsib_s, (m, k), sibling)

    def chip_sum(part, rx, cs, m):
        cs[m] = (part[m, keep_rows].astype(F32) + rx[m].astype(F32)).astype(BF16)

    def send_across(cs, m):
        for k in range(2):
            for z in range(2):
                cross(cs, m, z, k).start()

    def arrived(src, m, k):
        for z in range(2):
            cross(src, m, z, k, arrival=True).wait_recv()
        rows = slice(k * 64, (k + 1) * 64)
        return xrx[m, 0, rows].astype(F32) + xrx[m, 1, rows].astype(F32)

    def context(m):
        first_end = lens[m, 0]
        second_end = first_end + lens[m, 1]
        third_end = second_end + lens[m, 2]
        i = lax.broadcasted_iota(jnp.int32, (ROWS, ROWS), 0)
        j = lax.broadcasted_iota(jnp.int32, (ROWS, ROWS), 1)
        start = jnp.where(i >= first_end, first_end, 0)
        start = jnp.where(i >= second_end, second_end, start)
        start = jnp.where(i >= third_end, third_end, start)
        mask[m] = ((j <= i) & (j >= start)).astype(F32)
        hot = ((i - start) == j).astype(F32).astype(BF16)
        cosine = dot_nn(hot, cst[0:256, :]) + dot_nn(hot, cst[256:512, :])
        sine = dot_nn(hot, cst[512:768, :]) + dot_nn(hot, cst[768:1024, :])
        column = lax.rem(j, DIM)
        rot[m, 0] = cosine
        rot[m, 1] = jnp.where(column < ROT // 2, -sine, 0.0)
        rot[m, 2] = jnp.where(column >= ROT // 2, sine, 0.0)

    def norm_rows(rows):
        normed, _ = ln_rows(xin[rows, :].astype(F32))
        nrm[rows, :] = normed
        attn_in[rows, :] = (normed * gains[0:1, :]).astype(BF16)
        mlp_in[rows, :] = (normed * gains[1:2, :]).astype(BF16)

    def features(projected, m, turned_ref, phi_ref, low_ref):
        turned = (
            projected * rot[m, 0]
            + pltpu.roll(projected, LOCAL - ROT // 2, 1) * rot[m, 1]
            + pltpu.roll(projected, ROT // 2, 1) * rot[m, 2]
        )
        turned_ref[m] = turned
        high, rest = low_pieces(turned)
        square_high, square_rest = low_pieces(turned * turned)
        pieces = jnp.concatenate([high, rest, high, square_high, square_rest], axis=1)
        phi = fw[...] * jnp.exp(dot_nn(pieces, cst[1024:2304, :]))
        phi_ref[m] = phi
        low_ref[m] = phi.astype(BF16)

    def head_row(h):
        return cst[2816 + h * DIM : 2817 + h * DIM, :]

    def attend(m):
        queries, keys, values = qf[m], kf[m], vf[m]
        kept = mask[m] > 0.5
        total = jnp.zeros((ROWS, 2 * LOCAL), F32)
        for h in range(HEADS):
            row = head_row(h)
            scores = jnp.where(kept, dot_nt(queries * row, keys), 0.0).astype(BF16)
            sb[m, h] = scores
            right = jnp.concatenate(
                [values * row, jnp.broadcast_to(row, (ROWS, LOCAL))], axis=1
            )
            total = total + dot_nn(scores, right)
        norm = total[:, LOCAL:]
        attended = total[:, :LOCAL] / norm
        den[m] = norm
        att[m] = attended
        mixed[micro_rows(m), :] = attended.astype(BF16)

    def front(m, gradient):
        rows = micro_rows(m)
        normed_low = attn_in[rows, :]
        features(dot_nn(normed_low, wqkv[0]), m, tq, pq, qf)
        features(dot_nn(normed_low, wqkv[1]), m, tk, pk, kf)
        vf[m] = dot_nn(normed_low, wqkv[2]).astype(BF16)
        attend(m)
        for n in range(4):
            pre = dot_nn(mlp_in[rows, :], wup[:, cols(n)])
            cdf = 0.5 * (1.0 + lax.erf(pre * math.sqrt(0.5)))
            hidden[rows, cols(n)] = (pre * cdf).astype(BF16)
            density = jnp.exp(-0.5 * pre * pre) * (1.0 / math.sqrt(2.0 * math.pi))
            slope = cdf + pre * density
            if gradient:
                gpre[rows, cols(n)] = (ghp[rows, cols(n)] * slope).astype(BF16)
            else:
                ghp[rows, cols(n)] = slope

    def back_out(m):
        rows = micro_rows(m)
        for n in range(4):
            tile = dot_nn(mixed[rows, :], wout[:, cols(n)])
            tile = tile + dot_nn(hidden[rows, :], wdown[:, cols(n)])
            fpart[m, :, cols(n)] = tile.astype(BF16)

    def grad_hidden(m, known):
        rows = micro_rows(m)
        for n in range(4):
            grad = dot_nt(glow[rows, :], wdown[cols(n), :])
            if known:
                gpre[rows, cols(n)] = (grad * ghp[rows, cols(n)]).astype(BF16)
            else:
                ghp[rows, cols(n)] = grad

    def grad_mixed(m):
        rows = micro_rows(m)
        gm[rows, :] = dot_nt(glow[rows, :], wout[...]).astype(BF16)

    def feature_back(grad_phi, m, turned_ref, phi_ref):
        grad_s = grad_phi * phi_ref[m]
        small[0, 2:3, 0:LOCAL] = small[0, 2:3, 0:LOCAL] + jnp.sum(grad_s, axis=0, keepdims=True)
        low = grad_s.astype(BF16)
        grad = dot_nn(low, cst[2304:2560, :]) - turned_ref[m] * dot_nn(low, cst[2560:2816, :])
        return (
            grad * rot[m, 0]
            - pltpu.roll(grad, LOCAL - ROT // 2, 1) * rot[m, 1]
            - pltpu.roll(grad, ROT // 2, 1) * rot[m, 2]
        )

    def attend_back(m):
        rows = micro_rows(m)
        grad_num = gm[rows, :].astype(F32) / den[m]
        grad_low = grad_num.astype(BF16)
        high, rest = low_pieces(grad_low.astype(F32) * att[m])
        ones = cst[2816:3072, :]
        grad_den = -(dot_nn(high, ones) + dot_nn(rest, ones))
        kept = mask[m] > 0.5
        queries, keys, values = qf[m], kf[m], vf[m]
        grad_q = jnp.zeros((ROWS, LOCAL), F32)
        grad_k = jnp.zeros((ROWS, LOCAL), F32)
        grad_v = jnp.zeros((ROWS, LOCAL), F32)
        for h in range(HEADS):
            row = head_row(h)
            given = grad_low * row
            grad_scores = dot_nt(given, values) + grad_den[:, h * DIM : h * DIM + 1]
            grad_scores = jnp.where(kept, grad_scores, 0.0).astype(BF16)
            grad_q = grad_q + dot_nn(grad_scores, keys * row)
            grad_k = grad_k + dot_tn(grad_scores, queries * row)
            grad_v = grad_v + dot_tn(sb[m, h], given)
        gproj[0, rows, :] = feature_back(grad_q, m, tq, pq).astype(BF16)
        gproj[1, rows, :] = feature_back(grad_k, m, tk, pk).astype(BF16)
        gproj[2, rows, :] = grad_v.astype(BF16)

    def back_in(m):
        rows = micro_rows(m)
        for n in range(4):
            here = cols(n)
            grad_a = dot_nt(gproj[0, rows, :], wqkv[0, here, :])
            grad_a = grad_a + dot_nt(gproj[1, rows, :], wqkv[1, here, :])
            grad_a = grad_a + dot_nt(gproj[2, rows, :], wqkv[2, here, :])
            grad_m = dot_nt(gpre[rows, :], wup[here, :])
            tile = gains[0:1, here] * grad_a + gains[1:2, here] * grad_m
            bpart[m, :, here] = tile.astype(BF16)
            normed = nrm[rows, here]
            for k, grad in enumerate((grad_a, grad_m)):
                line = jnp.sum(normed * grad, axis=0, keepdims=True)
                small[0, k : k + 1, here] = small[0, k : k + 1, here] + line

    def grads_down(n):
        gbuf[cols(n), :] = dot_tn(hidden[:, cols(n)], glow[...]).astype(BF16)
        chains[0][n].step(0)

    def grads_up(n):
        rows = slice(1024 + n * 256, 1280 + n * 256)
        gbuf[rows, :] = dot_tn(mlp_in[:, cols(n)], gpre[...]).astype(BF16)
        chains[1][n].step(0)

    def grads_attn(n):
        rows = slice(2048 + n * 256, 2304 + n * 256)
        for k in range(3):
            gbuf[rows, cols(k)] = dot_tn(attn_in[:, cols(n)], gproj[k]).astype(BF16)
        gbuf[rows, cols(3)] = dot_tn(mixed[...], glow[:, cols(n)]).astype(BF16)
        chains[2][n].step(0)

    def finish_forward(m):
        f_spread(m).wait_recv()
        total = fcs[m].astype(F32) + fin[m].astype(F32)
        acts[half_rows(m), :] = (xin[half_rows(m), :].astype(F32) + total).astype(BF16)
        f_share(m).start()

    def finish_backward(m):
        b_spread(m).wait_recv()
        total = bcs[m].astype(F32) + bin_[m].astype(F32)
        normed, inv = ln_rows(xin[half_rows(m), :].astype(F32))
        in_grads[half_rows(m), :] = glow[half_rows(m), :].astype(F32) + ln_back(total, normed, inv)
        b_share(m).start()

    chains = [
        [
            Chain(
                gbuf, gsum, j * 1024 + q * 256, STREAMS[q], near.at[j * 4 + q], far.at[j * 4 + q],
                (sent_s.at[j * 4 + q], got_s.at[j * 4 + q]), place, at,
            )
            for q in range(4)
        ]
        for j in range(PARTS)
    ]

    def hop(j, step):
        for chain in chains[j]:
            chain.step(step)

    def small_step(k):
        def copy(k):
            if k < 2:
                return [remote(small.at[k], srx.at[k], small_s, (k,), (sibling, partner)[k])]
            axis = "xy"[k - 2]
            return [
                pltpu.make_async_remote_copy(
                    src_ref=small.at[k], dst_ref=sall.at[k - 2, place[axis]],
                    send_sem=all_s.at[0, k - 2, d], recv_sem=all_s.at[1, k - 2, d],
                    device_id=at(axis, d), device_id_type=MESH,
                )
                for d in (1, 2, 3)
            ]

        if k == -1:
            return [one for j in range(4) for one in copy(j)]
        if k > 0:
            for one in copy(k - 1):
                one.wait_recv()
        if k in (1, 2):
            line = lax.broadcasted_iota(jnp.int32, (8, WIDTH), 0)
            small[k] = small[k - 1] + jnp.where(line < 2, srx[k - 1], 0.0)
        if k in (3, 4):
            parts = sall[k - 3]
            small[k] = (parts[0] + parts[1]) + (parts[2] + parts[3])
        if k in (2, 3):
            sall[k - 2, place["xy"[k - 2]]] = small[k]
        if k < 4:
            for one in copy(k):
                one.start()
        return None

    def spread_feats():
        exact = dot_exact(feats[...], cst[3072:3136, :].astype(F32), 0)
        fw[...] = jnp.sum(exact * heads_of(), axis=0, keepdims=True)

    def heads_of():
        return jnp.concatenate([head_row(h) for h in range(HEADS)], axis=0).astype(F32)

    def wait_all(*copies):
        for one in copies:
            one.wait()

    small[...] = jnp.zeros(small.shape, F32)

    @pl.when(s == 0)
    def _():
        wait_all(load(tok_h.at[first], xin.at[first], 9), load_gains)
        for one in (load_up, load_out, load_down, load(tok_h.at[second], xin.at[second], 10)):
            one.start()
        load(cot_h, aux, 11).start()
        for k in range(4):
            norm_rows(slice(k * 64, (k + 1) * 64))
        wait_all(load_feats, load_cst)
        spread_feats()
        context(0)
        wait_all(*load_qkv, load_up)
        front(0, False)
        wait_all(load_out, load_down)
        back_out(0)
        pl.semaphore_wait(barrier, len(peers))
        f_swap(0).start()
        wait_all(load(tok_h.at[second], xin.at[second], 10))
        for k in range(4, 8):
            norm_rows(slice(k * 64, (k + 1) * 64))
        f_swap(0).wait_recv()
        chip_sum(fpart, frx, fcs, 0)
        send_across(fcs, 0)
        context(1)
        front(1, False)
        back_out(1)
        f_swap(1).start()
        wait_all(load(cot_h, aux, 11))
        f_swap(1).wait_recv()
        chip_sum(fpart, frx, fcs, 1)
        send_across(fcs, 1)

        def gradient_in(m):
            for z in range(2):
                send_back(m, z, arrival=True).wait_recv()
            normed, inv = ln_rows(acts[half_rows(m), :].astype(F32))
            nx[m] = normed
            inv_x[m] = jnp.broadcast_to(inv, (HALF, 128))
            f_share(m).start()
            for k in range(2):
                total = arrived(bcs, m, k)
                rows = slice(k * 64, (k + 1) * 64)
                back = ln_back(total, nx[m, rows], inv_x[m, rows, 0:1])
                grad = aux[part_rows(m, c, k), :].astype(F32) + back
                glow[part_rows(m, c, k), :] = grad.astype(BF16)
                x_share(glow, m, k).start()
            for k in range(2):
                x_share(glow, m, k).wait_recv()

        gradient_in(0)
        grad_mixed(0)
        grad_hidden(0, True)
        attend_back(0)
        back_in(0)
        b_swap(0).start()
        gradient_in(1)
        for n in range(4):
            grads_down(n)
        grad_hidden(1, True)
        for n in range(4):
            grads_up(n)
        grad_mixed(1)
        attend_back(1)
        for n in range(4):
            grads_attn(n)
        hop(0, 1)
        back_in(1)
        b_swap(1).start()
        hop(1, 1)
        for m in range(MICROS):
            b_swap(m).wait_recv()
            chip_sum(bpart, brx, bcs, m)
            b_spread(m).start()
        hop(2, 1)
        for m in range(MICROS):
            for k in range(2):
                x_share(glow, m, k).wait_send()
                for z in range(2):
                    cross(fcs, m, z, k).wait_send()

    @pl.when(s == 1)
    def _():
        wait_all(load(cot_h, glow, 9), load_down)
        for m in range(MICROS):
            grad_hidden(m, False)
        wait_all(load_out, load_cst, load_gains, load_feats)
        spread_feats()
        for m in range(MICROS):
            grad_mixed(m)
            context(m)
        wait_all(*load_qkv, load_up, load(tok_h, aux, 11))
        pl.semaphore_wait(barrier, len(peers))

        def take_in(m):
            for k in range(2):
                total = arrived(fcs, m, k)
                own = part_rows(m, c, k)
                xin[own, :] = (aux[own, :].astype(F32) + total).astype(BF16)
                x_share(xin, m, k).start()
                if m == 0:
                    norm_rows(own)
                    x_share(xin, m, k).wait_recv()
                    norm_rows(part_rows(m, 1 - c, k))
            for z in range(2):
                send_back(m, z).start()
            if m == 1:
                for k in range(2):
                    norm_rows(part_rows(m, c, k))
                for k in range(2):
                    x_share(xin, m, k).wait_recv()
                    norm_rows(part_rows(m, 1 - c, k))

        def both(m):
            front(m, True)
            attend_back(m)
            back_in(m)
            b_swap(m).start()

        def cross_over(m):
            b_swap(m).wait_recv()
            chip_sum(bpart, brx, bcs, m)
            send_across(bcs, m)

        take_in(0)
        both(0)
        take_in(1)
        cross_over(0)
        both(1)
        grads_down(0)
        grads_down(1)
        cross_over(1)
        grads_down(2)
        grads_down(3)
        for n in range(4):
            grads_up(n)
        for n in range(4):
            grads_attn(n)
        hop(0, 1)
        for m in range(MICROS):
            back_out(m)
            f_swap(m).start()
        hop(1, 1)
        for m in range(MICROS):
            f_swap(m).wait_recv()
            chip_sum(fpart, frx, fcs, m)
            f_spread(m).start()
            for z in range(2):
                for k in range(2):
                    cross(bcs, m, z, k).wait_send()
            b_spread(m).start()
        hop(2, 1)
        for m in range(MICROS):
            for k in range(2):
                x_share(xin, m, k).wait_send()
                send_back(m, k).wait_send()

    for step in range(2, Chain.LAST + 1):
        for j in range(PARTS):
            hop(j, step)
        if step in (2, 3, 5, 6, 7):
            small_step((2, 3, 5, 6, 7).index(step))
        if step == 2:
            for m in range(MICROS):
                finish_backward(m)

            @pl.when(s == 1)
            def _():
                for m in range(MICROS):
                    finish_forward(m)
                    f_spread(m).wait_send()

        if step == 5:
            for m in range(MICROS):
                f_share(m).wait_recv()
                b_share(m).wait_recv()
                for one in (f_swap(m), f_share(m), b_swap(m), b_spread(m), b_share(m)):
                    one.wait_send()
        if step == 7:
            gain_out[...] = small[4, 0:2, :]
            line = jnp.broadcast_to(small[4, 2:3, 0:LOCAL] / fw[...], (HEADS, LOCAL))
            feat_out[...] = dot_exact(line * heads_of(), cst[3072:3136, :].astype(F32), 1)
            for one in small_step(-1):
                one.wait_send()
    for row in chains:
        for chain in row:
            chain.finish()


def layers(lengths, tok, cot, wqkv, wout, wup, wdown, gains, feats):
    vm = pl.BlockSpec(memory_space=pltpu.VMEM)
    far_off = pl.BlockSpec(memory_space=pl.ANY)

    def low(*shape):
        return pltpu.VMEM(shape, BF16)

    def wide(*shape):
        return pltpu.VMEM(shape, F32)

    full = (MICROS, ROWS, WIDTH)
    half = (MICROS, HALF, WIDTH)
    square = (MICROS, ROWS, LOCAL)
    rows = (ALL_ROWS, WIDTH)
    sems = pltpu.SemaphoreType.DMA
    return pl.pallas_call(
        layers_kernel,
        out_shape=(
            low(*rows), wide(*rows), low(PARTS * WIDTH, WIDTH), wide(2, WIDTH), wide(HEADS, DIM),
        ),
        in_specs=[pl.BlockSpec(memory_space=pltpu.SMEM)] + [far_off] * 9,
        out_specs=(vm, vm, vm, vm, vm),
        scratch_shapes=[
            low(*rows), low(*rows), low(*rows),
            low(3, WIDTH, LOCAL), low(LOCAL, WIDTH), low(WIDTH, WIDTH), low(WIDTH, WIDTH),
            wide(2, WIDTH), wide(HEADS, DIM), low(3136, LOCAL), low(PARTS * WIDTH, WIDTH),
            low(CHAINS, 3, 64, WIDTH), low(CHAINS, 3, 16, WIDTH),
            wide(1, LOCAL), wide(*square), wide(MICROS, 3, ROWS, LOCAL),
            wide(*rows), low(*rows), low(*rows),
            wide(*square), wide(*square), wide(*square), wide(*square),
            low(*square), low(*square), low(*square),
            low(MICROS, HEADS, ROWS, ROWS), wide(*square), wide(*square),
            low(ALL_ROWS, LOCAL), low(*rows), wide(*rows), low(ALL_ROWS, LOCAL),
            low(3, ALL_ROWS, LOCAL), low(*rows), wide(*half), wide(MICROS, HALF, 128),
            low(*full), low(*half), low(*half), low(*half),
            low(*full), low(*half), low(*half), low(*half),
            low(MICROS, 2, HALF, WIDTH), wide(5, 8, WIDTH), wide(2, 8, WIDTH), wide(2, 4, 8, WIDTH),
            sems((12,)),
            sems((2, MICROS)), sems((2, MICROS)), sems((2, MICROS)),
            sems((2, MICROS)), sems((2, MICROS)), sems((2, MICROS)),
            sems((2, MICROS, 2, 2)), sems((2, MICROS, 2)), sems((2, MICROS, 2)), sems((2, 2)), sems((2, 2, 4)),
            sems((CHAINS, 12)), sems((CHAINS, 12)),
        ],
        compiler_params=pltpu.CompilerParams(
            collective_id=0, has_side_effects=True, vmem_limit_bytes=53 * 2**20
        ),
        name="layers",
    )(lengths, tok, cot, wqkv, wout, wup, wdown, gains, feats, jnp.asarray(constants()))


STEPS = 8
TALL = WIDTH // STEPS


def widen_kernel(grads, acts, in_grads, gains, feats, o_down, o_up, o_qkv, o_out, o_acts, o_in, o_gains, o_feats, sems):
    step = pl.program_id(0)
    copies = [
        pltpu.make_async_copy(src, dst, sems.at[k])
        for k, (src, dst) in enumerate(
            ((in_grads, o_in), (acts, o_acts), (gains, o_gains), (feats, o_feats))
        )
    ]

    @pl.when(step == 0)
    def _():
        for one in copies:
            one.start()

    def part(j):
        return pl.ds(pl.multiple_of(j * WIDTH + step * TALL, TALL), TALL)

    o_down[...] = grads[part(0), :].astype(F32)
    o_up[...] = grads[part(1), :].astype(F32)
    for k in range(3):
        o_qkv[k] = grads[part(2), k * 256 : (k + 1) * 256].astype(F32)
    o_out[...] = grads[part(2), 768:].astype(F32)

    @pl.when(step == STEPS - 1)
    def _():
        for one in copies:
            one.wait()


def widen(grads, acts, in_grads, gains, feats):
    vm = pl.BlockSpec(memory_space=pltpu.VMEM)
    far_off = pl.BlockSpec(memory_space=pl.ANY)
    one = pl.BlockSpec((TALL, WIDTH), lambda i: (i, 0))

    def like(*shape):
        return jax.ShapeDtypeStruct(shape, F32)

    return pl.pallas_call(
        widen_kernel,
        grid=(STEPS,),
        in_specs=[vm] * 5,
        out_specs=[
            one, one, pl.BlockSpec((3, TALL, LOCAL), lambda i: (0, i, 0)),
            pl.BlockSpec((TALL, LOCAL), lambda i: (lax.rem(i, 2), i // 2)),
            far_off, far_off, far_off, far_off,
        ],
        out_shape=(
            like(WIDTH, WIDTH), like(WIDTH, WIDTH), like(3, WIDTH, LOCAL), like(LOCAL, WIDTH),
            jax.ShapeDtypeStruct((ALL_ROWS, WIDTH), BF16), like(ALL_ROWS, WIDTH),
            like(2, WIDTH), like(HEADS, DIM),
        ),
        scratch_shapes=[pltpu.SemaphoreType.DMA((4,))],
        compiler_params=pltpu.CompilerParams(vmem_limit_bytes=40 * 2**20),
        name="widen",
    )(grads, acts, in_grads, gains, feats)


def per_device(
    tokens, lengths, cotangent, qkv_weight, out_weight, up_weight, down_weight, norm_gains,
    feat_weights,
):
    acts, in_grads, grads, gains, feats = layers(
        lengths, tokens, cotangent, jnp.transpose(qkv_weight[0], (1, 0, 2)), out_weight[0],
        up_weight[0], down_weight[0], norm_gains[0], feat_weights[0],
    )
    down, up, qkv, out, acts, in_grads, gains, feats = widen(grads, acts, in_grads, gains, feats)
    qkv = jnp.transpose(qkv, (1, 0, 2))
    return tuple(one[None] for one in (acts, in_grads, qkv, out, up, down, gains, feats))


PLACED = (
    P("dp", None),
    P("dp", None),
    P("dp", None),
    P("section", None, None, "tensor"),
    P("section", "tensor", None),
    P("section", None, "tensor"),
    P("section", "tensor", None),
    P("section", None, None),
    P("section", "tensor", None),
)
GIVEN = (
    P("section", "dp", None),
    P("section", "dp", None),
    P("section", None, None, "tensor"),
    P("section", "tensor", None),
    P("section", None, "tensor"),
    P("section", "tensor", None),
    P("section", None, None),
    P("section", "tensor", None),
)


def solution(mesh):
    return jax.shard_map(
        per_device, mesh=mesh, in_specs=PLACED, out_specs=GIVEN, check_vma=False
    )
```

```python
import functools
import math

import jax
import jax.numpy as jnp
import numpy as np
from jax import lax
from jax.experimental import pallas as pl
from jax.experimental.pallas import tpu as pltpu
from jax.sharding import PartitionSpec as P

F32 = jnp.float32
BF16 = jnp.bfloat16
MESH = pl.DeviceIdType.MESH
EPS = 1e-05
ROWS = 256
HALF = 128
WIDTH = 1024
LOCAL = 256
HEADS = 4
DIM = 64
ROT = 16
MICROS = 2
ALL_ROWS = MICROS * ROWS


def feature_table(head_dim, feat_count):
    golden = 0.6180339887498949
    row_grid = np.arange(feat_count)[:, None] + 0.5
    columns = np.arange(head_dim)[None, :] * 1.0
    points = np.mod(row_grid * (2.0 * columns + 1.0) / feat_count + golden * columns, 1.0)
    radius = np.sqrt(-2.0 * np.log(points[:, 0::2]))
    turning = 2.0 * np.pi * points[:, 1::2]
    omega_rows = np.stack([radius * np.cos(turning), radius * np.sin(turning)], axis=2).reshape(
        feat_count, head_dim
    )
    frequency = np.arange(head_dim)[:, None] * 1.0
    cosine_basis = np.sqrt(2.0 / head_dim) * np.cos(
        np.pi * (2.0 * columns + 1.0) * frequency / (2.0 * head_dim)
    )
    cosine_basis = np.where(frequency == 0, np.sqrt(0.5), 1.0) * cosine_basis
    return np.sum(omega_rows[:, :, None] * cosine_basis[None, :, :], axis=1)


def low_pieces(values):
    high = values.astype(BF16)
    rest = (values - high.astype(values.dtype)).astype(BF16)
    return high, rest


def constants():
    table = feature_table(DIM, DIM).astype(np.float32)
    eye = np.eye(HEADS, dtype=np.float32)
    blocks = np.kron(eye, table.T / math.sqrt(DIM)).astype(np.float32)
    ones = np.kron(eye, np.ones((DIM, DIM), np.float32))
    high, rest = low_pieces(blocks)
    scaled = (ones * (-1.0 / (2.0 * DIM))).astype(BF16)
    forward = np.concatenate([high, high, rest, scaled, scaled], axis=0)
    backward = np.concatenate([blocks.T.astype(BF16), (ones / DIM).astype(BF16)], axis=1)
    half_rot = ROT // 2
    inverse = (10000.0 ** (-2.0 * np.arange(half_rot) / ROT)).astype(np.float32)
    angles = np.arange(ROWS, dtype=np.float32)[:, None] * inverse[None, :]
    cosine = np.ones((ROWS, DIM), np.float32)
    sine = np.zeros((ROWS, DIM), np.float32)
    for start in (0, half_rot):
        cosine[:, start : start + half_rot] = np.cos(angles.astype(np.float64))
        sine[:, start : start + half_rot] = np.sin(angles.astype(np.float64))
    cosine = np.tile(cosine, (1, HEADS))
    sine = np.tile(sine, (1, HEADS))
    turns = np.concatenate([*low_pieces(cosine), *low_pieces(sine)], axis=1)
    spread = np.tile(np.eye(DIM, dtype=np.float32), (1, HEADS))
    return np.concatenate(
        [
            *np.split(turns, 4, axis=1), forward, *np.split(backward, 2, axis=1), ones.astype(BF16),
            spread.astype(BF16),
        ],
        axis=0,
    )


def dot_nn(a, b):
    return lax.dot_general(a, b, (((1,), (0,)), ((), ())), preferred_element_type=F32)


def dot_nt(a, b):
    return lax.dot_general(a, b, (((1,), (1,)), ((), ())), preferred_element_type=F32)


def dot_exact(a, b, side):
    return lax.dot_general(
        a, b, (((1,), (side,)), ((), ())), preferred_element_type=F32,
        precision=lax.Precision.HIGHEST,
    )


def dot_tn(a, b):
    return lax.dot_general(a, b, (((0,), (0,)), ((), ())), preferred_element_type=F32)


def normal_cdf(v):
    bell = jnp.exp(-0.5 * v * v)
    t = pl.reciprocal(1.0 + (0.3275911 * math.sqrt(0.5)) * jnp.abs(v))
    poly = 0.5 * 1.061405429 * t - 0.5 * 1.453152027
    for coefficient in (1.421413741, -0.284496736, 0.254829592):
        poly = poly * t + 0.5 * coefficient
    tail = poly * t * bell
    cdf = jnp.where(v >= 0.0, 1.0 - tail, tail)
    return cdf, cdf + v * bell * (1.0 / math.sqrt(2.0 * math.pi))


def ln_rows(x):
    mean = jnp.mean(x, axis=-1, keepdims=True)
    centered = x - mean
    inv = lax.rsqrt(jnp.mean(centered * centered, axis=-1, keepdims=True) + EPS)
    return centered * inv, inv


def ln_back(combined, normed, inv):
    mean_c = jnp.mean(combined, axis=-1, keepdims=True)
    mean_p = jnp.mean(combined * normed, axis=-1, keepdims=True)
    return inv * (combined - mean_c - normed * mean_p)


STREAMS = (("x", 1, "y"), ("x", -1, "y"), ("y", 1, "x"), ("y", -1, "x"))
PARTS = 3


def wrap(v):
    return lax.rem(v + 8, 4)


class Sums:
    LAST = 8

    def __init__(self, own, g, row0, near, far, sent, got, place, at):
        self.own, self.g, self.row0, self.at = own, g, row0, at
        self.near, self.far, self.sent, self.got, self.place = near, far, sent, got, place

    def own1(self, q):
        axis1, d1, _ = STREAMS[q]
        return wrap(self.place[axis1] + d1)

    def block(self, q, b):
        return pl.ds(pl.multiple_of(self.row0 + q * 256 + b * 64, 64), 64)

    def piece(self, q, k):
        return pl.ds(pl.multiple_of(self.row0 + q * 256 + self.own1(q) * 64 + k * 16, 16), 16)

    def copies(self, q, t):
        axis1, d1, axis2 = STREAMS[q]
        p1, p2 = self.place[axis1], self.place[axis2]
        next1 = self.at(axis1, d1)
        if t < 3:
            src = self.near.at[t - 1, q] if t else self.own.at[self.block(q, p1)]
            pairs = [(src, self.near.at[t, q], next1)]
        elif t == 3:
            pairs = []
            for k in range(3):
                rows = pl.ds(pl.multiple_of(wrap(p2 + k + 1) * 16, 16), 16)
                pairs.append((self.near.at[2, q, rows], self.far.at[q, k], self.at(axis2, k + 1)))
        elif t == 4:
            src = self.g.at[self.piece(q, p2)]
            pairs = [(src, src, self.at(axis2, k + 1)) for k in range(3)]
        else:
            src = self.g.at[self.block(q, wrap(self.own1(q) - d1 * (t - 5)))]
            pairs = [(src, src, next1)]
        return [
            pltpu.make_async_remote_copy(
                src_ref=src, dst_ref=dst, send_sem=self.sent, recv_sem=self.got.at[t],
                device_id=target, device_id_type=MESH,
            )
            for src, dst, target in pairs
        ]

    def wait(self, t):
        if t < 3:
            all_of = self.near.at[t]
        elif t == 3:
            all_of = self.far
        else:
            count = 192 if t == 4 else 256
            all_of = self.g.at[self.row0 : self.row0 + count]
        pltpu.make_async_copy(all_of, all_of, self.got.at[t]).wait()

    def start(self, q, t):
        axis1, d1, axis2 = STREAMS[q]
        p1, p2 = self.place[axis1], self.place[axis2]
        if 0 < t < 3:
            block = self.block(q, wrap(p1 - d1 * t))
            self.near[t - 1, q] = self.near[t - 1, q] + self.own[block, :]
        elif t == 3:
            self.near[2, q] = self.near[2, q] + self.own[self.block(q, self.own1(q)), :]
        elif t == 4:
            rows = pl.ds(pl.multiple_of(p2 * 16, 16), 16)
            total = self.near[2, q, rows].astype(F32) + self.far[q, 0].astype(F32)
            total = total + (self.far[q, 1].astype(F32) + self.far[q, 2].astype(F32))
            self.g[self.piece(q, p2), :] = total.astype(BF16)
        for one in self.copies(q, t):
            one.start()

    def step(self, t):
        self.wait(t - 1)
        if t < self.LAST:
            for q in range(4):
                self.start(q, t)

    def finish(self):
        all_of = self.own.at[0 : 4 * (6 * 64 + 6 * 16)]
        pltpu.make_async_copy(all_of, all_of, self.sent).wait()


def layers_kernel(
    lens_h, tok_h, cot_h, wqkv_h, wout_h, wup_h, wdown_h, gains_h, feats_h, cst_h,
    acts, in_grads, gsum, gain_out, feat_out,
    lens, xin, glow, aux, wqkv, wout, wup, wdown, gains, feats, cst, gbuf, near, far,
    fw, mask, rot, nrm, attn_in, mlp_in, tq, tk, pq, pk, qf, kf, vf, sb, den, att,
    mixed, hidden, ghp, gm, gproj, gpre, nx, inv_x,
    fpart, frx, fcs, fin, bpart, brx, bcs, bin_, xrx, small, srx, sall,
    load_s, frx_s, fin_s, facts_s, brx_s, bin_s, bout_s, x_s, xsib_s, ret_s, small_s,
    sent_s, got_s, all_s,
):
    s = lax.axis_index("section")
    t = lax.axis_index("tensor")
    dp = lax.axis_index("dp")
    zh = t // 2
    c = lax.rem(t, 2)
    sibling = {"tensor": zh * 2 + 1 - c}
    partner = {"tensor": lax.rem(t + 2, 4)}
    across = [{"section": 1 - s, "tensor": z * 2 + c} for z in range(2)]
    place = {"x": dp // 4, "y": lax.rem(dp, 4)}

    def at(axis, d):
        there = dict(place)
        there[axis] = lax.rem(place[axis] + d + 4, 4)
        return {"dp": there["x"] * 4 + there["y"]}

    def load(src, dst, k):
        return pltpu.make_async_copy(src, dst, load_s.at[k])

    first, second = slice(0, ROWS), slice(ROWS, ALL_ROWS)
    load_lens = load(lens_h, lens, 12)
    load_gains = load(gains_h, gains, 0)
    load_feats = load(feats_h, feats, 1)
    load_cst = load(cst_h, cst, 2)
    load_qkv = [load(wqkv_h.at[k], wqkv.at[k], 3 + k) for k in range(3)]
    load_up = load(wup_h, wup, 6)
    load_out = load(wout_h, wout, 7)
    load_down = load(wdown_h, wdown, 8)

    @pl.when(s == 0)
    def _():
        load(tok_h.at[first], xin.at[first], 9).start()
        for one in (load_gains, load_lens, load_feats, load_cst, *load_qkv):
            one.start()

    @pl.when(s == 1)
    def _():
        load(cot_h, glow, 9).start()
        for one in (load_down, load_out, load_lens, load_cst, load_gains, load_feats, *load_qkv, load_up):
            one.start()
        load(tok_h, aux, 11).start()

    barrier = pltpu.get_barrier_semaphore()
    peers = [sibling, partner, *across] + [at(axis, d) for axis in ("x", "y") for d in (1, 2, 3)]
    for target in peers:
        pl.semaphore_signal(barrier, inc=1, device_id=target, device_id_type=MESH)

    def remote(src, dst, sems, index, target):
        return pltpu.make_async_remote_copy(
            src_ref=src, dst_ref=dst, send_sem=sems.at[(0, *index)],
            recv_sem=sems.at[(1, *index)], device_id=target, device_id_type=MESH,
        )

    def micro_rows(m):
        if isinstance(m, int):
            return slice(m * ROWS, (m + 1) * ROWS)
        return pl.ds(pl.multiple_of(m * ROWS, ROWS), ROWS)

    def half_rows(m):
        return pl.ds(pl.multiple_of(m * ROWS + c * HALF, HALF), HALF)

    def part_rows(m, core, k):
        return pl.ds(pl.multiple_of(m * ROWS + core * HALF + k * 64, 64), 64)

    keep_rows = pl.ds(pl.multiple_of(c * HALF, HALF), HALF)
    give_rows = pl.ds(pl.multiple_of((1 - c) * HALF, HALF), HALF)

    def cols(n):
        return slice(n * 256, (n + 1) * 256)

    def f_swap(m):
        return remote(fpart.at[m, give_rows], frx.at[m], frx_s, (m,), sibling)

    def f_spread(m):
        return remote(fcs.at[m], fin.at[m], fin_s, (m,), partner)

    def f_share(m):
        return remote(acts.at[half_rows(m)], acts.at[half_rows(m)], facts_s, (m,), sibling)

    def b_swap(m):
        return remote(bpart.at[m, give_rows], brx.at[m], brx_s, (m,), sibling)

    def b_spread(m):
        return remote(bcs.at[m], bin_.at[m], bin_s, (m,), partner)

    def b_share(m):
        return remote(in_grads.at[half_rows(m)], in_grads.at[half_rows(m)], bout_s, (m,), sibling)

    def cross(src, m, z, k, arrival=False):
        here = z if arrival else zh
        rows = slice(k * 64, (k + 1) * 64)
        return pltpu.make_async_remote_copy(
            src_ref=src.at[m, rows], dst_ref=xrx.at[m, here, rows], send_sem=x_s.at[0, m, z, k],
            recv_sem=x_s.at[1, m, here, k], device_id=across[z], device_id_type=MESH,
        )

    def send_back(m, z, arrival=False):
        rows = part_rows(m, c, z if arrival else zh)
        return pltpu.make_async_remote_copy(
            src_ref=xin.at[rows], dst_ref=acts.at[rows], send_sem=ret_s.at[0, m, z],
            recv_sem=ret_s.at[1, m, z if arrival else zh], device_id=across[z], device_id_type=MESH,
        )

    def x_share(buf, m, k):
        rows = part_rows(m, c, k)
        return remote(buf.at[rows], buf.at[rows], xsib_s, (m, k), sibling)

    def chip_sum(part, rx, cs, m):
        cs[m] = (part[m, keep_rows].astype(F32) + rx[m].astype(F32)).astype(BF16)

    def send_across(cs, m):
        for k in range(2):
            for z in range(2):
                cross(cs, m, z, k).start()

    def arrived(src, m, k):
        for z in range(2):
            cross(src, m, z, k, arrival=True).wait_recv()
        rows = slice(k * 64, (k + 1) * 64)
        return xrx[m, 0, rows].astype(F32) + xrx[m, 1, rows].astype(F32)

    def context(m):
        length = lens[pl.ds(m, 1), :]
        first_end = length[:, 0:1]
        second_end = first_end + length[:, 1:2]
        third_end = second_end + length[:, 2:3]
        i = lax.broadcasted_iota(jnp.int32, (ROWS, ROWS), 0)
        j = lax.broadcasted_iota(jnp.int32, (ROWS, ROWS), 1)
        start = jnp.where(i >= first_end, first_end, 0)
        start = jnp.where(i >= second_end, second_end, start)
        start = jnp.where(i >= third_end, third_end, start)
        mask[m] = ((j <= i) & (j >= start)).astype(F32)
        hot = ((i - start) == j).astype(F32).astype(BF16)
        cosine = dot_nn(hot, cst[0:256, :]) + dot_nn(hot, cst[256:512, :])
        sine = dot_nn(hot, cst[512:768, :]) + dot_nn(hot, cst[768:1024, :])
        column = lax.rem(j, DIM)
        rot[m, 0] = cosine
        rot[m, 1] = jnp.where(column < ROT // 2, -sine, 0.0)
        rot[m, 2] = jnp.where(column >= ROT // 2, sine, 0.0)

    def norm_rows(rows):
        normed, _ = ln_rows(xin[rows, :].astype(F32))
        nrm[rows, :] = normed
        attn_in[rows, :] = (normed * gains[0:1, :]).astype(BF16)
        mlp_in[rows, :] = (normed * gains[1:2, :]).astype(BF16)

    def features(projected, m, turned_ref, phi_ref, low_ref):
        turned = (
            projected * rot[m, 0]
            + pltpu.roll(projected, LOCAL - ROT // 2, 1) * rot[m, 1]
            + pltpu.roll(projected, ROT // 2, 1) * rot[m, 2]
        )
        turned_ref[m] = turned
        high, rest = low_pieces(turned)
        square_high, square_rest = low_pieces(turned * turned)
        pieces = jnp.concatenate([high, rest, high, square_high, square_rest], axis=1)
        phi = fw[...] * jnp.exp(dot_nn(pieces, cst[1024:2304, :]))
        phi_ref[m] = phi
        low_ref[m] = phi.astype(BF16)

    def head_row(h):
        return cst[2816 + h * DIM : 2817 + h * DIM, :]

    def attend(m):
        queries, keys, values = qf[m], kf[m], vf[m]
        kept = mask[m] > 0.5
        total = jnp.zeros((ROWS, 2 * LOCAL), F32)
        for h in range(HEADS):
            row = head_row(h)
            scores = jnp.where(kept, dot_nt(queries * row, keys), 0.0).astype(BF16)
            sb[m, h] = scores
            right = jnp.concatenate(
                [values * row, jnp.broadcast_to(row, (ROWS, LOCAL))], axis=1
            )
            total = total + dot_nn(scores, right)
        norm = total[:, LOCAL:]
        attended = total[:, :LOCAL] / norm
        den[m] = norm
        att[m] = attended
        mixed[micro_rows(m), :] = attended.astype(BF16)

    def front(m):
        rows = micro_rows(m)
        normed_low = attn_in[rows, :]
        features(dot_nn(normed_low, wqkv[0]), m, tq, pq, qf)
        features(dot_nn(normed_low, wqkv[1]), m, tk, pk, kf)
        vf[m] = dot_nn(normed_low, wqkv[2]).astype(BF16)
        attend(m)
        for n in range(4):
            pre = dot_nn(mlp_in[rows, :], wup[:, cols(n)])
            cdf, slope = normal_cdf(pre)
            hidden[rows, cols(n)] = (pre * cdf).astype(BF16)
            gpre[rows, cols(n)] = (ghp[rows, cols(n)] * slope).astype(BF16)
            ghp[rows, cols(n)] = slope

    def back_out(m):
        rows = micro_rows(m)
        for n in range(4):
            tile = dot_nn(mixed[rows, :], wout[:, cols(n)])
            tile = tile + dot_nn(hidden[rows, :], wdown[:, cols(n)])
            fpart[m, :, cols(n)] = tile.astype(BF16)

    def grad_hidden(m, known):
        rows = micro_rows(m)
        for n in range(4):
            grad = dot_nt(glow[rows, :], wdown[cols(n), :])
            if known:
                gpre[rows, cols(n)] = (grad * ghp[rows, cols(n)]).astype(BF16)
            else:
                ghp[rows, cols(n)] = grad

    def grad_mixed(m):
        rows = micro_rows(m)
        gm[rows, :] = dot_nt(glow[rows, :], wout[...]).astype(BF16)

    def feature_back(grad_phi, m, turned_ref, phi_ref):
        grad_s = grad_phi * phi_ref[m]
        small[0, 2:3, 0:LOCAL] = small[0, 2:3, 0:LOCAL] + jnp.sum(grad_s, axis=0, keepdims=True)
        low = grad_s.astype(BF16)
        grad = dot_nn(low, cst[2304:2560, :]) - turned_ref[m] * dot_nn(low, cst[2560:2816, :])
        return (
            grad * rot[m, 0]
            - pltpu.roll(grad, LOCAL - ROT // 2, 1) * rot[m, 1]
            - pltpu.roll(grad, ROT // 2, 1) * rot[m, 2]
        )

    def attend_back(m):
        rows = micro_rows(m)
        grad_num = gm[rows, :].astype(F32) / den[m]
        grad_low = grad_num.astype(BF16)
        high, rest = low_pieces(grad_low.astype(F32) * att[m])
        ones = cst[2816:3072, :]
        grad_den = -(dot_nn(high, ones) + dot_nn(rest, ones))
        kept = mask[m] > 0.5
        queries, keys, values = qf[m], kf[m], vf[m]
        grad_q = jnp.zeros((ROWS, LOCAL), F32)
        grad_k = jnp.zeros((ROWS, LOCAL), F32)
        grad_v = jnp.zeros((ROWS, LOCAL), F32)
        for h in range(HEADS):
            row = head_row(h)
            given = grad_low * row
            grad_scores = dot_nt(given, values) + grad_den[:, h * DIM : h * DIM + 1]
            grad_scores = jnp.where(kept, grad_scores, 0.0).astype(BF16)
            grad_q = grad_q + dot_nn(grad_scores, keys * row)
            grad_k = grad_k + dot_tn(grad_scores, queries * row)
            grad_v = grad_v + dot_tn(sb[m, h], given)
        gproj[0, rows, :] = feature_back(grad_q, m, tq, pq).astype(BF16)
        gproj[1, rows, :] = feature_back(grad_k, m, tk, pk).astype(BF16)
        gproj[2, rows, :] = grad_v.astype(BF16)

    def back_in(m):
        rows = micro_rows(m)
        for n in range(4):
            here = cols(n)
            grad_a = dot_nt(gproj[0, rows, :], wqkv[0, here, :])
            grad_a = grad_a + dot_nt(gproj[1, rows, :], wqkv[1, here, :])
            grad_a = grad_a + dot_nt(gproj[2, rows, :], wqkv[2, here, :])
            grad_m = dot_nt(gpre[rows, :], wup[here, :])
            tile = gains[0:1, here] * grad_a + gains[1:2, here] * grad_m
            bpart[m, :, here] = tile.astype(BF16)
            normed = nrm[rows, here]
            for k, grad in enumerate((grad_a, grad_m)):
                line = jnp.sum(normed * grad, axis=0, keepdims=True)
                small[0, k : k + 1, here] = small[0, k : k + 1, here] + line

    def grads_down(n):
        gbuf[cols(n), :] = dot_tn(hidden[:, cols(n)], glow[...]).astype(BF16)
        sums[0].start(n, 0)

    def grads_up(n):
        rows = slice(1024 + n * 256, 1280 + n * 256)
        gbuf[rows, :] = dot_tn(mlp_in[:, cols(n)], gpre[...]).astype(BF16)
        sums[1].start(n, 0)

    def grads_attn(n):
        rows = slice(2048 + n * 256, 2304 + n * 256)
        for k in range(3):
            gbuf[rows, cols(k)] = dot_tn(attn_in[:, cols(n)], gproj[k]).astype(BF16)
        gbuf[rows, cols(3)] = dot_tn(mixed[...], glow[:, cols(n)]).astype(BF16)
        sums[2].start(n, 0)

    def finish_forward(m):
        f_spread(m).wait_recv()
        total = fcs[m].astype(F32) + fin[m].astype(F32)
        acts[half_rows(m), :] = (xin[half_rows(m), :].astype(F32) + total).astype(BF16)
        f_share(m).start()

    def finish_backward(m):
        b_spread(m).wait_recv()
        total = bcs[m].astype(F32) + bin_[m].astype(F32)
        normed, inv = ln_rows(xin[half_rows(m), :].astype(F32))
        in_grads[half_rows(m), :] = glow[half_rows(m), :].astype(F32) + ln_back(total, normed, inv)
        b_share(m).start()

    sums = [
        Sums(gbuf, gsum, j * 1024, near.at[j], far.at[j], sent_s.at[j], got_s.at[j], place, at)
        for j in range(PARTS)
    ]

    def hop(j, step):
        sums[j].step(step)

    def small_step(k):
        def copy(k):
            if k < 2:
                return [remote(small.at[k], srx.at[k], small_s, (k,), (sibling, partner)[k])]
            axis = "xy"[k - 2]
            return [
                pltpu.make_async_remote_copy(
                    src_ref=small.at[k], dst_ref=sall.at[k - 2, place[axis]],
                    send_sem=all_s.at[0, k - 2], recv_sem=all_s.at[1, k - 2],
                    device_id=at(axis, d), device_id_type=MESH,
                )
                for d in (1, 2, 3)
            ]

        if k == -1:
            for j in range(2):
                copy(j)[0].wait_send()
                three = sall.at[j, 0:3]
                pltpu.make_async_copy(three, three, all_s.at[0, j]).wait()
            return
        if k in (1, 2):
            copy(k - 1)[0].wait_recv()
        if k > 2:
            three = sall.at[k - 3, 0:3]
            pltpu.make_async_copy(three, three, all_s.at[1, k - 3]).wait()
        if k in (1, 2):
            line = lax.broadcasted_iota(jnp.int32, (8, WIDTH), 0)
            small[k] = small[k - 1] + jnp.where(line < 2, srx[k - 1], 0.0)
        if k in (3, 4):
            parts = sall[k - 3]
            small[k] = (parts[0] + parts[1]) + (parts[2] + parts[3])
        if k in (2, 3):
            sall[k - 2, place["xy"[k - 2]]] = small[k]
        if k < 4:
            for one in copy(k):
                one.start()

    def spread_feats():
        exact = dot_exact(feats[...], cst[3072:3136, :].astype(F32), 0)
        fw[...] = jnp.sum(exact * heads_of(), axis=0, keepdims=True)

    def heads_of():
        return jnp.concatenate([head_row(h) for h in range(HEADS)], axis=0).astype(F32)

    def wait_all(*copies):
        for one in copies:
            one.wait()

    small[...] = jnp.zeros(small.shape, F32)

    @pl.when(s == 0)
    def _():
        def forward(m, carry):
            @pl.when(m == 0)
            def _():
                wait_all(load(tok_h.at[first], xin.at[first], 9), load_gains)
                for one in (load_up, load_out, load_down, load(tok_h.at[second], xin.at[second], 10)):
                    one.start()
                load(cot_h, aux, 11).start()

            for k in range(4):
                norm_rows(pl.ds(pl.multiple_of(m * ROWS + k * 64, 64), 64))

            @pl.when(m == 0)
            def _():
                wait_all(load_lens, load_feats, load_cst)
                spread_feats()

            context(m)

            @pl.when(m == 0)
            def _():
                wait_all(*load_qkv, load_up)

            front(m)

            @pl.when(m == 0)
            def _():
                wait_all(load_out, load_down)

            back_out(m)

            @pl.when(m == 0)
            def _():
                pl.semaphore_wait(barrier, len(peers))

            f_swap(m).start()

            @pl.when(m == 0)
            def _():
                wait_all(load(tok_h.at[second], xin.at[second], 10), load(cot_h, aux, 11))

            f_swap(m).wait_recv()
            chip_sum(fpart, frx, fcs, m)
            send_across(fcs, m)
            return carry

        lax.fori_loop(0, MICROS, forward, 0)

        def gradient_in(m):
            for z in range(2):
                send_back(m, z, arrival=True).wait_recv()
            normed, inv = ln_rows(acts[half_rows(m), :].astype(F32))
            nx[m] = normed
            inv_x[m] = jnp.broadcast_to(inv, (HALF, 128))
            f_share(m).start()
            for k in range(2):
                total = arrived(bcs, m, k)
                rows = slice(k * 64, (k + 1) * 64)
                back = ln_back(total, nx[m, rows], inv_x[m, rows, 0:1])
                grad = aux[part_rows(m, c, k), :].astype(F32) + back
                glow[part_rows(m, c, k), :] = grad.astype(BF16)
                x_share(glow, m, k).start()
            for k in range(2):
                x_share(glow, m, k).wait_recv()

        def backward(m, carry):
            last = m == MICROS - 1
            gradient_in(m)

            @pl.when(last)
            def _():
                for n in range(4):
                    grads_down(n)

            grad_hidden(m, True)

            @pl.when(last)
            def _():
                for n in range(4):
                    grads_up(n)

            grad_mixed(m)
            attend_back(m)

            @pl.when(last)
            def _():
                for n in range(4):
                    grads_attn(n)
                hop(0, 1)

            back_in(m)
            b_swap(m).start()
            return carry

        lax.fori_loop(0, MICROS, backward, 0)
        hop(1, 1)
        for m in range(MICROS):
            b_swap(m).wait_recv()
            chip_sum(bpart, brx, bcs, m)
            b_spread(m).start()
        hop(2, 1)
        for m in range(MICROS):
            for k in range(2):
                x_share(glow, m, k).wait_send()
                for z in range(2):
                    cross(fcs, m, z, k).wait_send()

    @pl.when(s == 1)
    def _():
        wait_all(load(cot_h, glow, 9), load_down)
        for m in range(MICROS):
            grad_hidden(m, False)
        wait_all(load_out, load_lens, load_cst, load_gains, load_feats)
        spread_feats()
        for m in range(MICROS):
            grad_mixed(m)
            context(m)
        wait_all(*load_qkv, load_up, load(tok_h, aux, 11))
        pl.semaphore_wait(barrier, len(peers))

        def cross_over(m):
            b_swap(m).wait_recv()
            chip_sum(bpart, brx, bcs, m)
            send_across(bcs, m)

        def both(m, carry):
            for k in range(2):
                total = arrived(fcs, m, k)
                own = part_rows(m, c, k)
                xin[own, :] = (aux[own, :].astype(F32) + total).astype(BF16)
                x_share(xin, m, k).start()
                norm_rows(own)
            for z in range(2):
                send_back(m, z).start()
            for k in range(2):
                x_share(xin, m, k).wait_recv()
                norm_rows(part_rows(m, 1 - c, k))

            @pl.when(m == 1)
            def _():
                cross_over(0)

            front(m)
            attend_back(m)
            back_in(m)
            b_swap(m).start()
            return carry

        lax.fori_loop(0, MICROS, both, 0)
        grads_down(0)
        grads_down(1)
        cross_over(1)
        grads_down(2)
        grads_down(3)
        for n in range(4):
            grads_up(n)
        for n in range(4):
            grads_attn(n)
        hop(0, 1)
        for m in range(MICROS):
            back_out(m)
            f_swap(m).start()
        hop(1, 1)
        for m in range(MICROS):
            f_swap(m).wait_recv()
            chip_sum(fpart, frx, fcs, m)
            f_spread(m).start()
            for z in range(2):
                for k in range(2):
                    cross(bcs, m, z, k).wait_send()
            b_spread(m).start()
        hop(2, 1)
        for m in range(MICROS):
            for k in range(2):
                x_share(xin, m, k).wait_send()
                send_back(m, k).wait_send()

    for step in range(2, Sums.LAST + 1):
        for j in range(PARTS):
            hop(j, step)
        if step in (2, 3, 5, 6, 7):
            small_step((2, 3, 5, 6, 7).index(step))
        if step == 2:
            for m in range(MICROS):
                finish_backward(m)

            @pl.when(s == 1)
            def _():
                for m in range(MICROS):
                    finish_forward(m)
                    f_spread(m).wait_send()

        if step == 5:
            for m in range(MICROS):
                f_share(m).wait_recv()
                b_share(m).wait_recv()
                for one in (f_swap(m), f_share(m), b_swap(m), b_spread(m), b_share(m)):
                    one.wait_send()
        if step == 7:
            gain_out[...] = small[4, 0:2, :]
            line = jnp.broadcast_to(small[4, 2:3, 0:LOCAL] / fw[...], (HEADS, LOCAL))
            feat_out[...] = dot_exact(line * heads_of(), cst[3072:3136, :].astype(F32), 1)
            small_step(-1)
    for one in sums:
        one.finish()


def layers(lengths, tok, cot, wqkv, wout, wup, wdown, gains, feats):
    vm = pl.BlockSpec(memory_space=pltpu.VMEM)
    far_off = pl.BlockSpec(memory_space=pl.ANY)

    def low(*shape):
        return pltpu.VMEM(shape, BF16)

    def wide(*shape):
        return pltpu.VMEM(shape, F32)

    full = (MICROS, ROWS, WIDTH)
    half = (MICROS, HALF, WIDTH)
    square = (MICROS, ROWS, LOCAL)
    rows = (ALL_ROWS, WIDTH)
    sems = pltpu.SemaphoreType.DMA
    return pl.pallas_call(
        layers_kernel,
        out_shape=(
            low(*rows), wide(*rows), low(PARTS * WIDTH, WIDTH), wide(2, WIDTH), wide(HEADS, DIM),
        ),
        in_specs=[far_off] * 10,
        out_specs=(vm, vm, vm, vm, vm),
        scratch_shapes=[
            pltpu.VMEM((MICROS, 4), jnp.int32), low(*rows), low(*rows), low(*rows),
            low(3, WIDTH, LOCAL), low(LOCAL, WIDTH), low(WIDTH, WIDTH), low(WIDTH, WIDTH),
            wide(2, WIDTH), wide(HEADS, DIM), low(3136, LOCAL), low(PARTS * WIDTH, WIDTH),
            low(PARTS, 3, 4, 64, WIDTH), low(PARTS, 4, 3, 16, WIDTH),
            wide(1, LOCAL), wide(*square), wide(MICROS, 3, ROWS, LOCAL),
            wide(*rows), low(*rows), low(*rows),
            wide(*square), wide(*square), wide(*square), wide(*square),
            low(*square), low(*square), low(*square),
            low(MICROS, HEADS, ROWS, ROWS), wide(*square), wide(*square),
            low(ALL_ROWS, LOCAL), low(*rows), wide(*rows), low(ALL_ROWS, LOCAL),
            low(3, ALL_ROWS, LOCAL), low(*rows), wide(*half), wide(MICROS, HALF, 128),
            low(*full), low(*half), low(*half), low(*half),
            low(*full), low(*half), low(*half), low(*half),
            low(MICROS, 2, HALF, WIDTH), wide(5, 8, WIDTH), wide(2, 8, WIDTH), wide(2, 4, 8, WIDTH),
            sems((13,)),
            sems((2, MICROS)), sems((2, MICROS)), sems((2, MICROS)),
            sems((2, MICROS)), sems((2, MICROS)), sems((2, MICROS)),
            sems((2, MICROS, 2, 2)), sems((2, MICROS, 2)), sems((2, MICROS, 2)), sems((2, 2)),
            sems((PARTS,)), sems((PARTS, Sums.LAST)), sems((2, 2)),
        ],
        compiler_params=pltpu.CompilerParams(
            collective_id=0, has_side_effects=True, vmem_limit_bytes=53 * 2**20
        ),
        name="layers",
    )(lengths, tok, cot, wqkv, wout, wup, wdown, gains, feats, jnp.asarray(constants()))


def widen_kernel(
    grads, acts, in_grads, gains, feats, o_down, o_up, o_qkv, o_out, o_acts, o_in, o_gains, o_feats,
    down, up, qkv, out, sems, more,
):
    def copies(n):
        rows = pl.ds(pl.multiple_of(n * 256, 256), 256)
        return [
            pltpu.make_async_copy(down.at[rows], o_down.at[rows], sems.at[0, n]),
            pltpu.make_async_copy(up.at[rows], o_up.at[rows], sems.at[1, n]),
            pltpu.make_async_copy(qkv.at[:, rows], o_qkv.at[:, rows], sems.at[2, n]),
            pltpu.make_async_copy(out.at[n], o_out.at[:, rows], sems.at[3, n]),
        ]

    whole = [
        pltpu.make_async_copy(src, dst, more.at[k])
        for k, (src, dst) in enumerate(
            ((in_grads, o_in), (acts, o_acts), (gains, o_gains), (feats, o_feats))
        )
    ]
    for one in whole:
        one.start()

    def body(n, carry):
        rows = pl.ds(pl.multiple_of(n * 256, 256), 256)
        attn = pl.ds(pl.multiple_of(2 * WIDTH + n * 256, 256), 256)
        first, second, third, fourth = copies(n)
        down[rows, :] = grads[rows, :].astype(F32)
        first.start()
        up[rows, :] = grads[pl.ds(pl.multiple_of(WIDTH + n * 256, 256), 256), :].astype(F32)
        second.start()
        for k in range(3):
            qkv[k, rows, :] = grads[attn, k * 256 : (k + 1) * 256].astype(F32)
        third.start()
        out[n] = grads[attn, 768:].astype(F32)
        fourth.start()
        return carry

    lax.fori_loop(0, 4, body, 0)
    for n in range(4):
        for one in copies(n):
            one.wait()
    for one in whole:
        one.wait()


def widen(grads, acts, in_grads, gains, feats):
    vm = pl.BlockSpec(memory_space=pltpu.VMEM)
    far_off = pl.BlockSpec(memory_space=pl.ANY)

    def like(*shape):
        return jax.ShapeDtypeStruct(shape, F32)

    def wide(*shape):
        return pltpu.VMEM(shape, F32)

    return pl.pallas_call(
        widen_kernel,
        in_specs=[vm] * 5,
        out_specs=[far_off] * 8,
        out_shape=(
            like(WIDTH, WIDTH), like(WIDTH, WIDTH), like(3, WIDTH, LOCAL), like(LOCAL, WIDTH),
            jax.ShapeDtypeStruct((ALL_ROWS, WIDTH), BF16), like(ALL_ROWS, WIDTH),
            like(2, WIDTH), like(HEADS, DIM),
        ),
        scratch_shapes=[
            wide(WIDTH, WIDTH), wide(WIDTH, WIDTH), wide(3, WIDTH, LOCAL), wide(4, LOCAL, LOCAL),
            pltpu.SemaphoreType.DMA((4, 4)), pltpu.SemaphoreType.DMA((4,)),
        ],
        compiler_params=pltpu.CompilerParams(vmem_limit_bytes=40 * 2**20),
        name="widen",
    )(grads, acts, in_grads, gains, feats)


def per_device(
    tokens, lengths, cotangent, qkv_weight, out_weight, up_weight, down_weight, norm_gains,
    feat_weights,
):
    acts, in_grads, grads, gains, feats = layers(
        lengths, tokens, cotangent, jnp.transpose(qkv_weight[0], (1, 0, 2)), out_weight[0],
        up_weight[0], down_weight[0], norm_gains[0], feat_weights[0],
    )
    down, up, qkv, out, acts, in_grads, gains, feats = widen(grads, acts, in_grads, gains, feats)
    qkv = jnp.transpose(qkv, (1, 0, 2))
    return tuple(one[None] for one in (acts, in_grads, qkv, out, up, down, gains, feats))


PLACED = (
    P("dp", None),
    P("dp", None),
    P("dp", None),
    P("section", None, None, "tensor"),
    P("section", "tensor", None),
    P("section", None, "tensor"),
    P("section", "tensor", None),
    P("section", None, None),
    P("section", "tensor", None),
)
GIVEN = (
    P("section", "dp", None),
    P("section", "dp", None),
    P("section", None, None, "tensor"),
    P("section", "tensor", None),
    P("section", None, "tensor"),
    P("section", "tensor", None),
    P("section", None, None),
    P("section", "tensor", None),
)


def solution(mesh):
    return jax.shard_map(
        per_device, mesh=mesh, in_specs=PLACED, out_specs=GIVEN, check_vma=False
    )
```

```python
import functools
import math

import jax
import jax.numpy as jnp
import numpy as np
from jax import lax
from jax.experimental import pallas as pl
from jax.experimental.pallas import tpu as pltpu
from jax.sharding import PartitionSpec as P

F32 = jnp.float32
BF16 = jnp.bfloat16
MESH = pl.DeviceIdType.MESH
EPS = 1e-05
ROWS = 256
HALF = 128
WIDTH = 1024
LOCAL = 256
HEADS = 4
DIM = 64
ROT = 16
MICROS = 2
ALL_ROWS = MICROS * ROWS


def feature_table(head_dim, feat_count):
    golden = 0.6180339887498949
    row_grid = np.arange(feat_count)[:, None] + 0.5
    columns = np.arange(head_dim)[None, :] * 1.0
    points = np.mod(row_grid * (2.0 * columns + 1.0) / feat_count + golden * columns, 1.0)
    radius = np.sqrt(-2.0 * np.log(points[:, 0::2]))
    turning = 2.0 * np.pi * points[:, 1::2]
    omega_rows = np.stack([radius * np.cos(turning), radius * np.sin(turning)], axis=2).reshape(
        feat_count, head_dim
    )
    frequency = np.arange(head_dim)[:, None] * 1.0
    cosine_basis = np.sqrt(2.0 / head_dim) * np.cos(
        np.pi * (2.0 * columns + 1.0) * frequency / (2.0 * head_dim)
    )
    cosine_basis = np.where(frequency == 0, np.sqrt(0.5), 1.0) * cosine_basis
    return np.sum(omega_rows[:, :, None] * cosine_basis[None, :, :], axis=1)


def low_pieces(values):
    high = values.astype(BF16)
    rest = (values - high.astype(values.dtype)).astype(BF16)
    return high, rest


def constants():
    table = feature_table(DIM, DIM).astype(np.float32)
    eye = np.eye(HEADS, dtype=np.float32)
    blocks = np.kron(eye, table.T / math.sqrt(DIM)).astype(np.float32)
    ones = np.kron(eye, np.ones((DIM, DIM), np.float32))
    high, rest = low_pieces(blocks)
    scaled = (ones * (-1.0 / (2.0 * DIM))).astype(BF16)
    forward = np.concatenate([high, high, rest, scaled, scaled], axis=0)
    backward = np.concatenate([blocks.T.astype(BF16), (ones / DIM).astype(BF16)], axis=1)
    half_rot = ROT // 2
    inverse = (10000.0 ** (-2.0 * np.arange(half_rot) / ROT)).astype(np.float32)
    angles = np.arange(ROWS, dtype=np.float32)[:, None] * inverse[None, :]
    cosine = np.ones((ROWS, DIM), np.float32)
    sine = np.zeros((ROWS, DIM), np.float32)
    for start in (0, half_rot):
        cosine[:, start : start + half_rot] = np.cos(angles.astype(np.float64))
        sine[:, start : start + half_rot] = np.sin(angles.astype(np.float64))
    cosine = np.tile(cosine, (1, HEADS))
    sine = np.tile(sine, (1, HEADS))
    turns = np.concatenate([*low_pieces(cosine), *low_pieces(sine)], axis=1)
    spread = np.tile(np.eye(DIM, dtype=np.float32), (1, HEADS))
    return np.concatenate(
        [
            *np.split(turns, 4, axis=1), forward, *np.split(backward, 2, axis=1), ones.astype(BF16),
            spread.astype(BF16),
        ],
        axis=0,
    )


def dot_nn(a, b):
    return lax.dot_general(a, b, (((1,), (0,)), ((), ())), preferred_element_type=F32)


def dot_nt(a, b):
    return lax.dot_general(a, b, (((1,), (1,)), ((), ())), preferred_element_type=F32)


def dot_exact(a, b, side):
    return lax.dot_general(
        a, b, (((1,), (side,)), ((), ())), preferred_element_type=F32,
        precision=lax.Precision.HIGHEST,
    )


def dot_tn(a, b):
    return lax.dot_general(a, b, (((0,), (0,)), ((), ())), preferred_element_type=F32)


def normal_cdf(v):
    bell = jnp.exp(-0.5 * v * v)
    t = pl.reciprocal(1.0 + (0.3275911 * math.sqrt(0.5)) * jnp.abs(v))
    poly = 0.5 * 1.061405429 * t - 0.5 * 1.453152027
    for coefficient in (1.421413741, -0.284496736, 0.254829592):
        poly = poly * t + 0.5 * coefficient
    tail = poly * t * bell
    cdf = jnp.where(v >= 0.0, 1.0 - tail, tail)
    return cdf, cdf + v * bell * (1.0 / math.sqrt(2.0 * math.pi))


def ln_rows(x):
    mean = jnp.mean(x, axis=-1, keepdims=True)
    centered = x - mean
    inv = lax.rsqrt(jnp.mean(centered * centered, axis=-1, keepdims=True) + EPS)
    return centered * inv, inv


def ln_back(combined, normed, inv):
    mean_c = jnp.mean(combined, axis=-1, keepdims=True)
    mean_p = jnp.mean(combined * normed, axis=-1, keepdims=True)
    return inv * (combined - mean_c - normed * mean_p)


PARTS = 3


ORDER = (
    (0, 2), (2, 1), (1, 2), (0, 3), (2, 2), (1, 3), (0, 4), (2, 3),
    (1, 4), (2, 4), (0, 5), (1, 5), (2, 5), (0, 6), (1, 6), (2, 6),
)


def wrap(v):
    return lax.rem(v + 8, 4)


class Sums:
    LAST = 6

    def __init__(self, own, g, row0, near, far, sent, got, place, at):
        self.own, self.g, self.row0, self.at = own, g, row0, at
        self.near, self.far, self.sent, self.got, self.place = near, far, sent, got, place

    def ends(self, q):
        axis1, axis2 = ("x", "y") if q == 0 else ("y", "x")
        return axis1, axis2, self.place[axis1], self.place[axis2]

    def half(self, q, b, h):
        return pl.ds(pl.multiple_of(self.row0 + q * 512 + b * 128 + h * 64, 64), 64)

    def piece(self, q, k):
        _, _, p1, _ = self.ends(q)
        return pl.ds(pl.multiple_of(self.row0 + q * 512 + p1 * 128 + k * 32, 32), 32)

    def near_piece(self, q, k):
        return (q, 2 + k // 2, pl.ds(pl.multiple_of(lax.rem(k, 2) * 32, 32), 32))

    def copies(self, q, t):
        axis1, axis2, p1, p2 = self.ends(q)
        near, own, g = self.near, self.own, self.g
        up, down = (axis1, 1), (axis1, 3)
        if t == 0:
            plan = [
                (own.at[self.half(q, wrap(p1 + 2), 0)], near.at[q, 0], up, 0),
                (own.at[self.half(q, wrap(p1 + 2), 1)], near.at[q, 1], down, 0),
                (own.at[self.half(q, wrap(p1 + 1), 1)], near.at[q, 3], up, 1),
                (own.at[self.half(q, wrap(p1 - 1), 0)], near.at[q, 2], down, 1),
            ]
        elif t == 1:
            plan = [(near.at[q, 0], near.at[q, 4], up, 2), (near.at[q, 1], near.at[q, 5], down, 2)]
        elif t == 2:
            plan = [
                (near.at[self.near_piece(q, wrap(p2 + k + 1))], self.far.at[q, k], (axis2, k + 1), 3)
                for k in range(3)
            ]
        elif t == 3:
            src = g.at[self.piece(q, p2)]
            plan = [(src, src, (axis2, k + 1), 4) for k in range(3)]
        elif t == 4:
            first, second = g.at[self.half(q, p1, 0)], g.at[self.half(q, p1, 1)]
            plan = [
                (first, first, up, 5), (second, second, down, 5),
                (second, second, up, 6), (first, first, down, 6),
            ]
        else:
            first = g.at[self.half(q, wrap(p1 - 1), 0)]
            second = g.at[self.half(q, wrap(p1 + 1), 1)]
            plan = [(first, first, up, 7), (second, second, down, 7)]
        return [
            pltpu.make_async_remote_copy(
                src_ref=src, dst_ref=dst, send_sem=self.sent, recv_sem=self.got.at[k],
                device_id=self.at(*target), device_id_type=MESH,
            )
            for src, dst, target, k in plan
        ]

    def wait(self, k):
        if k < 3:
            all_of = self.near.at[:, 2 * k : 2 * k + 2]
        elif k == 3:
            all_of = self.far
        else:
            all_of = self.g.at[self.row0 : self.row0 + (192 if k == 4 else 256)]
        pltpu.make_async_copy(all_of, all_of, self.got.at[k]).wait()

    def start(self, q, t):
        _, _, p1, p2 = self.ends(q)
        near, own = self.near, self.own
        if t == 1:
            near[q, 0] = near[q, 0] + own[self.half(q, wrap(p1 + 1), 0), :]
            near[q, 1] = near[q, 1] + own[self.half(q, wrap(p1 - 1), 1), :]
        elif t == 2:
            for h in range(2):
                total = near[q, 2 + h].astype(F32) + near[q, 4 + h].astype(F32)
                near[q, 2 + h] = (total + own[self.half(q, p1, h), :].astype(F32)).astype(BF16)
        elif t == 3:
            total = near[self.near_piece(q, p2)].astype(F32) + self.far[q, 0].astype(F32)
            total = total + (self.far[q, 1].astype(F32) + self.far[q, 2].astype(F32))
            self.g[self.piece(q, p2), :] = total.astype(BF16)
        for one in self.copies(q, t):
            one.start()

    def step(self, t):
        for k in ((), (0,), (1, 2), (3,), (4,), (5,), (6, 7))[t]:
            self.wait(k)
        if t < self.LAST:
            for q in range(2):
                self.start(q, t)

    def finish(self):
        all_of = self.own.at[0 : 2 * (12 * 64 + 6 * 32)]
        pltpu.make_async_copy(all_of, all_of, self.sent).wait()


def layers_kernel(
    lens_h, tok_h, cot_h, wqkv_h, wout_h, wup_h, wdown_h, gains_h, feats_h, cst_h,
    acts, in_grads, gsum, gain_out, feat_out,
    lens, xin, glow, aux, wqkv, wout, wup, wdown, gains, feats, cst, gbuf, near, far,
    fw, mask, rot, nrm, attn_in, mlp_in, tq, tk, pq, pk, qf, kf, vf, sb, den, att,
    mixed, hidden, ghp, gm, gproj, gpre, nx, inv_x,
    fpart, frx, fcs, fin, bpart, brx, bcs, bin_, xrx, small, srx, sall,
    load_s, frx_s, fin_s, facts_s, brx_s, bin_s, bout_s, x_s, xsib_s, ret_s, small_s,
    sent_s, got_s, all_s,
):
    s = lax.axis_index("section")
    t = lax.axis_index("tensor")
    dp = lax.axis_index("dp")
    zh = t // 2
    c = lax.rem(t, 2)
    sibling = {"tensor": zh * 2 + 1 - c}
    partner = {"tensor": lax.rem(t + 2, 4)}
    across = [{"section": 1 - s, "tensor": z * 2 + c} for z in range(2)]
    place = {"x": dp // 4, "y": lax.rem(dp, 4)}

    def at(axis, d):
        there = dict(place)
        there[axis] = lax.rem(place[axis] + d + 4, 4)
        return {"dp": there["x"] * 4 + there["y"]}

    def load(src, dst, k):
        return pltpu.make_async_copy(src, dst, load_s.at[k])

    first, second = slice(0, ROWS), slice(ROWS, ALL_ROWS)
    load_lens = load(lens_h, lens, 12)
    load_gains = load(gains_h, gains, 0)
    load_feats = load(feats_h, feats, 1)
    load_cst = load(cst_h, cst, 2)
    load_qkv = [load(wqkv_h.at[k], wqkv.at[k], 3 + k) for k in range(3)]
    load_up = load(wup_h, wup, 6)
    load_out = load(wout_h, wout, 7)
    load_down = load(wdown_h, wdown, 8)

    @pl.when(s == 0)
    def _():
        load(tok_h.at[first], xin.at[first], 9).start()
        for one in (load_gains, load_lens, load_feats, load_cst, *load_qkv):
            one.start()

    @pl.when(s == 1)
    def _():
        load(cot_h, glow, 9).start()
        for one in (load_down, load_out, load_lens, load_cst, load_gains, load_feats, *load_qkv, load_up):
            one.start()
        load(tok_h, aux, 11).start()

    barrier = pltpu.get_barrier_semaphore()
    peers = [sibling, partner, *across] + [at(axis, d) for axis in ("x", "y") for d in (1, 2, 3)]
    for target in peers:
        pl.semaphore_signal(barrier, inc=1, device_id=target, device_id_type=MESH)

    def remote(src, dst, sems, index, target):
        return pltpu.make_async_remote_copy(
            src_ref=src, dst_ref=dst, send_sem=sems.at[(0, *index)],
            recv_sem=sems.at[(1, *index)], device_id=target, device_id_type=MESH,
        )

    def micro_rows(m):
        if isinstance(m, int):
            return slice(m * ROWS, (m + 1) * ROWS)
        return pl.ds(pl.multiple_of(m * ROWS, ROWS), ROWS)

    def half_rows(m):
        return pl.ds(pl.multiple_of(m * ROWS + c * HALF, HALF), HALF)

    def part_rows(m, core, k):
        return pl.ds(pl.multiple_of(m * ROWS + core * HALF + k * 64, 64), 64)

    keep_rows = pl.ds(pl.multiple_of(c * HALF, HALF), HALF)
    give_rows = pl.ds(pl.multiple_of((1 - c) * HALF, HALF), HALF)

    def cols(n):
        return slice(n * 256, (n + 1) * 256)

    def f_swap(m):
        return remote(fpart.at[m, give_rows], frx.at[m], frx_s, (m,), sibling)

    def f_spread(m):
        return remote(fcs.at[m], fin.at[m], fin_s, (m,), partner)

    def f_share(m):
        return remote(acts.at[half_rows(m)], acts.at[half_rows(m)], facts_s, (m,), sibling)

    def b_swap(m):
        return remote(bpart.at[m, give_rows], brx.at[m], brx_s, (m,), sibling)

    def b_spread(m):
        return remote(bcs.at[m], bin_.at[m], bin_s, (m,), partner)

    def b_share(m):
        return remote(in_grads.at[half_rows(m)], in_grads.at[half_rows(m)], bout_s, (m,), sibling)

    def cross(src, m, z, k, arrival=False):
        here = z if arrival else zh
        rows = slice(k * 64, (k + 1) * 64)
        return pltpu.make_async_remote_copy(
            src_ref=src.at[m, rows], dst_ref=xrx.at[m, here, rows], send_sem=x_s.at[0, m, z, k],
            recv_sem=x_s.at[1, m, here, k], device_id=across[z], device_id_type=MESH,
        )

    def send_back(m, z, arrival=False):
        rows = part_rows(m, c, z if arrival else zh)
        return pltpu.make_async_remote_copy(
            src_ref=xin.at[rows], dst_ref=acts.at[rows], send_sem=ret_s.at[0, m, z],
            recv_sem=ret_s.at[1, m, z if arrival else zh], device_id=across[z], device_id_type=MESH,
        )

    def x_share(buf, m, k):
        rows = part_rows(m, c, k)
        return remote(buf.at[rows], buf.at[rows], xsib_s, (m, k), sibling)

    def chip_sum(part, rx, cs, m):
        cs[m] = (part[m, keep_rows].astype(F32) + rx[m].astype(F32)).astype(BF16)

    def send_across(cs, m):
        for k in range(2):
            for z in range(2):
                cross(cs, m, z, k).start()

    def arrived(src, m, k):
        for z in range(2):
            cross(src, m, z, k, arrival=True).wait_recv()
        rows = slice(k * 64, (k + 1) * 64)
        return xrx[m, 0, rows].astype(F32) + xrx[m, 1, rows].astype(F32)

    def context(m):
        length = lens[pl.ds(m, 1), :]
        first_end = length[:, 0:1]
        second_end = first_end + length[:, 1:2]
        third_end = second_end + length[:, 2:3]
        i = lax.broadcasted_iota(jnp.int32, (ROWS, ROWS), 0)
        j = lax.broadcasted_iota(jnp.int32, (ROWS, ROWS), 1)
        start = jnp.where(i >= first_end, first_end, 0)
        start = jnp.where(i >= second_end, second_end, start)
        start = jnp.where(i >= third_end, third_end, start)
        mask[m] = ((j <= i) & (j >= start)).astype(F32)
        hot = ((i - start) == j).astype(F32).astype(BF16)
        cosine = dot_nn(hot, cst[0:256, :]) + dot_nn(hot, cst[256:512, :])
        sine = dot_nn(hot, cst[512:768, :]) + dot_nn(hot, cst[768:1024, :])
        column = lax.rem(j, DIM)
        rot[m, 0] = cosine
        rot[m, 1] = jnp.where(column < ROT // 2, -sine, 0.0)
        rot[m, 2] = jnp.where(column >= ROT // 2, sine, 0.0)

    def norm_rows(rows):
        normed, _ = ln_rows(xin[rows, :].astype(F32))
        nrm[rows, :] = normed
        attn_in[rows, :] = (normed * gains[0:1, :]).astype(BF16)
        mlp_in[rows, :] = (normed * gains[1:2, :]).astype(BF16)

    def features(projected, m, turned_ref, phi_ref, low_ref):
        turned = (
            projected * rot[m, 0]
            + pltpu.roll(projected, LOCAL - ROT // 2, 1) * rot[m, 1]
            + pltpu.roll(projected, ROT // 2, 1) * rot[m, 2]
        )
        turned_ref[m] = turned
        high, rest = low_pieces(turned)
        square_high, square_rest = low_pieces(turned * turned)
        pieces = jnp.concatenate([high, rest, high, square_high, square_rest], axis=1)
        phi = fw[...] * jnp.exp(dot_nn(pieces, cst[1024:2304, :]))
        phi_ref[m] = phi
        low_ref[m] = phi.astype(BF16)

    def head_row(h):
        return cst[2816 + h * DIM : 2817 + h * DIM, :]

    def attend(m, up):
        queries, keys, values = qf[m], kf[m], vf[m]
        kept = mask[m] > 0.5
        total = jnp.zeros((ROWS, 2 * LOCAL), F32)
        for h in range(HEADS):
            row = head_row(h)
            scores = jnp.where(kept, dot_nt(queries * row, keys), 0.0).astype(BF16)
            sb[m, h] = scores
            right = jnp.concatenate(
                [values * row, jnp.broadcast_to(row, (ROWS, LOCAL))], axis=1
            )
            total = total + dot_nn(scores, right)
            if h % 2 == 0:
                up(2 + h // 2)
        norm = total[:, LOCAL:]
        attended = total[:, :LOCAL] / norm
        den[m] = norm
        att[m] = attended
        mixed[micro_rows(m), :] = attended.astype(BF16)

    def front(m):
        rows = micro_rows(m)
        normed_low = attn_in[rows, :]

        def up(n):
            pre = dot_nn(mlp_in[rows, :], wup[:, cols(n)])
            cdf, slope = normal_cdf(pre)
            hidden[rows, cols(n)] = (pre * cdf).astype(BF16)
            gpre[rows, cols(n)] = (ghp[rows, cols(n)] * slope).astype(BF16)
            ghp[rows, cols(n)] = slope

        queries = dot_nn(normed_low, wqkv[0])
        keys = dot_nn(normed_low, wqkv[1])
        up(0)
        features(queries, m, tq, pq, qf)
        up(1)
        features(keys, m, tk, pk, kf)
        vf[m] = dot_nn(normed_low, wqkv[2]).astype(BF16)
        attend(m, up)

    def back_out(m):
        rows = micro_rows(m)
        for n in range(4):
            tile = dot_nn(mixed[rows, :], wout[:, cols(n)])
            tile = tile + dot_nn(hidden[rows, :], wdown[:, cols(n)])
            fpart[m, :, cols(n)] = tile.astype(BF16)

    def grad_hidden(m, known):
        rows = micro_rows(m)
        for n in range(4):
            grad = dot_nt(glow[rows, :], wdown[cols(n), :])
            if known:
                gpre[rows, cols(n)] = (grad * ghp[rows, cols(n)]).astype(BF16)
            else:
                ghp[rows, cols(n)] = grad

    def grad_mixed(m):
        rows = micro_rows(m)
        gm[rows, :] = dot_nt(glow[rows, :], wout[...]).astype(BF16)

    def feature_back(grad_phi, m, turned_ref, phi_ref):
        grad_s = grad_phi * phi_ref[m]
        small[0, 2:3, 0:LOCAL] = small[0, 2:3, 0:LOCAL] + jnp.sum(grad_s, axis=0, keepdims=True)
        low = grad_s.astype(BF16)
        grad = dot_nn(low, cst[2304:2560, :]) - turned_ref[m] * dot_nn(low, cst[2560:2816, :])
        return (
            grad * rot[m, 0]
            - pltpu.roll(grad, LOCAL - ROT // 2, 1) * rot[m, 1]
            - pltpu.roll(grad, ROT // 2, 1) * rot[m, 2]
        )

    def attend_back(m):
        rows = micro_rows(m)
        grad_num = gm[rows, :].astype(F32) / den[m]
        grad_low = grad_num.astype(BF16)
        high, rest = low_pieces(grad_low.astype(F32) * att[m])
        ones = cst[2816:3072, :]
        grad_den = -(dot_nn(high, ones) + dot_nn(rest, ones))
        kept = mask[m] > 0.5
        queries, keys, values = qf[m], kf[m], vf[m]
        grad_q = jnp.zeros((ROWS, LOCAL), F32)
        grad_k = jnp.zeros((ROWS, LOCAL), F32)
        grad_v = jnp.zeros((ROWS, LOCAL), F32)
        for h in range(HEADS):
            row = head_row(h)
            given = grad_low * row
            grad_scores = dot_nt(given, values) + grad_den[:, h * DIM : h * DIM + 1]
            grad_scores = jnp.where(kept, grad_scores, 0.0).astype(BF16)
            grad_q = grad_q + dot_nn(grad_scores, keys * row)
            grad_k = grad_k + dot_tn(grad_scores, queries * row)
            grad_v = grad_v + dot_tn(sb[m, h], given)
            here = cols(h)
            grad_m = dot_nt(gpre[rows, :], wup[here, :])
            ghp[rows, here] = gains[1:2, here] * grad_m
            line = jnp.sum(nrm[rows, here] * grad_m, axis=0, keepdims=True)
            small[0, 1:2, here] = small[0, 1:2, here] + line
        gproj[0, rows, :] = feature_back(grad_q, m, tq, pq).astype(BF16)
        gproj[1, rows, :] = feature_back(grad_k, m, tk, pk).astype(BF16)
        gproj[2, rows, :] = grad_v.astype(BF16)

    def back_in(m):
        rows = micro_rows(m)
        for n in range(4):
            here = cols(n)
            grad_a = dot_nt(gproj[0, rows, :], wqkv[0, here, :])
            grad_a = grad_a + dot_nt(gproj[1, rows, :], wqkv[1, here, :])
            grad_a = grad_a + dot_nt(gproj[2, rows, :], wqkv[2, here, :])
            bpart[m, :, here] = (gains[0:1, here] * grad_a + ghp[rows, here]).astype(BF16)
            line = jnp.sum(nrm[rows, here] * grad_a, axis=0, keepdims=True)
            small[0, 0:1, here] = small[0, 0:1, here] + line

    def grads_down(n):
        gbuf[cols(n), :] = dot_tn(hidden[:, cols(n)], glow[...]).astype(BF16)
        if n % 2 == 1:
            sums[0].start(n // 2, 0)

    def grads_up(n):
        rows = slice(1024 + n * 256, 1280 + n * 256)
        gbuf[rows, :] = dot_tn(mlp_in[:, cols(n)], gpre[...]).astype(BF16)
        if n % 2 == 1:
            sums[1].start(n // 2, 0)

    def grads_attn(n):
        rows = slice(2048 + n * 256, 2304 + n * 256)
        for k in range(3):
            gbuf[rows, cols(k)] = dot_tn(attn_in[:, cols(n)], gproj[k]).astype(BF16)
        gbuf[rows, cols(3)] = dot_tn(mixed[...], glow[:, cols(n)]).astype(BF16)
        if n % 2 == 1:
            sums[2].start(n // 2, 0)

    def finish_forward(m):
        f_spread(m).wait_recv()
        total = fcs[m].astype(F32) + fin[m].astype(F32)
        acts[half_rows(m), :] = (xin[half_rows(m), :].astype(F32) + total).astype(BF16)
        f_share(m).start()

    def finish_backward(m):
        b_spread(m).wait_recv()
        total = bcs[m].astype(F32) + bin_[m].astype(F32)
        normed, inv = ln_rows(xin[half_rows(m), :].astype(F32))
        in_grads[half_rows(m), :] = glow[half_rows(m), :].astype(F32) + ln_back(total, normed, inv)
        b_share(m).start()

    sums = [
        Sums(gbuf, gsum, j * 1024, near.at[j], far.at[j], sent_s.at[j], got_s.at[j], place, at)
        for j in range(PARTS)
    ]

    def hop(j, step):
        sums[j].step(step)

    def small_step(k):
        def copy(k):
            if k < 2:
                return [remote(small.at[k], srx.at[k], small_s, (k,), (sibling, partner)[k])]
            axis = "xy"[k - 2]
            return [
                pltpu.make_async_remote_copy(
                    src_ref=small.at[k], dst_ref=sall.at[k - 2, place[axis]],
                    send_sem=all_s.at[0, k - 2], recv_sem=all_s.at[1, k - 2],
                    device_id=at(axis, d), device_id_type=MESH,
                )
                for d in (1, 2, 3)
            ]

        if k == -1:
            for j in range(2):
                copy(j)[0].wait_send()
                three = sall.at[j, 0:3]
                pltpu.make_async_copy(three, three, all_s.at[0, j]).wait()
            return
        if k in (1, 2):
            copy(k - 1)[0].wait_recv()
        if k > 2:
            three = sall.at[k - 3, 0:3]
            pltpu.make_async_copy(three, three, all_s.at[1, k - 3]).wait()
        if k in (1, 2):
            line = lax.broadcasted_iota(jnp.int32, (8, WIDTH), 0)
            small[k] = small[k - 1] + jnp.where(line < 2, srx[k - 1], 0.0)
        if k in (3, 4):
            parts = sall[k - 3]
            small[k] = (parts[0] + parts[1]) + (parts[2] + parts[3])
        if k in (2, 3):
            sall[k - 2, place["xy"[k - 2]]] = small[k]
        if k < 4:
            for one in copy(k):
                one.start()

    def spread_feats():
        exact = dot_exact(feats[...], cst[3072:3136, :].astype(F32), 0)
        fw[...] = jnp.sum(exact * heads_of(), axis=0, keepdims=True)

    def heads_of():
        return jnp.concatenate([head_row(h) for h in range(HEADS)], axis=0).astype(F32)

    def wait_all(*copies):
        for one in copies:
            one.wait()

    small[...] = jnp.zeros(small.shape, F32)

    @pl.when(s == 0)
    def _():
        def forward(m, carry):
            @pl.when(m == 0)
            def _():
                wait_all(load(tok_h.at[first], xin.at[first], 9), load_gains)
                for one in (load_up, load_out, load_down, load(tok_h.at[second], xin.at[second], 10)):
                    one.start()
                load(cot_h, aux, 11).start()

            for k in range(4):
                norm_rows(pl.ds(pl.multiple_of(m * ROWS + k * 64, 64), 64))

            @pl.when(m == 0)
            def _():
                wait_all(load_lens, load_feats, load_cst)
                spread_feats()

            context(m)

            @pl.when(m == 0)
            def _():
                wait_all(*load_qkv, load_up)

            front(m)

            @pl.when(m == 0)
            def _():
                wait_all(load_out, load_down)

            back_out(m)

            @pl.when(m == 0)
            def _():
                pl.semaphore_wait(barrier, len(peers))

            f_swap(m).start()

            @pl.when(m == 0)
            def _():
                wait_all(load(tok_h.at[second], xin.at[second], 10), load(cot_h, aux, 11))

            f_swap(m).wait_recv()
            chip_sum(fpart, frx, fcs, m)
            send_across(fcs, m)
            return carry

        lax.fori_loop(0, MICROS, forward, 0)

        def gradient_in(m):
            for z in range(2):
                send_back(m, z, arrival=True).wait_recv()
            normed, inv = ln_rows(acts[half_rows(m), :].astype(F32))
            nx[m] = normed
            inv_x[m] = jnp.broadcast_to(inv, (HALF, 128))
            f_share(m).start()
            for k in range(2):
                total = arrived(bcs, m, k)
                rows = slice(k * 64, (k + 1) * 64)
                back = ln_back(total, nx[m, rows], inv_x[m, rows, 0:1])
                grad = aux[part_rows(m, c, k), :].astype(F32) + back
                glow[part_rows(m, c, k), :] = grad.astype(BF16)
                x_share(glow, m, k).start()
            for k in range(2):
                x_share(glow, m, k).wait_recv()

        def backward(m, carry):
            last = m == MICROS - 1
            gradient_in(m)

            @pl.when(last)
            def _():
                for n in range(4):
                    grads_down(n)

            grad_hidden(m, True)

            @pl.when(last)
            def _():
                for n in range(4):
                    grads_up(n)

            grad_mixed(m)
            attend_back(m)

            @pl.when(last)
            def _():
                hop(0, 1)
                for n in range(4):
                    grads_attn(n)

            back_in(m)
            b_swap(m).start()
            return carry

        lax.fori_loop(0, MICROS, backward, 0)
        hop(1, 1)
        for m in range(MICROS):
            b_swap(m).wait_recv()
            chip_sum(bpart, brx, bcs, m)
            b_spread(m).start()
        for m in range(MICROS):
            for k in range(2):
                x_share(glow, m, k).wait_send()
                for z in range(2):
                    cross(fcs, m, z, k).wait_send()

    @pl.when(s == 1)
    def _():
        wait_all(load(cot_h, glow, 9), load_down)
        for m in range(MICROS):
            grad_hidden(m, False)
        wait_all(load_out, load_lens, load_cst, load_gains, load_feats)
        spread_feats()
        for m in range(MICROS):
            grad_mixed(m)
            context(m)
        wait_all(*load_qkv, load_up, load(tok_h, aux, 11))
        pl.semaphore_wait(barrier, len(peers))

        def cross_over(m):
            b_swap(m).wait_recv()
            chip_sum(bpart, brx, bcs, m)
            send_across(bcs, m)

        def take_in(m, k):
            total = arrived(fcs, m, k)
            own = part_rows(m, c, k)
            xin[own, :] = (aux[own, :].astype(F32) + total).astype(BF16)
            x_share(xin, m, k).start()

        def both(m, carry):
            @pl.when(m == 0)
            def _():
                for k in range(2):
                    take_in(0, k)
                    norm_rows(part_rows(0, c, k))
                for z in range(2):
                    send_back(0, z).start()

            @pl.when(m == 1)
            def _():
                for k in range(2):
                    norm_rows(part_rows(1, c, k))

            for k in range(2):
                x_share(xin, m, k).wait_recv()
                norm_rows(part_rows(m, 1 - c, k))

            @pl.when(m == 1)
            def _():
                cross_over(0)

            front(m)
            attend_back(m)

            @pl.when(m == 0)
            def _():
                for k in range(2):
                    take_in(1, k)
                for z in range(2):
                    send_back(1, z).start()

            back_in(m)
            b_swap(m).start()
            return carry

        lax.fori_loop(0, MICROS, both, 0)
        grads_down(0)
        grads_down(1)
        cross_over(1)
        grads_down(2)
        grads_down(3)
        for n in range(4):
            grads_up(n)
        hop(0, 1)
        for n in range(4):
            grads_attn(n)
        for m in range(MICROS):
            back_out(m)
            f_swap(m).start()
        hop(1, 1)
        for m in range(MICROS):
            f_swap(m).wait_recv()
            chip_sum(fpart, frx, fcs, m)
            f_spread(m).start()
            for z in range(2):
                for k in range(2):
                    cross(bcs, m, z, k).wait_send()
            b_spread(m).start()
        for m in range(MICROS):
            for k in range(2):
                x_share(xin, m, k).wait_send()
                send_back(m, k).wait_send()

    small_step(0)
    for part, step in ORDER:
        if part == 0 and 2 < step < 6:
            small_step(step - 2)
        hop(part, step)
        if part < PARTS - 1:
            continue
        if step == 4:
            for m in range(MICROS):
                finish_backward(m)

            @pl.when(s == 1)
            def _():
                for m in range(MICROS):
                    finish_forward(m)
                    f_spread(m).wait_send()

        if step == 5:
            small_step(4)
            gain_out[...] = small[4, 0:2, :]
            line = jnp.broadcast_to(small[4, 2:3, 0:LOCAL] / fw[...], (HEADS, LOCAL))
            feat_out[...] = dot_exact(line * heads_of(), cst[3072:3136, :].astype(F32), 1)
            small_step(-1)
            for m in range(MICROS):
                f_share(m).wait_recv()
                b_share(m).wait_recv()
                for one in (f_swap(m), f_share(m), b_swap(m), b_spread(m), b_share(m)):
                    one.wait_send()
    for one in sums:
        one.finish()


def layers(lengths, tok, cot, wqkv, wout, wup, wdown, gains, feats):
    vm = pl.BlockSpec(memory_space=pltpu.VMEM)
    far_off = pl.BlockSpec(memory_space=pl.ANY)

    def low(*shape):
        return pltpu.VMEM(shape, BF16)

    def wide(*shape):
        return pltpu.VMEM(shape, F32)

    full = (MICROS, ROWS, WIDTH)
    half = (MICROS, HALF, WIDTH)
    square = (MICROS, ROWS, LOCAL)
    rows = (ALL_ROWS, WIDTH)
    sems = pltpu.SemaphoreType.DMA
    return pl.pallas_call(
        layers_kernel,
        out_shape=(
            low(*rows), wide(*rows), low(PARTS * WIDTH, WIDTH), wide(2, WIDTH), wide(HEADS, DIM),
        ),
        in_specs=[far_off] * 10,
        out_specs=(vm, vm, vm, vm, vm),
        scratch_shapes=[
            pltpu.VMEM((MICROS, 4), jnp.int32), low(*rows), low(*rows), low(*rows),
            low(3, WIDTH, LOCAL), low(LOCAL, WIDTH), low(WIDTH, WIDTH), low(WIDTH, WIDTH),
            wide(2, WIDTH), wide(HEADS, DIM), low(3136, LOCAL), low(PARTS * WIDTH, WIDTH),
            low(PARTS, 2, 6, 64, WIDTH), low(PARTS, 2, 3, 32, WIDTH),
            wide(1, LOCAL), wide(*square), wide(MICROS, 3, ROWS, LOCAL),
            wide(*rows), low(*rows), low(*rows),
            wide(*square), wide(*square), wide(*square), wide(*square),
            low(*square), low(*square), low(*square),
            low(MICROS, HEADS, ROWS, ROWS), wide(*square), wide(*square),
            low(ALL_ROWS, LOCAL), low(*rows), wide(*rows), low(ALL_ROWS, LOCAL),
            low(3, ALL_ROWS, LOCAL), low(*rows), wide(*half), wide(MICROS, HALF, 128),
            low(*full), low(*half), low(*half), low(*half),
            low(*full), low(*half), low(*half), low(*half),
            low(MICROS, 2, HALF, WIDTH), wide(5, 8, WIDTH), wide(2, 8, WIDTH), wide(2, 4, 8, WIDTH),
            sems((13,)),
            sems((2, MICROS)), sems((2, MICROS)), sems((2, MICROS)),
            sems((2, MICROS)), sems((2, MICROS)), sems((2, MICROS)),
            sems((2, MICROS, 2, 2)), sems((2, MICROS, 2)), sems((2, MICROS, 2)), sems((2, 2)),
            sems((PARTS,)), sems((PARTS, 8)), sems((2, 2)),
        ],
        compiler_params=pltpu.CompilerParams(
            collective_id=0, has_side_effects=True, vmem_limit_bytes=53 * 2**20
        ),
        name="layers",
    )(lengths, tok, cot, wqkv, wout, wup, wdown, gains, feats, jnp.asarray(constants()))


def widen_kernel(
    grads, acts, in_grads, gains, feats, o_down, o_up, o_qkv, o_out, o_acts, o_in, o_gains, o_feats,
    down, up, qkv, out, sems, more,
):
    def copies(n):
        rows = pl.ds(pl.multiple_of(n * 256, 256), 256)
        return [
            pltpu.make_async_copy(down.at[rows], o_down.at[rows], sems.at[0, n]),
            pltpu.make_async_copy(up.at[rows], o_up.at[rows], sems.at[1, n]),
            pltpu.make_async_copy(qkv.at[:, rows], o_qkv.at[:, rows], sems.at[2, n]),
            pltpu.make_async_copy(out.at[n], o_out.at[:, rows], sems.at[3, n]),
        ]

    whole = [
        pltpu.make_async_copy(src, dst, more.at[k])
        for k, (src, dst) in enumerate(
            ((in_grads, o_in), (acts, o_acts), (gains, o_gains), (feats, o_feats))
        )
    ]
    for one in whole:
        one.start()

    def body(n, carry):
        rows = pl.ds(pl.multiple_of(n * 256, 256), 256)
        attn = pl.ds(pl.multiple_of(2 * WIDTH + n * 256, 256), 256)
        first, second, third, fourth = copies(n)
        down[rows, :] = grads[rows, :].astype(F32)
        first.start()
        up[rows, :] = grads[pl.ds(pl.multiple_of(WIDTH + n * 256, 256), 256), :].astype(F32)
        second.start()
        for k in range(3):
            qkv[k, rows, :] = grads[attn, k * 256 : (k + 1) * 256].astype(F32)
        third.start()
        out[n] = grads[attn, 768:].astype(F32)
        fourth.start()
        return carry

    lax.fori_loop(0, 4, body, 0)
    for n in range(4):
        for one in copies(n):
            one.wait()
    for one in whole:
        one.wait()


def widen(grads, acts, in_grads, gains, feats):
    vm = pl.BlockSpec(memory_space=pltpu.VMEM)
    far_off = pl.BlockSpec(memory_space=pl.ANY)

    def like(*shape):
        return jax.ShapeDtypeStruct(shape, F32)

    def wide(*shape):
        return pltpu.VMEM(shape, F32)

    return pl.pallas_call(
        widen_kernel,
        in_specs=[vm] * 5,
        out_specs=[far_off] * 8,
        out_shape=(
            like(WIDTH, WIDTH), like(WIDTH, WIDTH), like(3, WIDTH, LOCAL), like(LOCAL, WIDTH),
            jax.ShapeDtypeStruct((ALL_ROWS, WIDTH), BF16), like(ALL_ROWS, WIDTH),
            like(2, WIDTH), like(HEADS, DIM),
        ),
        scratch_shapes=[
            wide(WIDTH, WIDTH), wide(WIDTH, WIDTH), wide(3, WIDTH, LOCAL), wide(4, LOCAL, LOCAL),
            pltpu.SemaphoreType.DMA((4, 4)), pltpu.SemaphoreType.DMA((4,)),
        ],
        compiler_params=pltpu.CompilerParams(vmem_limit_bytes=40 * 2**20),
        name="widen",
    )(grads, acts, in_grads, gains, feats)


def per_device(
    tokens, lengths, cotangent, qkv_weight, out_weight, up_weight, down_weight, norm_gains,
    feat_weights,
):
    acts, in_grads, grads, gains, feats = layers(
        lengths, tokens, cotangent, jnp.transpose(qkv_weight[0], (1, 0, 2)), out_weight[0],
        up_weight[0], down_weight[0], norm_gains[0], feat_weights[0],
    )
    down, up, qkv, out, acts, in_grads, gains, feats = widen(grads, acts, in_grads, gains, feats)
    qkv = jnp.transpose(qkv, (1, 0, 2))
    return tuple(one[None] for one in (acts, in_grads, qkv, out, up, down, gains, feats))


PLACED = (
    P("dp", None),
    P("dp", None),
    P("dp", None),
    P("section", None, None, "tensor"),
    P("section", "tensor", None),
    P("section", None, "tensor"),
    P("section", "tensor", None),
    P("section", None, None),
    P("section", "tensor", None),
)
GIVEN = (
    P("section", "dp", None),
    P("section", "dp", None),
    P("section", None, None, "tensor"),
    P("section", "tensor", None),
    P("section", None, "tensor"),
    P("section", "tensor", None),
    P("section", None, None),
    P("section", "tensor", None),
)


def solution(mesh):
    return jax.shard_map(
        per_device, mesh=mesh, in_specs=PLACED, out_specs=GIVEN, check_vma=False
    )
```

```python
import functools
import math

import jax
import jax.numpy as jnp
import numpy as np
from jax import lax
from jax.experimental import pallas as pl
from jax.experimental.pallas import tpu as pltpu
from jax.sharding import PartitionSpec as P

F32 = jnp.float32
BF16 = jnp.bfloat16
MESH = pl.DeviceIdType.MESH
EPS = 1e-05
ROWS = 256
HALF = 128
WIDTH = 1024
LOCAL = 256
HEADS = 4
DIM = 64
ROT = 16
MICROS = 2
ALL_ROWS = MICROS * ROWS


def feature_table(head_dim, feat_count):
    golden = 0.6180339887498949
    row_grid = np.arange(feat_count)[:, None] + 0.5
    columns = np.arange(head_dim)[None, :] * 1.0
    points = np.mod(row_grid * (2.0 * columns + 1.0) / feat_count + golden * columns, 1.0)
    radius = np.sqrt(-2.0 * np.log(points[:, 0::2]))
    turning = 2.0 * np.pi * points[:, 1::2]
    omega_rows = np.stack([radius * np.cos(turning), radius * np.sin(turning)], axis=2).reshape(
        feat_count, head_dim
    )
    frequency = np.arange(head_dim)[:, None] * 1.0
    cosine_basis = np.sqrt(2.0 / head_dim) * np.cos(
        np.pi * (2.0 * columns + 1.0) * frequency / (2.0 * head_dim)
    )
    cosine_basis = np.where(frequency == 0, np.sqrt(0.5), 1.0) * cosine_basis
    return np.sum(omega_rows[:, :, None] * cosine_basis[None, :, :], axis=1)


def low_pieces(values):
    high = values.astype(BF16)
    rest = (values - high.astype(values.dtype)).astype(BF16)
    return high, rest


def constants():
    table = feature_table(DIM, DIM).astype(np.float32)
    eye = np.eye(HEADS, dtype=np.float32)
    blocks = np.kron(eye, table.T / math.sqrt(DIM)).astype(np.float32)
    ones = np.kron(eye, np.ones((DIM, DIM), np.float32))
    high, rest = low_pieces(blocks)
    scaled = (ones * (-1.0 / (2.0 * DIM))).astype(BF16)
    forward = np.concatenate([high, high, rest, scaled, scaled], axis=0)
    backward = np.concatenate([blocks.T.astype(BF16), (ones / DIM).astype(BF16)], axis=1)
    half_rot = ROT // 2
    inverse = (10000.0 ** (-2.0 * np.arange(half_rot) / ROT)).astype(np.float32)
    angles = np.arange(ROWS, dtype=np.float32)[:, None] * inverse[None, :]
    cosine = np.ones((ROWS, DIM), np.float32)
    sine = np.zeros((ROWS, DIM), np.float32)
    for start in (0, half_rot):
        cosine[:, start : start + half_rot] = np.cos(angles.astype(np.float64))
        sine[:, start : start + half_rot] = np.sin(angles.astype(np.float64))
    cosine = np.tile(cosine, (1, HEADS))
    sine = np.tile(sine, (1, HEADS))
    turns = np.concatenate([*low_pieces(cosine), *low_pieces(sine)], axis=1)
    spread = np.tile(np.eye(DIM, dtype=np.float32), (1, HEADS))
    return np.concatenate(
        [
            *np.split(turns, 4, axis=1), forward, *np.split(backward, 2, axis=1), ones.astype(BF16),
            spread.astype(BF16),
        ],
        axis=0,
    )


def dot_nn(a, b):
    return lax.dot_general(a, b, (((1,), (0,)), ((), ())), preferred_element_type=F32)


def dot_nt(a, b):
    return lax.dot_general(a, b, (((1,), (1,)), ((), ())), preferred_element_type=F32)


def dot_exact(a, b, side):
    return lax.dot_general(
        a, b, (((1,), (side,)), ((), ())), preferred_element_type=F32,
        precision=lax.Precision.HIGHEST,
    )


def dot_tn(a, b):
    return lax.dot_general(a, b, (((0,), (0,)), ((), ())), preferred_element_type=F32)


def normal_cdf(v):
    bell = jnp.exp(-0.5 * v * v)
    t = pl.reciprocal(1.0 + (0.3275911 * math.sqrt(0.5)) * jnp.abs(v))
    poly = 0.5 * 1.061405429 * t - 0.5 * 1.453152027
    for coefficient in (1.421413741, -0.284496736, 0.254829592):
        poly = poly * t + 0.5 * coefficient
    tail = poly * t * bell
    cdf = jnp.where(v >= 0.0, 1.0 - tail, tail)
    return cdf, cdf + v * bell * (1.0 / math.sqrt(2.0 * math.pi))


def ln_rows(x):
    mean = jnp.mean(x, axis=-1, keepdims=True)
    centered = x - mean
    inv = lax.rsqrt(jnp.mean(centered * centered, axis=-1, keepdims=True) + EPS)
    return centered * inv, inv


def ln_back(combined, normed, inv):
    mean_c = jnp.mean(combined, axis=-1, keepdims=True)
    mean_p = jnp.mean(combined * normed, axis=-1, keepdims=True)
    return inv * (combined - mean_c - normed * mean_p)


DOWN, UP, ATTN, OUT = range(4)
ORDER = (
    (DOWN, 2), (ATTN, 1), (UP, 2), (OUT, 0), (DOWN, 3), (ATTN, 2),
    (OUT, 1), (UP, 3), (OUT, 2), (ATTN, 3), (OUT, 3), (DOWN, 4),
    (OUT, 4), (UP, 4), (OUT, 5), (ATTN, 4), (OUT, 6), (DOWN, 5),
    (UP, 5), (ATTN, 5), (DOWN, 6), (UP, 6), (ATTN, 6),
)


def wrap(v):
    return lax.rem(v + 8, 4)


class Sums:
    LAST = 6

    def __init__(self, own, g, row0, near, far, sent, got, place, at):
        self.own, self.g, self.row0, self.at = own, g, row0, at
        self.near, self.far, self.sent, self.got, self.place = near, far, sent, got, place

    def ends(self, q):
        axis1, axis2 = ("x", "y") if q == 0 else ("y", "x")
        return axis1, axis2, self.place[axis1], self.place[axis2]

    def half(self, q, b, h):
        return pl.ds(pl.multiple_of(self.row0 + q * 512 + b * 128 + h * 64, 64), 64)

    def piece(self, q, k):
        _, _, p1, _ = self.ends(q)
        return pl.ds(pl.multiple_of(self.row0 + q * 512 + p1 * 128 + k * 32, 32), 32)

    def near_piece(self, q, k):
        return (q, 2 + k // 2, pl.ds(pl.multiple_of(lax.rem(k, 2) * 32, 32), 32))

    def copies(self, q, t):
        axis1, axis2, p1, p2 = self.ends(q)
        near, own, g = self.near, self.own, self.g
        up, down = (axis1, 1), (axis1, 3)
        if t == 0:
            plan = [
                (own.at[self.half(q, wrap(p1 + 2), 0)], near.at[q, 0], up, 0),
                (own.at[self.half(q, wrap(p1 + 2), 1)], near.at[q, 1], down, 0),
                (own.at[self.half(q, wrap(p1 + 1), 1)], near.at[q, 3], up, 1),
                (own.at[self.half(q, wrap(p1 - 1), 0)], near.at[q, 2], down, 1),
            ]
        elif t == 1:
            plan = [(near.at[q, 0], near.at[q, 4], up, 2), (near.at[q, 1], near.at[q, 5], down, 2)]
        elif t == 2:
            plan = [
                (near.at[self.near_piece(q, wrap(p2 + k + 1))], self.far.at[q, k], (axis2, k + 1), 3)
                for k in range(3)
            ]
        elif t == 3:
            src = g.at[self.piece(q, p2)]
            plan = [(src, src, (axis2, k + 1), 4) for k in range(3)]
        elif t == 4:
            first, second = g.at[self.half(q, p1, 0)], g.at[self.half(q, p1, 1)]
            plan = [
                (first, first, up, 5), (second, second, down, 5),
                (second, second, up, 6), (first, first, down, 6),
            ]
        else:
            first = g.at[self.half(q, wrap(p1 - 1), 0)]
            second = g.at[self.half(q, wrap(p1 + 1), 1)]
            plan = [(first, first, up, 7), (second, second, down, 7)]
        return [
            pltpu.make_async_remote_copy(
                src_ref=src, dst_ref=dst, send_sem=self.sent, recv_sem=self.got.at[k],
                device_id=self.at(*target), device_id_type=MESH,
            )
            for src, dst, target, k in plan
        ]

    def wait(self, k):
        if k < 3:
            all_of = self.near.at[:, 2 * k : 2 * k + 2]
        elif k == 3:
            all_of = self.far
        else:
            all_of = self.g.at[self.row0 : self.row0 + (192 if k == 4 else 256)]
        pltpu.make_async_copy(all_of, all_of, self.got.at[k]).wait()

    def start(self, q, t):
        _, _, p1, p2 = self.ends(q)
        near, own = self.near, self.own
        if t == 1:
            near[q, 0] = near[q, 0] + own[self.half(q, wrap(p1 + 1), 0), :]
            near[q, 1] = near[q, 1] + own[self.half(q, wrap(p1 - 1), 1), :]
        elif t == 2:
            for h in range(2):
                total = near[q, 2 + h].astype(F32) + near[q, 4 + h].astype(F32)
                near[q, 2 + h] = (total + own[self.half(q, p1, h), :].astype(F32)).astype(BF16)
        elif t == 3:
            total = near[self.near_piece(q, p2)].astype(F32) + self.far[q, 0].astype(F32)
            total = total + (self.far[q, 1].astype(F32) + self.far[q, 2].astype(F32))
            self.g[self.piece(q, p2), :] = total.astype(BF16)
        for one in self.copies(q, t):
            one.start()

    def step(self, t):
        for k in ((), (0,), (1, 2), (3,), (4,), (5,), (6, 7))[t]:
            self.wait(k)
        if t < self.LAST:
            for q in range(2):
                self.start(q, t)

    def finish(self, ref):
        rows = 2 * (12 * 64 + 6 * 32) * self.own.shape[1] // WIDTH
        pltpu.make_async_copy(ref.at[0:rows], ref.at[0:rows], self.sent).wait()


def layers_kernel(
    lens_h, tok_h, cot_h, wqkv_h, wout_h, wup_h, wdown_h, gains_h, feats_h, cst_h,
    acts, in_grads, gsum, csum, esum, gain_out, feat_out,
    lens, xin, glow, aux, wqkv, wout, wup, wdown, gains, feats, cst, gbuf, cbuf, ebuf, near, near_c, near_e, far, far_c, far_e,
    fw, mask, rot, nrm, attn_in, mlp_in, tq, tk, pq, pk, qf, kf, vf, sb, den, att,
    mixed, hidden, ghp, gm, gproj, gpre, nx, inv_x,
    fpart, frx, fcs, fin, bpart, brx, bcs, bin_, xrx, small, srx, sall,
    load_s, frx_s, fin_s, facts_s, brx_s, bin_s, bout_s, x_s, xsib_s, ret_s, small_s,
    sent_s, got_s, all_s, give_s, give_back_s,
):
    s = lax.axis_index("section")
    t = lax.axis_index("tensor")
    dp = lax.axis_index("dp")
    zh = t // 2
    c = lax.rem(t, 2)
    sibling = {"tensor": zh * 2 + 1 - c}
    partner = {"tensor": lax.rem(t + 2, 4)}
    across = [{"section": 1 - s, "tensor": z * 2 + c} for z in range(2)]
    place = {"x": dp // 4, "y": lax.rem(dp, 4)}

    def at(axis, d):
        there = dict(place)
        there[axis] = lax.rem(place[axis] + d + 4, 4)
        return {"dp": there["x"] * 4 + there["y"]}

    def load(src, dst, k):
        return pltpu.make_async_copy(src, dst, load_s.at[k])

    first, second = slice(0, ROWS), slice(ROWS, ALL_ROWS)
    load_lens = load(lens_h, lens, 12)
    load_gains = load(gains_h, gains, 0)
    load_feats = load(feats_h, feats, 1)
    load_cst = load(cst_h, cst, 2)
    load_qkv = [load(wqkv_h.at[k], wqkv.at[k], 3 + k) for k in range(3)]
    load_up = load(wup_h, wup, 6)
    load_out = load(wout_h, wout, 7)
    load_down = load(wdown_h, wdown, 8)

    @pl.when(s == 0)
    def _():
        load(tok_h.at[first], xin.at[first], 9).start()
        for one in (load_gains, load_lens, load_feats, load_cst, *load_qkv):
            one.start()

    @pl.when(s == 1)
    def _():
        load(cot_h, glow, 9).start()
        for one in (load_down, load_out, load_lens, load_cst, load_gains, load_feats, *load_qkv, load_up):
            one.start()
        load(tok_h, aux, 11).start()

    barrier = pltpu.get_barrier_semaphore()
    peers = [sibling, partner, *across] + [at(axis, d) for axis in ("x", "y") for d in (1, 2, 3)]
    for target in peers:
        pl.semaphore_signal(barrier, inc=1, device_id=target, device_id_type=MESH)

    def remote(src, dst, sems, index, target):
        return pltpu.make_async_remote_copy(
            src_ref=src, dst_ref=dst, send_sem=sems.at[(0, *index)],
            recv_sem=sems.at[(1, *index)], device_id=target, device_id_type=MESH,
        )

    def micro_rows(m):
        if isinstance(m, int):
            return slice(m * ROWS, (m + 1) * ROWS)
        return pl.ds(pl.multiple_of(m * ROWS, ROWS), ROWS)

    def half_rows(m):
        return pl.ds(pl.multiple_of(m * ROWS + c * HALF, HALF), HALF)

    def part_rows(m, core, k):
        return pl.ds(pl.multiple_of(m * ROWS + core * HALF + k * 64, 64), 64)

    keep_rows = pl.ds(pl.multiple_of(c * HALF, HALF), HALF)
    give_rows = pl.ds(pl.multiple_of((1 - c) * HALF, HALF), HALF)

    def cols(n):
        return slice(n * 256, (n + 1) * 256)

    def f_swap(m):
        return remote(fpart.at[m, give_rows], frx.at[m], frx_s, (m,), sibling)

    def f_spread(m):
        return remote(fcs.at[m], fin.at[m], fin_s, (m,), partner)

    def f_share(m):
        return remote(acts.at[half_rows(m)], acts.at[half_rows(m)], facts_s, (m,), sibling)

    def b_swap(m):
        return remote(bpart.at[m, give_rows], brx.at[m], brx_s, (m,), sibling)

    def b_spread(m):
        return remote(bcs.at[m], bin_.at[m], bin_s, (m,), partner)

    def b_share(m):
        return remote(in_grads.at[half_rows(m)], in_grads.at[half_rows(m)], bout_s, (m,), sibling)

    def cross(src, m, z, k, arrival=False):
        here = z if arrival else zh
        rows = slice(k * 64, (k + 1) * 64)
        return pltpu.make_async_remote_copy(
            src_ref=src.at[m, rows], dst_ref=xrx.at[m, here, rows], send_sem=x_s.at[0, m, z, k],
            recv_sem=x_s.at[1, m, here, k], device_id=across[z], device_id_type=MESH,
        )

    def send_back(m, z, arrival=False):
        rows = part_rows(m, c, z if arrival else zh)
        return pltpu.make_async_remote_copy(
            src_ref=xin.at[rows], dst_ref=acts.at[rows], send_sem=ret_s.at[0, m, z],
            recv_sem=ret_s.at[1, m, z if arrival else zh], device_id=across[z], device_id_type=MESH,
        )

    def x_share(buf, m, k):
        rows = part_rows(m, c, k)
        return remote(buf.at[rows], buf.at[rows], xsib_s, (m, k), sibling)

    def chip_sum(part, rx, cs, m):
        cs[m] = (part[m, keep_rows].astype(F32) + rx[m].astype(F32)).astype(BF16)

    def send_across(cs, m):
        for k in range(2):
            for z in range(2):
                cross(cs, m, z, k).start()

    def arrived(src, m, k):
        for z in range(2):
            cross(src, m, z, k, arrival=True).wait_recv()
        rows = slice(k * 64, (k + 1) * 64)
        return xrx[m, 0, rows].astype(F32) + xrx[m, 1, rows].astype(F32)

    def context(m):
        length = lens[pl.ds(m, 1), :]
        first_end = length[:, 0:1]
        second_end = first_end + length[:, 1:2]
        third_end = second_end + length[:, 2:3]
        i = lax.broadcasted_iota(jnp.int32, (ROWS, ROWS), 0)
        j = lax.broadcasted_iota(jnp.int32, (ROWS, ROWS), 1)
        start = jnp.where(i >= first_end, first_end, 0)
        start = jnp.where(i >= second_end, second_end, start)
        start = jnp.where(i >= third_end, third_end, start)
        mask[m] = ((j <= i) & (j >= start)).astype(F32)
        hot = ((i - start) == j).astype(F32).astype(BF16)
        cosine = dot_nn(hot, cst[0:256, :]) + dot_nn(hot, cst[256:512, :])
        sine = dot_nn(hot, cst[512:768, :]) + dot_nn(hot, cst[768:1024, :])
        column = lax.rem(j, DIM)
        rot[m, 0] = cosine
        rot[m, 1] = jnp.where(column < ROT // 2, -sine, 0.0)
        rot[m, 2] = jnp.where(column >= ROT // 2, sine, 0.0)

    def norm_rows(rows):
        normed, _ = ln_rows(xin[rows, :].astype(F32))
        nrm[rows, :] = normed
        attn_in[rows, :] = (normed * gains[0:1, :]).astype(BF16)
        mlp_in[rows, :] = (normed * gains[1:2, :]).astype(BF16)

    def features(projected, m, turned_ref, phi_ref, low_ref):
        turned = (
            projected * rot[m, 0]
            + pltpu.roll(projected, LOCAL - ROT // 2, 1) * rot[m, 1]
            + pltpu.roll(projected, ROT // 2, 1) * rot[m, 2]
        )
        turned_ref[m] = turned
        high, rest = low_pieces(turned)
        square_high, square_rest = low_pieces(turned * turned)
        pieces = jnp.concatenate([high, rest, high, square_high, square_rest], axis=1)
        phi = fw[...] * jnp.exp(dot_nn(pieces, cst[1024:2304, :]))
        phi_ref[m] = phi
        low_ref[m] = phi.astype(BF16)

    def head_row(h):
        return cst[2816 + h * DIM : 2817 + h * DIM, :]

    def attend(m, up):
        queries, keys, values = qf[m], kf[m], vf[m]
        kept = mask[m] > 0.5
        total = jnp.zeros((ROWS, 2 * LOCAL), F32)
        for h in range(HEADS):
            row = head_row(h)
            scores = jnp.where(kept, dot_nt(queries * row, keys), 0.0).astype(BF16)
            sb[m, h] = scores
            right = jnp.concatenate(
                [values * row, jnp.broadcast_to(row, (ROWS, LOCAL))], axis=1
            )
            total = total + dot_nn(scores, right)
            if h % 2 == 0:
                up(2 + h // 2)
        norm = total[:, LOCAL:]
        attended = total[:, :LOCAL] / norm
        den[m] = norm
        att[m] = attended
        mixed[micro_rows(m), :] = attended.astype(BF16)

    def front(m):
        rows = micro_rows(m)
        normed_low = attn_in[rows, :]

        def up(n):
            pre = dot_nn(mlp_in[rows, :], wup[:, cols(n)])
            cdf, slope = normal_cdf(pre)
            hidden[rows, cols(n)] = (pre * cdf).astype(BF16)
            gpre[rows, cols(n)] = (ghp[rows, cols(n)] * slope).astype(BF16)
            ghp[rows, cols(n)] = slope

        queries = dot_nn(normed_low, wqkv[0])
        keys = dot_nn(normed_low, wqkv[1])
        up(0)
        features(queries, m, tq, pq, qf)
        up(1)
        features(keys, m, tk, pk, kf)
        vf[m] = dot_nn(normed_low, wqkv[2]).astype(BF16)
        attend(m, up)

    def back_out(m):
        rows = micro_rows(m)
        for n in range(4):
            tile = dot_nn(mixed[rows, :], wout[:, cols(n)])
            tile = tile + dot_nn(hidden[rows, :], wdown[:, cols(n)])
            fpart[m, :, cols(n)] = tile.astype(BF16)

    def grad_hidden(m, known):
        rows = micro_rows(m)
        for n in range(4):
            grad = dot_nt(glow[rows, :], wdown[cols(n), :])
            if known:
                gpre[rows, cols(n)] = (grad * ghp[rows, cols(n)]).astype(BF16)
            else:
                ghp[rows, cols(n)] = grad

    def grad_mixed(m):
        rows = micro_rows(m)
        gm[rows, :] = dot_nt(glow[rows, :], wout[...]).astype(BF16)

    def feature_back(grad_phi, m, turned_ref, phi_ref):
        grad_s = grad_phi * phi_ref[m]
        small[0, 2:3, 0:LOCAL] = small[0, 2:3, 0:LOCAL] + jnp.sum(grad_s, axis=0, keepdims=True)
        low = grad_s.astype(BF16)
        grad = dot_nn(low, cst[2304:2560, :]) - turned_ref[m] * dot_nn(low, cst[2560:2816, :])
        return (
            grad * rot[m, 0]
            - pltpu.roll(grad, LOCAL - ROT // 2, 1) * rot[m, 1]
            - pltpu.roll(grad, ROT // 2, 1) * rot[m, 2]
        )

    def attend_back(m):
        rows = micro_rows(m)
        grad_num = gm[rows, :].astype(F32) / den[m]
        grad_low = grad_num.astype(BF16)
        high, rest = low_pieces(grad_low.astype(F32) * att[m])
        ones = cst[2816:3072, :]
        grad_den = -(dot_nn(high, ones) + dot_nn(rest, ones))
        kept = mask[m] > 0.5
        queries, keys, values = qf[m], kf[m], vf[m]
        grad_q = jnp.zeros((ROWS, LOCAL), F32)
        grad_k = jnp.zeros((ROWS, LOCAL), F32)
        grad_v = jnp.zeros((ROWS, LOCAL), F32)
        for h in range(HEADS):
            row = head_row(h)
            given = grad_low * row
            grad_scores = dot_nt(given, values) + grad_den[:, h * DIM : h * DIM + 1]
            grad_scores = jnp.where(kept, grad_scores, 0.0).astype(BF16)
            grad_q = grad_q + dot_nn(grad_scores, keys * row)
            grad_k = grad_k + dot_tn(grad_scores, queries * row)
            grad_v = grad_v + dot_tn(sb[m, h], given)
            here = cols(h)
            grad_m = dot_nt(gpre[rows, :], wup[here, :])
            ghp[rows, here] = gains[1:2, here] * grad_m
            line = jnp.sum(nrm[rows, here] * grad_m, axis=0, keepdims=True)
            small[0, 1:2, here] = small[0, 1:2, here] + line
        gproj[0, rows, :] = feature_back(grad_q, m, tq, pq).astype(BF16)
        gproj[1, rows, :] = feature_back(grad_k, m, tk, pk).astype(BF16)
        gproj[2, rows, :] = grad_v.astype(BF16)

    def back_in(m):
        rows = micro_rows(m)
        for n in range(4):
            here = cols(n)
            grad_a = dot_nt(gproj[0, rows, :], wqkv[0, here, :])
            grad_a = grad_a + dot_nt(gproj[1, rows, :], wqkv[1, here, :])
            grad_a = grad_a + dot_nt(gproj[2, rows, :], wqkv[2, here, :])
            bpart[m, :, here] = (gains[0:1, here] * grad_a + ghp[rows, here]).astype(BF16)
            line = jnp.sum(nrm[rows, here] * grad_a, axis=0, keepdims=True)
            small[0, 0:1, here] = small[0, 0:1, here] + line

    def grads_down(n):
        gbuf[cols(n), :] = dot_tn(hidden[:, cols(n)], glow[...]).astype(BF16)
        if n % 2 == 1:
            sums[DOWN].start(n // 2, 0)

    def grads_up(n):
        rows = slice(1024 + n * 256, 1280 + n * 256)
        gbuf[rows, :] = dot_tn(mlp_in[:, cols(n)], gpre[...]).astype(BF16)
        if n % 2 == 1:
            sums[UP].start(n // 2, 0)

    def grads_attn(n):
        for k in range(3):
            cbuf[cols(n), cols(k)] = dot_tn(attn_in[:, cols(n)], gproj[k]).astype(BF16)
        if n % 2 == 1:
            sums[ATTN].start(n // 2, 0)

    def grads_out():
        for z in range(2):
            part = dot_tn(mixed[...], glow[:, z * 512 : (z + 1) * 512])
            ebuf[512 + z * 256 : 768 + z * 256, :] = part.astype(BF16)

    def finish_forward(m):
        f_spread(m).wait_recv()
        total = fcs[m].astype(F32) + fin[m].astype(F32)
        acts[half_rows(m), :] = (xin[half_rows(m), :].astype(F32) + total).astype(BF16)
        f_share(m).start()

    def finish_backward(m):
        b_spread(m).wait_recv()
        total = bcs[m].astype(F32) + bin_[m].astype(F32)
        normed, inv = ln_rows(xin[half_rows(m), :].astype(F32))
        in_grads[half_rows(m), :] = glow[half_rows(m), :].astype(F32) + ln_back(total, normed, inv)
        b_share(m).start()

    sums = [
        Sums(own, total, row0, *scratch, sent_s.at[j], got_s.at[j], place, at)
        for j, (own, total, row0, scratch) in enumerate(
            (
                (gbuf, gsum, 0, (near.at[0], far.at[0])),
                (gbuf, gsum, 1024, (near.at[1], far.at[1])),
                (cbuf, csum, 0, (near_c, far_c)),
                (ebuf, esum, 0, (near_e, far_e)),
            )
        )
    ]

    def give(z, arrival=False):
        place_there = z if arrival else zh
        return pltpu.make_async_remote_copy(
            src_ref=ebuf.at[512 + z * 256 : 768 + z * 256],
            dst_ref=ebuf.at[pl.ds(pl.multiple_of(place_there * 256, 256), 256)],
            send_sem=give_s.at[0, z], recv_sem=give_s.at[1, place_there],
            device_id=across[z], device_id_type=MESH,
        )

    def give_back(z, arrival=False):
        place_there = z if arrival else zh
        return pltpu.make_async_remote_copy(
            src_ref=esum.at[z * 256 : (z + 1) * 256],
            dst_ref=esum.at[pl.ds(pl.multiple_of(512 + place_there * 256, 256), 256)],
            send_sem=give_back_s.at[0, z], recv_sem=give_back_s.at[1, place_there],
            device_id=across[z], device_id_type=MESH,
        )

    def hop(j, step):
        sums[j].step(step)

    def small_step(k):
        def copy(k):
            if k < 2:
                return [remote(small.at[k], srx.at[k], small_s, (k,), (sibling, partner)[k])]
            axis = "xy"[k - 2]
            return [
                pltpu.make_async_remote_copy(
                    src_ref=small.at[k], dst_ref=sall.at[k - 2, place[axis]],
                    send_sem=all_s.at[0, k - 2], recv_sem=all_s.at[1, k - 2],
                    device_id=at(axis, d), device_id_type=MESH,
                )
                for d in (1, 2, 3)
            ]

        if k == -1:
            for j in range(2):
                copy(j)[0].wait_send()
                three = sall.at[j, 0:3]
                pltpu.make_async_copy(three, three, all_s.at[0, j]).wait()
            return
        if k in (1, 2):
            copy(k - 1)[0].wait_recv()
        if k > 2:
            three = sall.at[k - 3, 0:3]
            pltpu.make_async_copy(three, three, all_s.at[1, k - 3]).wait()
        if k in (1, 2):
            line = lax.broadcasted_iota(jnp.int32, (8, WIDTH), 0)
            small[k] = small[k - 1] + jnp.where(line < 2, srx[k - 1], 0.0)
        if k in (3, 4):
            parts = sall[k - 3]
            small[k] = (parts[0] + parts[1]) + (parts[2] + parts[3])
        if k in (2, 3):
            sall[k - 2, place["xy"[k - 2]]] = small[k]
        if k < 4:
            for one in copy(k):
                one.start()

    def spread_feats():
        exact = dot_exact(feats[...], cst[3072:3136, :].astype(F32), 0)
        fw[...] = jnp.sum(exact * heads_of(), axis=0, keepdims=True)

    def heads_of():
        return jnp.concatenate([head_row(h) for h in range(HEADS)], axis=0).astype(F32)

    def wait_all(*copies):
        for one in copies:
            one.wait()

    small[...] = jnp.zeros(small.shape, F32)

    @pl.when(s == 0)
    def _():
        def forward(m, carry):
            @pl.when(m == 0)
            def _():
                wait_all(load(tok_h.at[first], xin.at[first], 9), load_gains)
                for one in (load_up, load_out, load_down, load(tok_h.at[second], xin.at[second], 10)):
                    one.start()
                load(cot_h, aux, 11).start()

            for k in range(4):
                norm_rows(pl.ds(pl.multiple_of(m * ROWS + k * 64, 64), 64))

            @pl.when(m == 0)
            def _():
                wait_all(load_lens, load_feats, load_cst)
                spread_feats()

            context(m)

            @pl.when(m == 0)
            def _():
                wait_all(*load_qkv, load_up)

            front(m)

            @pl.when(m == 0)
            def _():
                wait_all(load_out, load_down)

            back_out(m)

            @pl.when(m == 0)
            def _():
                pl.semaphore_wait(barrier, len(peers))

            f_swap(m).start()

            @pl.when(m == 0)
            def _():
                wait_all(load(tok_h.at[second], xin.at[second], 10), load(cot_h, aux, 11))

            f_swap(m).wait_recv()
            chip_sum(fpart, frx, fcs, m)
            send_across(fcs, m)
            return carry

        lax.fori_loop(0, MICROS, forward, 0)

        def gradient_in(m):
            for z in range(2):
                send_back(m, z, arrival=True).wait_recv()
            normed, inv = ln_rows(acts[half_rows(m), :].astype(F32))
            nx[m] = normed
            inv_x[m] = jnp.broadcast_to(inv, (HALF, 128))
            f_share(m).start()
            for k in range(2):
                total = arrived(bcs, m, k)
                rows = slice(k * 64, (k + 1) * 64)
                back = ln_back(total, nx[m, rows], inv_x[m, rows, 0:1])
                grad = aux[part_rows(m, c, k), :].astype(F32) + back
                glow[part_rows(m, c, k), :] = grad.astype(BF16)
                x_share(glow, m, k).start()
            for k in range(2):
                x_share(glow, m, k).wait_recv()

        def backward(m, carry):
            last = m == MICROS - 1
            gradient_in(m)

            @pl.when(last)
            def _():
                for n in range(4):
                    grads_down(n)
                grads_out()
                for z in range(2):
                    give(z).start()

            grad_hidden(m, True)

            @pl.when(last)
            def _():
                for n in range(4):
                    grads_up(n)

            grad_mixed(m)
            attend_back(m)

            @pl.when(last)
            def _():
                hop(0, 1)
                for n in range(4):
                    grads_attn(n)

            back_in(m)
            b_swap(m).start()
            return carry

        lax.fori_loop(0, MICROS, backward, 0)
        hop(1, 1)
        for m in range(MICROS):
            for k in range(2):
                x_share(glow, m, k).wait_send()
                for z in range(2):
                    cross(fcs, m, z, k).wait_send()

    @pl.when(s == 1)
    def _():
        wait_all(load(cot_h, glow, 9), load_down)
        for m in range(MICROS):
            grad_hidden(m, False)
        wait_all(load_out, load_lens, load_cst, load_gains, load_feats)
        spread_feats()
        for m in range(MICROS):
            grad_mixed(m)
            context(m)
        wait_all(*load_qkv, load_up, load(tok_h, aux, 11))
        pl.semaphore_wait(barrier, len(peers))

        def cross_over(m):
            b_swap(m).wait_recv()
            chip_sum(bpart, brx, bcs, m)
            send_across(bcs, m)

        def take_in(m, k):
            total = arrived(fcs, m, k)
            own = part_rows(m, c, k)
            xin[own, :] = (aux[own, :].astype(F32) + total).astype(BF16)
            x_share(xin, m, k).start()

        def both(m, carry):
            @pl.when(m == 0)
            def _():
                for k in range(2):
                    take_in(0, k)
                    norm_rows(part_rows(0, c, k))
                for z in range(2):
                    send_back(0, z).start()

            @pl.when(m == 1)
            def _():
                for k in range(2):
                    norm_rows(part_rows(1, c, k))

            for k in range(2):
                x_share(xin, m, k).wait_recv()
                norm_rows(part_rows(m, 1 - c, k))

            @pl.when(m == 1)
            def _():
                cross_over(0)

            front(m)
            attend_back(m)

            @pl.when(m == 0)
            def _():
                for k in range(2):
                    take_in(1, k)
                for z in range(2):
                    send_back(1, z).start()

            back_in(m)
            b_swap(m).start()
            return carry

        lax.fori_loop(0, MICROS, both, 0)
        grads_down(0)
        grads_down(1)
        cross_over(1)
        grads_down(2)
        grads_down(3)
        for n in range(4):
            grads_up(n)
        hop(0, 1)
        for n in range(4):
            grads_attn(n)
        grads_out()
        for m in range(MICROS):
            back_out(m)
            f_swap(m).start()
        hop(1, 1)
        for m in range(MICROS):
            for z in range(2):
                for k in range(2):
                    cross(bcs, m, z, k).wait_send()
        for m in range(MICROS):
            for k in range(2):
                x_share(xin, m, k).wait_send()
                send_back(m, k).wait_send()

    small_step(0)
    for part, step in ORDER:
        if part == OUT:

            @pl.when(s == 1)
            def _():
                if step == 0:
                    for z in range(2):
                        give(z, arrival=True).wait_recv()
                    for q in range(2):
                        sums[OUT].start(q, 0)
                else:
                    hop(OUT, step)
                if step == Sums.LAST:
                    for z in range(2):
                        give_back(z).start()

            continue
        if (part, step) == (DOWN, 3):

            @pl.when(s == 0)
            def _():
                for m in range(MICROS):
                    b_swap(m).wait_recv()
                    chip_sum(bpart, brx, bcs, m)

            @pl.when(s == 1)
            def _():
                for m in range(MICROS):
                    f_swap(m).wait_recv()
                    chip_sum(fpart, frx, fcs, m)
                    f_spread(m).start()

            for m in range(MICROS):
                b_spread(m).start()

        if part == DOWN and 2 < step < 6:
            small_step(step - 2)
        hop(part, step)
        if part != ATTN:
            continue
        if step == 4:
            for m in range(MICROS):
                finish_backward(m)

            @pl.when(s == 1)
            def _():
                for m in range(MICROS):
                    finish_forward(m)
                    f_spread(m).wait_send()

        if step == 5:
            small_step(4)
            gain_out[...] = small[4, 0:2, :]
            line = jnp.broadcast_to(small[4, 2:3, 0:LOCAL] / fw[...], (HEADS, LOCAL))
            feat_out[...] = dot_exact(line * heads_of(), cst[3072:3136, :].astype(F32), 1)
            small_step(-1)
            for m in range(MICROS):
                f_share(m).wait_recv()
                b_share(m).wait_recv()
                for one in (f_swap(m), f_share(m), b_swap(m), b_spread(m), b_share(m)):
                    one.wait_send()
    for one in sums[:OUT]:
        one.finish(gbuf)

    @pl.when(s == 0)
    def _():
        for z in range(2):
            give(z).wait_send()
            give_back(z, arrival=True).wait_recv()

    @pl.when(s == 1)
    def _():
        sums[OUT].finish(gbuf)
        for z in range(2):
            give_back(z).wait_send()


def layers(lengths, tok, cot, wqkv, wout, wup, wdown, gains, feats):
    vm = pl.BlockSpec(memory_space=pltpu.VMEM)
    far_off = pl.BlockSpec(memory_space=pl.ANY)

    def low(*shape):
        return pltpu.VMEM(shape, BF16)

    def wide(*shape):
        return pltpu.VMEM(shape, F32)

    full = (MICROS, ROWS, WIDTH)
    half = (MICROS, HALF, WIDTH)
    square = (MICROS, ROWS, LOCAL)
    rows = (ALL_ROWS, WIDTH)
    sems = pltpu.SemaphoreType.DMA
    return pl.pallas_call(
        layers_kernel,
        out_shape=(
            low(*rows), wide(*rows), low(2 * WIDTH, WIDTH), low(WIDTH, 768), low(WIDTH, 512),
            wide(2, WIDTH), wide(HEADS, DIM),
        ),
        in_specs=[far_off] * 10,
        out_specs=(vm,) * 7,
        scratch_shapes=[
            pltpu.VMEM((MICROS, 4), jnp.int32), low(*rows), low(*rows), low(*rows),
            low(3, WIDTH, LOCAL), low(LOCAL, WIDTH), low(WIDTH, WIDTH), low(WIDTH, WIDTH),
            wide(2, WIDTH), wide(HEADS, DIM), low(3136, LOCAL),
            low(2 * WIDTH, WIDTH), low(WIDTH, 768), low(WIDTH, 512),
            low(2, 2, 6, 64, WIDTH), low(2, 6, 64, 768), low(2, 6, 64, 512),
            low(2, 2, 3, 32, WIDTH), low(2, 3, 32, 768), low(2, 3, 32, 512),
            wide(1, LOCAL), wide(*square), wide(MICROS, 3, ROWS, LOCAL),
            wide(*rows), low(*rows), low(*rows),
            wide(*square), wide(*square), wide(*square), wide(*square),
            low(*square), low(*square), low(*square),
            low(MICROS, HEADS, ROWS, ROWS), wide(*square), wide(*square),
            low(ALL_ROWS, LOCAL), low(*rows), wide(*rows), low(ALL_ROWS, LOCAL),
            low(3, ALL_ROWS, LOCAL), low(*rows), wide(*half), wide(MICROS, HALF, 128),
            low(*full), low(*half), low(*half), low(*half),
            low(*full), low(*half), low(*half), low(*half),
            low(MICROS, 2, HALF, WIDTH), wide(5, 8, WIDTH), wide(2, 8, WIDTH), wide(2, 4, 8, WIDTH),
            sems((13,)),
            sems((2, MICROS)), sems((2, MICROS)), sems((2, MICROS)),
            sems((2, MICROS)), sems((2, MICROS)), sems((2, MICROS)),
            sems((2, MICROS, 2, 2)), sems((2, MICROS, 2)), sems((2, MICROS, 2)), sems((2, 2)),
            sems((4,)), sems((4, 8)), sems((2, 2)), sems((2, 2)), sems((2, 2)),
        ],
        compiler_params=pltpu.CompilerParams(
            collective_id=0, has_side_effects=True, vmem_limit_bytes=53 * 2**20
        ),
        name="layers",
    )(lengths, tok, cot, wqkv, wout, wup, wdown, gains, feats, jnp.asarray(constants()))


def widen_kernel(
    grads, attn, out_part, acts, in_grads, gains, feats, o_down, o_up, o_qkv, o_out, o_acts, o_in, o_gains, o_feats,
    down, up, qkv, out, sems, more,
):
    def copies(n):
        rows = pl.ds(pl.multiple_of(n * 256, 256), 256)
        tall = pl.ds(pl.multiple_of(lax.rem(n, 2) * 128, 128), 128)
        broad = pl.ds(pl.multiple_of(n // 2 * 512, 512), 512)
        return [
            pltpu.make_async_copy(down.at[rows], o_down.at[rows], sems.at[0, n]),
            pltpu.make_async_copy(up.at[rows], o_up.at[rows], sems.at[1, n]),
            pltpu.make_async_copy(qkv.at[:, rows], o_qkv.at[:, rows], sems.at[2, n]),
            pltpu.make_async_copy(out.at[n], o_out.at[tall, broad], sems.at[3, n]),
        ]

    whole = [
        pltpu.make_async_copy(src, dst, more.at[k])
        for k, (src, dst) in enumerate(
            ((in_grads, o_in), (acts, o_acts), (gains, o_gains), (feats, o_feats))
        )
    ]
    for one in whole:
        one.start()

    def body(n, carry):
        rows = pl.ds(pl.multiple_of(n * 256, 256), 256)
        first, second, third, fourth = copies(n)
        down[rows, :] = grads[rows, :].astype(F32)
        first.start()
        up[rows, :] = grads[pl.ds(pl.multiple_of(WIDTH + n * 256, 256), 256), :].astype(F32)
        second.start()
        for k in range(3):
            qkv[k, rows, :] = attn[rows, k * 256 : (k + 1) * 256].astype(F32)
        third.start()
        out[n] = out_part[pl.ds(pl.multiple_of(512 + n * 128, 128), 128), :].astype(F32)
        fourth.start()
        return carry

    lax.fori_loop(0, 4, body, 0)
    for n in range(4):
        for one in copies(n):
            one.wait()
    for one in whole:
        one.wait()


def widen(grads, attn, out_part, acts, in_grads, gains, feats):
    vm = pl.BlockSpec(memory_space=pltpu.VMEM)
    far_off = pl.BlockSpec(memory_space=pl.ANY)

    def like(*shape):
        return jax.ShapeDtypeStruct(shape, F32)

    def wide(*shape):
        return pltpu.VMEM(shape, F32)

    return pl.pallas_call(
        widen_kernel,
        in_specs=[vm] * 7,
        out_specs=[far_off] * 8,
        out_shape=(
            like(WIDTH, WIDTH), like(WIDTH, WIDTH), like(3, WIDTH, LOCAL), like(LOCAL, WIDTH),
            jax.ShapeDtypeStruct((ALL_ROWS, WIDTH), BF16), like(ALL_ROWS, WIDTH),
            like(2, WIDTH), like(HEADS, DIM),
        ),
        scratch_shapes=[
            wide(WIDTH, WIDTH), wide(WIDTH, WIDTH), wide(3, WIDTH, LOCAL), wide(4, 128, 512),
            pltpu.SemaphoreType.DMA((4, 4)), pltpu.SemaphoreType.DMA((4,)),
        ],
        compiler_params=pltpu.CompilerParams(vmem_limit_bytes=40 * 2**20),
        name="widen",
    )(grads, attn, out_part, acts, in_grads, gains, feats)


def per_device(
    tokens, lengths, cotangent, qkv_weight, out_weight, up_weight, down_weight, norm_gains,
    feat_weights,
):
    acts, in_grads, grads, attn, out_part, gains, feats = layers(
        lengths, tokens, cotangent, jnp.transpose(qkv_weight[0], (1, 0, 2)), out_weight[0],
        up_weight[0], down_weight[0], norm_gains[0], feat_weights[0],
    )
    down, up, qkv, out, acts, in_grads, gains, feats = widen(
        grads, attn, out_part, acts, in_grads, gains, feats
    )
    qkv = jnp.transpose(qkv, (1, 0, 2))
    return tuple(one[None] for one in (acts, in_grads, qkv, out, up, down, gains, feats))


PLACED = (
    P("dp", None),
    P("dp", None),
    P("dp", None),
    P("section", None, None, "tensor"),
    P("section", "tensor", None),
    P("section", None, "tensor"),
    P("section", "tensor", None),
    P("section", None, None),
    P("section", "tensor", None),
)
GIVEN = (
    P("section", "dp", None),
    P("section", "dp", None),
    P("section", None, None, "tensor"),
    P("section", "tensor", None),
    P("section", None, "tensor"),
    P("section", "tensor", None),
    P("section", None, None),
    P("section", "tensor", None),
)


def solution(mesh):
    return jax.shard_map(
        per_device, mesh=mesh, in_specs=PLACED, out_specs=GIVEN, check_vma=False
    )
```

```python
import functools
import math

import jax
import jax.numpy as jnp
import numpy as np
from jax import lax
from jax.experimental import pallas as pl
from jax.experimental.pallas import tpu as pltpu
from jax.sharding import PartitionSpec as P

F32 = jnp.float32
BF16 = jnp.bfloat16
MESH = pl.DeviceIdType.MESH
EPS = 1e-05
ROWS = 256
HALF = 128
WIDTH = 1024
LOCAL = 256
HEADS = 4
DIM = 64
ROT = 16
MICROS = 2
ALL_ROWS = MICROS * ROWS


def feature_table(head_dim, feat_count):
    golden = 0.6180339887498949
    row_grid = np.arange(feat_count)[:, None] + 0.5
    columns = np.arange(head_dim)[None, :] * 1.0
    points = np.mod(row_grid * (2.0 * columns + 1.0) / feat_count + golden * columns, 1.0)
    radius = np.sqrt(-2.0 * np.log(points[:, 0::2]))
    turning = 2.0 * np.pi * points[:, 1::2]
    omega_rows = np.stack([radius * np.cos(turning), radius * np.sin(turning)], axis=2).reshape(
        feat_count, head_dim
    )
    frequency = np.arange(head_dim)[:, None] * 1.0
    cosine_basis = np.sqrt(2.0 / head_dim) * np.cos(
        np.pi * (2.0 * columns + 1.0) * frequency / (2.0 * head_dim)
    )
    cosine_basis = np.where(frequency == 0, np.sqrt(0.5), 1.0) * cosine_basis
    return np.sum(omega_rows[:, :, None] * cosine_basis[None, :, :], axis=1)


def low_pieces(values):
    high = values.astype(BF16)
    rest = (values - high.astype(values.dtype)).astype(BF16)
    return high, rest


def constants():
    table = feature_table(DIM, DIM).astype(np.float32)
    eye = np.eye(HEADS, dtype=np.float32)
    blocks = np.kron(eye, table.T / math.sqrt(DIM)).astype(np.float32)
    ones = np.kron(eye, np.ones((DIM, DIM), np.float32))
    high, rest = low_pieces(blocks)
    scaled = (ones * (-1.0 / (2.0 * DIM))).astype(BF16)
    forward = np.concatenate([high, high, rest, scaled, scaled], axis=0)
    backward = np.concatenate([blocks.T.astype(BF16), (ones / DIM).astype(BF16)], axis=1)
    half_rot = ROT // 2
    inverse = (10000.0 ** (-2.0 * np.arange(half_rot) / ROT)).astype(np.float32)
    angles = np.arange(ROWS, dtype=np.float32)[:, None] * inverse[None, :]
    cosine = np.ones((ROWS, DIM), np.float32)
    sine = np.zeros((ROWS, DIM), np.float32)
    for start in (0, half_rot):
        cosine[:, start : start + half_rot] = np.cos(angles.astype(np.float64))
        sine[:, start : start + half_rot] = np.sin(angles.astype(np.float64))
    cosine = np.tile(cosine, (1, HEADS))
    sine = np.tile(sine, (1, HEADS))
    turns = np.concatenate([*low_pieces(cosine), *low_pieces(sine)], axis=1)
    spread = np.tile(np.eye(DIM, dtype=np.float32), (1, HEADS))
    return np.concatenate(
        [
            *np.split(turns, 4, axis=1), forward, *np.split(backward, 2, axis=1), ones.astype(BF16),
            spread.astype(BF16),
        ],
        axis=0,
    )


def dot_nn(a, b):
    return lax.dot_general(a, b, (((1,), (0,)), ((), ())), preferred_element_type=F32)


def dot_nt(a, b):
    return lax.dot_general(a, b, (((1,), (1,)), ((), ())), preferred_element_type=F32)


def dot_exact(a, b, side):
    return lax.dot_general(
        a, b, (((1,), (side,)), ((), ())), preferred_element_type=F32,
        precision=lax.Precision.HIGHEST,
    )


def dot_tn(a, b):
    return lax.dot_general(a, b, (((0,), (0,)), ((), ())), preferred_element_type=F32)


def normal_cdf(v):
    bell = jnp.exp(-0.5 * v * v)
    t = pl.reciprocal(1.0 + (0.3275911 * math.sqrt(0.5)) * jnp.abs(v))
    poly = 0.5 * 1.061405429 * t - 0.5 * 1.453152027
    for coefficient in (1.421413741, -0.284496736, 0.254829592):
        poly = poly * t + 0.5 * coefficient
    tail = poly * t * bell
    cdf = jnp.where(v >= 0.0, 1.0 - tail, tail)
    return cdf, cdf + v * bell * (1.0 / math.sqrt(2.0 * math.pi))


def ln_rows(x):
    mean = jnp.mean(x, axis=-1, keepdims=True)
    centered = x - mean
    inv = lax.rsqrt(jnp.mean(centered * centered, axis=-1, keepdims=True) + EPS)
    return centered * inv, inv


def ln_back(combined, normed, inv):
    mean_c = jnp.mean(combined, axis=-1, keepdims=True)
    mean_p = jnp.mean(combined * normed, axis=-1, keepdims=True)
    return inv * (combined - mean_c - normed * mean_p)


DOWN, UP, ATTN, OUT = range(4)
ORDER = (
    (DOWN, 2), (ATTN, 1), (UP, 2), (OUT, 0), (DOWN, 3), (ATTN, 2),
    (OUT, 1), (UP, 3), (OUT, 2), (ATTN, 3), (OUT, 3), (DOWN, 4),
    (OUT, 4), (UP, 4), (OUT, 5), (ATTN, 4), (OUT, 6), (DOWN, 5),
    (UP, 5), (ATTN, 5), (DOWN, 6), (UP, 6), (ATTN, 6),
)


def wrap(v):
    return lax.rem(v + 8, 4)


class Sums:
    LAST = 6

    def __init__(self, own, g, row0, near, far, sent, got, place, at):
        self.own, self.g, self.row0, self.at = own, g, row0, at
        self.near, self.far, self.sent, self.got, self.place = near, far, sent, got, place

    def ends(self, q):
        axis1, axis2 = ("x", "y") if q == 0 else ("y", "x")
        return axis1, axis2, self.place[axis1], self.place[axis2]

    def half(self, q, b, h):
        return pl.ds(pl.multiple_of(self.row0 + q * 512 + b * 128 + h * 64, 64), 64)

    def piece(self, q, k):
        _, _, p1, _ = self.ends(q)
        return pl.ds(pl.multiple_of(self.row0 + q * 512 + p1 * 128 + k * 32, 32), 32)

    def near_piece(self, q, k):
        return (q, 2 + k // 2, pl.ds(pl.multiple_of(lax.rem(k, 2) * 32, 32), 32))

    def copies(self, q, t):
        axis1, axis2, p1, p2 = self.ends(q)
        near, own, g = self.near, self.own, self.g
        up, down = (axis1, 1), (axis1, 3)
        if t == 0:
            plan = [
                (own.at[self.half(q, wrap(p1 + 2), 0)], near.at[q, 0], up, 0),
                (own.at[self.half(q, wrap(p1 + 2), 1)], near.at[q, 1], down, 0),
                (own.at[self.half(q, wrap(p1 + 1), 1)], near.at[q, 3], up, 1),
                (own.at[self.half(q, wrap(p1 - 1), 0)], near.at[q, 2], down, 1),
            ]
        elif t == 1:
            plan = [(near.at[q, 0], near.at[q, 4], up, 2), (near.at[q, 1], near.at[q, 5], down, 2)]
        elif t == 2:
            plan = [
                (near.at[self.near_piece(q, wrap(p2 + k + 1))], self.far.at[q, k], (axis2, k + 1), 3)
                for k in range(3)
            ]
        elif t == 3:
            src = g.at[self.piece(q, p2)]
            plan = [(src, src, (axis2, k + 1), 4) for k in range(3)]
        elif t == 4:
            first, second = g.at[self.half(q, p1, 0)], g.at[self.half(q, p1, 1)]
            plan = [
                (first, first, up, 5), (second, second, down, 5),
                (second, second, up, 6), (first, first, down, 6),
            ]
        else:
            first = g.at[self.half(q, wrap(p1 - 1), 0)]
            second = g.at[self.half(q, wrap(p1 + 1), 1)]
            plan = [(first, first, up, 7), (second, second, down, 7)]
        return [
            pltpu.make_async_remote_copy(
                src_ref=src, dst_ref=dst, send_sem=self.sent, recv_sem=self.got.at[k],
                device_id=self.at(*target), device_id_type=MESH,
            )
            for src, dst, target, k in plan
        ]

    def wait(self, k):
        if k < 3:
            all_of = self.near.at[:, 2 * k : 2 * k + 2]
        elif k == 3:
            all_of = self.far
        else:
            all_of = self.g.at[self.row0 : self.row0 + (192 if k == 4 else 256)]
        pltpu.make_async_copy(all_of, all_of, self.got.at[k]).wait()

    def start(self, q, t):
        _, _, p1, p2 = self.ends(q)
        near, own = self.near, self.own
        if t == 1:
            near[q, 0] = near[q, 0] + own[self.half(q, wrap(p1 + 1), 0), :]
            near[q, 1] = near[q, 1] + own[self.half(q, wrap(p1 - 1), 1), :]
        elif t == 2:
            for h in range(2):
                total = near[q, 2 + h].astype(F32) + near[q, 4 + h].astype(F32)
                near[q, 2 + h] = (total + own[self.half(q, p1, h), :].astype(F32)).astype(BF16)
        elif t == 3:
            total = near[self.near_piece(q, p2)].astype(F32) + self.far[q, 0].astype(F32)
            total = total + (self.far[q, 1].astype(F32) + self.far[q, 2].astype(F32))
            self.g[self.piece(q, p2), :] = total.astype(BF16)
        for one in self.copies(q, t):
            one.start()

    def step(self, t):
        for k in ((), (0,), (1, 2), (3,), (4,), (5,), (6, 7))[t]:
            self.wait(k)
        if t < self.LAST:
            for q in range(2):
                self.start(q, t)

    def finish(self, ref):
        rows = 2 * (12 * 64 + 6 * 32) * self.own.shape[1] // WIDTH
        pltpu.make_async_copy(ref.at[0:rows], ref.at[0:rows], self.sent).wait()


def layers_kernel(
    lens_h, tok_h, cot_h, wqkv_h, wout_h, wup_h, wdown_h, gains_h, feats_h, cst_h,
    acts, in_grads, gsum, csum, esum, gain_out, feat_out,
    lens, xin, glow, aux, wqkv, wout, wup, wdown, gains, feats, cst, gbuf, cbuf, ebuf, near, near_c, near_e, far, far_c, far_e,
    fw, mask, rot, nrm, attn_in, mlp_in, tq, tk, pq, pk, qf, kf, vf, sb, den, att,
    mixed, hidden, ghp, gm, gproj, gpre, nx, inv_x,
    fpart, frx, fcs, fin, bpart, brx, bcs, bin_, xrx, small, srx, sall,
    load_s, frx_s, fin_s, facts_s, brx_s, bin_s, bout_s, x_s, xsib_s, ret_s, small_s,
    sent_s, got_s, all_s, give_s, give_back_s,
):
    s = lax.axis_index("section")
    t = lax.axis_index("tensor")
    dp = lax.axis_index("dp")
    zh = t // 2
    c = lax.rem(t, 2)
    sibling = {"tensor": zh * 2 + 1 - c}
    partner = {"tensor": lax.rem(t + 2, 4)}
    across = [{"section": 1 - s, "tensor": z * 2 + c} for z in range(2)]
    place = {"x": dp // 4, "y": lax.rem(dp, 4)}

    def at(axis, d):
        there = dict(place)
        there[axis] = lax.rem(place[axis] + d + 4, 4)
        return {"dp": there["x"] * 4 + there["y"]}

    def load(src, dst, k):
        return pltpu.make_async_copy(src, dst, load_s.at[k])

    first, second = slice(0, ROWS), slice(ROWS, ALL_ROWS)
    load_lens = load(lens_h, lens, 12)
    load_gains = load(gains_h, gains, 0)
    load_feats = load(feats_h, feats, 1)
    load_cst = load(cst_h, cst, 2)
    load_qkv = [load(wqkv_h.at[k], wqkv.at[k], 3 + k) for k in range(3)]
    load_up = load(wup_h, wup, 6)
    load_out = load(wout_h, wout, 7)
    load_down = load(wdown_h, wdown, 8)

    @pl.when(s == 0)
    def _():
        load(tok_h.at[first], xin.at[first], 9).start()
        for one in (load_gains, load_lens, load_feats, load_cst, *load_qkv):
            one.start()

    @pl.when(s == 1)
    def _():
        load(cot_h, glow, 9).start()
        for one in (load_down, load_out, load_lens, load_cst, load_gains, load_feats, *load_qkv, load_up):
            one.start()
        load(tok_h, aux, 11).start()

    barrier = pltpu.get_barrier_semaphore()
    peers = [sibling, partner, *across] + [at(axis, d) for axis in ("x", "y") for d in (1, 2, 3)]
    for target in peers:
        pl.semaphore_signal(barrier, inc=1, device_id=target, device_id_type=MESH)

    def remote(src, dst, sems, index, target):
        return pltpu.make_async_remote_copy(
            src_ref=src, dst_ref=dst, send_sem=sems.at[(0, *index)],
            recv_sem=sems.at[(1, *index)], device_id=target, device_id_type=MESH,
        )

    def micro_rows(m):
        if isinstance(m, int):
            return slice(m * ROWS, (m + 1) * ROWS)
        return pl.ds(pl.multiple_of(m * ROWS, ROWS), ROWS)

    def half_rows(m):
        return pl.ds(pl.multiple_of(m * ROWS + c * HALF, HALF), HALF)

    def part_rows(m, core, k):
        return pl.ds(pl.multiple_of(m * ROWS + core * HALF + k * 64, 64), 64)

    keep_rows = pl.ds(pl.multiple_of(c * HALF, HALF), HALF)
    give_rows = pl.ds(pl.multiple_of((1 - c) * HALF, HALF), HALF)

    def cols(n):
        return slice(n * 256, (n + 1) * 256)

    def f_swap(m):
        return remote(fpart.at[m, give_rows], frx.at[m], frx_s, (m,), sibling)

    def f_spread(m):
        return remote(fcs.at[m], fin.at[m], fin_s, (m,), partner)

    def f_share(m):
        return remote(acts.at[half_rows(m)], acts.at[half_rows(m)], facts_s, (m,), sibling)

    def b_swap(m):
        return remote(bpart.at[m, give_rows], brx.at[m], brx_s, (m,), sibling)

    def b_spread(m):
        return remote(bcs.at[m], bin_.at[m], bin_s, (m,), partner)

    def b_share(m):
        return remote(in_grads.at[half_rows(m)], in_grads.at[half_rows(m)], bout_s, (m,), sibling)

    def cross(src, m, z, k, arrival=False):
        here = z if arrival else zh
        rows = slice(k * 64, (k + 1) * 64)
        return pltpu.make_async_remote_copy(
            src_ref=src.at[m, rows], dst_ref=xrx.at[m, here, rows], send_sem=x_s.at[0, m, z, k],
            recv_sem=x_s.at[1, m, here, k], device_id=across[z], device_id_type=MESH,
        )

    def send_back(m, z, arrival=False):
        rows = part_rows(m, c, z if arrival else zh)
        return pltpu.make_async_remote_copy(
            src_ref=xin.at[rows], dst_ref=acts.at[rows], send_sem=ret_s.at[0, m, z],
            recv_sem=ret_s.at[1, m, z if arrival else zh], device_id=across[z], device_id_type=MESH,
        )

    def x_share(buf, m, k):
        rows = part_rows(m, c, k)
        return remote(buf.at[rows], buf.at[rows], xsib_s, (m, k), sibling)

    def chip_sum(part, rx, cs, m):
        cs[m] = (part[m, keep_rows].astype(F32) + rx[m].astype(F32)).astype(BF16)

    def send_across(cs, m):
        for k in range(2):
            for z in range(2):
                cross(cs, m, z, k).start()

    def arrived(src, m, k):
        for z in range(2):
            cross(src, m, z, k, arrival=True).wait_recv()
        rows = slice(k * 64, (k + 1) * 64)
        return xrx[m, 0, rows].astype(F32) + xrx[m, 1, rows].astype(F32)

    def context(m):
        length = lens[pl.ds(m, 1), :]
        first_end = length[:, 0:1]
        second_end = first_end + length[:, 1:2]
        third_end = second_end + length[:, 2:3]
        i = lax.broadcasted_iota(jnp.int32, (ROWS, ROWS), 0)
        j = lax.broadcasted_iota(jnp.int32, (ROWS, ROWS), 1)
        start = jnp.where(i >= first_end, first_end, 0)
        start = jnp.where(i >= second_end, second_end, start)
        start = jnp.where(i >= third_end, third_end, start)
        mask[m] = ((j <= i) & (j >= start)).astype(F32)
        hot = ((i - start) == j).astype(F32).astype(BF16)
        cosine = dot_nn(hot, cst[0:256, :]) + dot_nn(hot, cst[256:512, :])
        sine = dot_nn(hot, cst[512:768, :]) + dot_nn(hot, cst[768:1024, :])
        column = lax.rem(j, DIM)
        rot[m, 0] = cosine
        rot[m, 1] = jnp.where(column < ROT // 2, -sine, 0.0)
        rot[m, 2] = jnp.where(column >= ROT // 2, sine, 0.0)

    def norm_rows(rows):
        normed, _ = ln_rows(xin[rows, :].astype(F32))
        nrm[rows, :] = normed
        attn_in[rows, :] = (normed * gains[0:1, :]).astype(BF16)
        mlp_in[rows, :] = (normed * gains[1:2, :]).astype(BF16)

    def features(projected, m, turned_ref, phi_ref, low_ref):
        turned = (
            projected * rot[m, 0]
            + pltpu.roll(projected, LOCAL - ROT // 2, 1) * rot[m, 1]
            + pltpu.roll(projected, ROT // 2, 1) * rot[m, 2]
        )
        turned_ref[m] = turned
        high, rest = low_pieces(turned)
        square_high, square_rest = low_pieces(turned * turned)
        pieces = jnp.concatenate([high, rest, high, square_high, square_rest], axis=1)
        phi = fw[...] * jnp.exp(dot_nn(pieces, cst[1024:2304, :]))
        phi_ref[m] = phi
        low_ref[m] = phi.astype(BF16)

    def head_row(h):
        return cst[2816 + h * DIM : 2817 + h * DIM, :]

    def attend(m, up):
        queries, keys, values = qf[m], kf[m], vf[m]
        kept = mask[m] > 0.5
        total = jnp.zeros((ROWS, 2 * LOCAL), F32)
        for h in range(HEADS):
            row = head_row(h)
            scores = jnp.where(kept, dot_nt(queries * row, keys), 0.0).astype(BF16)
            sb[m, h] = scores
            right = jnp.concatenate(
                [values * row, jnp.broadcast_to(row, (ROWS, LOCAL))], axis=1
            )
            total = total + dot_nn(scores, right)
            if h % 2 == 0:
                up(2 + h // 2)
        norm = total[:, LOCAL:]
        attended = total[:, :LOCAL] / norm
        den[m] = norm
        att[m] = attended
        mixed[micro_rows(m), :] = attended.astype(BF16)

    def front(m):
        rows = micro_rows(m)
        normed_low = attn_in[rows, :]

        def up(n):
            pre = dot_nn(mlp_in[rows, :], wup[:, cols(n)])
            cdf, slope = normal_cdf(pre)
            hidden[rows, cols(n)] = (pre * cdf).astype(BF16)
            gpre[rows, cols(n)] = (ghp[rows, cols(n)] * slope).astype(BF16)
            ghp[rows, cols(n)] = slope

        queries = dot_nn(normed_low, wqkv[0])
        keys = dot_nn(normed_low, wqkv[1])
        up(0)
        features(queries, m, tq, pq, qf)
        up(1)
        features(keys, m, tk, pk, kf)
        vf[m] = dot_nn(normed_low, wqkv[2]).astype(BF16)
        attend(m, up)

    def back_out(m):
        rows = micro_rows(m)
        for n in range(4):
            tile = dot_nn(mixed[rows, :], wout[:, cols(n)])
            tile = tile + dot_nn(hidden[rows, :], wdown[:, cols(n)])
            fpart[m, :, cols(n)] = tile.astype(BF16)

    def grad_hidden(m, known):
        rows = micro_rows(m)
        for n in range(4):
            grad = dot_nt(glow[rows, :], wdown[cols(n), :])
            if known:
                gpre[rows, cols(n)] = (grad * ghp[rows, cols(n)]).astype(BF16)
            else:
                ghp[rows, cols(n)] = grad

    def grad_mixed(m):
        rows = micro_rows(m)
        gm[rows, :] = dot_nt(glow[rows, :], wout[...]).astype(BF16)

    def feature_back(grad_phi, m, turned_ref, phi_ref):
        grad_s = grad_phi * phi_ref[m]
        small[0, 2:3, 0:LOCAL] = small[0, 2:3, 0:LOCAL] + jnp.sum(grad_s, axis=0, keepdims=True)
        low = grad_s.astype(BF16)
        grad = dot_nn(low, cst[2304:2560, :]) - turned_ref[m] * dot_nn(low, cst[2560:2816, :])
        return (
            grad * rot[m, 0]
            - pltpu.roll(grad, LOCAL - ROT // 2, 1) * rot[m, 1]
            - pltpu.roll(grad, ROT // 2, 1) * rot[m, 2]
        )

    def attend_back(m):
        rows = micro_rows(m)
        grad_num = gm[rows, :].astype(F32) / den[m]
        grad_low = grad_num.astype(BF16)
        high, rest = low_pieces(grad_low.astype(F32) * att[m])
        ones = cst[2816:3072, :]
        grad_den = -(dot_nn(high, ones) + dot_nn(rest, ones))
        kept = mask[m] > 0.5
        queries, keys, values = qf[m], kf[m], vf[m]
        grad_q = jnp.zeros((ROWS, LOCAL), F32)
        grad_k = jnp.zeros((ROWS, LOCAL), F32)
        grad_v = jnp.zeros((ROWS, LOCAL), F32)
        for h in range(HEADS):
            row = head_row(h)
            given = grad_low * row
            grad_scores = dot_nt(given, values) + grad_den[:, h * DIM : h * DIM + 1]
            grad_scores = jnp.where(kept, grad_scores, 0.0).astype(BF16)
            grad_q = grad_q + dot_nn(grad_scores, keys * row)
            grad_k = grad_k + dot_tn(grad_scores, queries * row)
            grad_v = grad_v + dot_tn(sb[m, h], given)
            here = cols(h)
            grad_m = dot_nt(gpre[rows, :], wup[here, :])
            ghp[rows, here] = gains[1:2, here] * grad_m
            line = jnp.sum(nrm[rows, here] * grad_m, axis=0, keepdims=True)
            small[0, 1:2, here] = small[0, 1:2, here] + line
        gproj[0, rows, :] = feature_back(grad_q, m, tq, pq).astype(BF16)
        gproj[1, rows, :] = feature_back(grad_k, m, tk, pk).astype(BF16)
        gproj[2, rows, :] = grad_v.astype(BF16)

    def back_in(m):
        rows = micro_rows(m)
        for n in range(4):
            here = cols(n)
            grad_a = dot_nt(gproj[0, rows, :], wqkv[0, here, :])
            grad_a = grad_a + dot_nt(gproj[1, rows, :], wqkv[1, here, :])
            grad_a = grad_a + dot_nt(gproj[2, rows, :], wqkv[2, here, :])
            bpart[m, :, here] = (gains[0:1, here] * grad_a + ghp[rows, here]).astype(BF16)
            line = jnp.sum(nrm[rows, here] * grad_a, axis=0, keepdims=True)
            small[0, 0:1, here] = small[0, 0:1, here] + line

    def grads_down(n):
        gbuf[cols(n), :] = dot_tn(hidden[:, cols(n)], glow[...]).astype(BF16)
        if n % 2 == 1:
            sums[DOWN].start(n // 2, 0)

    def grads_up(n):
        rows = slice(1024 + n * 256, 1280 + n * 256)
        gbuf[rows, :] = dot_tn(mlp_in[:, cols(n)], gpre[...]).astype(BF16)
        if n % 2 == 1:
            sums[UP].start(n // 2, 0)

    def grads_attn(n):
        for k in range(3):
            cbuf[cols(n), cols(k)] = dot_tn(attn_in[:, cols(n)], gproj[k]).astype(BF16)
        if n % 2 == 1:
            sums[ATTN].start(n // 2, 0)

    def grads_out():
        for z in range(2):
            part = dot_tn(mixed[...], glow[:, z * 512 : (z + 1) * 512])
            ebuf[512 + z * 256 : 768 + z * 256, :] = part.astype(BF16)

    def finish_forward(m):
        f_spread(m).wait_recv()
        total = fcs[m].astype(F32) + fin[m].astype(F32)
        acts[half_rows(m), :] = (xin[half_rows(m), :].astype(F32) + total).astype(BF16)
        f_share(m).start()

    def finish_backward(m):
        b_spread(m).wait_recv()
        total = bcs[m].astype(F32) + bin_[m].astype(F32)
        normed, inv = ln_rows(xin[half_rows(m), :].astype(F32))
        in_grads[half_rows(m), :] = glow[half_rows(m), :].astype(F32) + ln_back(total, normed, inv)
        b_share(m).start()

    sums = [
        Sums(own, total, row0, *scratch, sent_s.at[j], got_s.at[j], place, at)
        for j, (own, total, row0, scratch) in enumerate(
            (
                (gbuf, gsum, 0, (near.at[0], far.at[0])),
                (gbuf, gsum, 1024, (near.at[1], far.at[1])),
                (cbuf, csum, 0, (near_c, far_c)),
                (ebuf, esum, 0, (near_e, far_e)),
            )
        )
    ]

    def give(z, arrival=False):
        place_there = z if arrival else zh
        return pltpu.make_async_remote_copy(
            src_ref=ebuf.at[512 + z * 256 : 768 + z * 256],
            dst_ref=ebuf.at[pl.ds(pl.multiple_of(place_there * 256, 256), 256)],
            send_sem=give_s.at[0, z], recv_sem=give_s.at[1, place_there],
            device_id=across[z], device_id_type=MESH,
        )

    def give_back(z, arrival=False):
        place_there = z if arrival else zh
        return pltpu.make_async_remote_copy(
            src_ref=esum.at[z * 256 : (z + 1) * 256],
            dst_ref=esum.at[pl.ds(pl.multiple_of(512 + place_there * 256, 256), 256)],
            send_sem=give_back_s.at[0, z], recv_sem=give_back_s.at[1, place_there],
            device_id=across[z], device_id_type=MESH,
        )

    def hop(j, step):
        sums[j].step(step)

    def small_step(k):
        def copy(k):
            if k < 2:
                return [remote(small.at[k], srx.at[k], small_s, (k,), (sibling, partner)[k])]
            axis = "xy"[k - 2]
            return [
                pltpu.make_async_remote_copy(
                    src_ref=small.at[k], dst_ref=sall.at[k - 2, place[axis]],
                    send_sem=all_s.at[0, k - 2], recv_sem=all_s.at[1, k - 2],
                    device_id=at(axis, d), device_id_type=MESH,
                )
                for d in (1, 2, 3)
            ]

        if k == -1:
            for j in range(2):
                copy(j)[0].wait_send()
                three = sall.at[j, 0:3]
                pltpu.make_async_copy(three, three, all_s.at[0, j]).wait()
            return
        if k in (1, 2):
            copy(k - 1)[0].wait_recv()
        if k > 2:
            three = sall.at[k - 3, 0:3]
            pltpu.make_async_copy(three, three, all_s.at[1, k - 3]).wait()
        if k in (1, 2):
            line = lax.broadcasted_iota(jnp.int32, (8, WIDTH), 0)
            small[k] = small[k - 1] + jnp.where(line < 2, srx[k - 1], 0.0)
        if k in (3, 4):
            parts = sall[k - 3]
            small[k] = (parts[0] + parts[1]) + (parts[2] + parts[3])
        if k in (2, 3):
            sall[k - 2, place["xy"[k - 2]]] = small[k]
        if k < 4:
            for one in copy(k):
                one.start()

    def spread_feats():
        exact = dot_exact(feats[...], cst[3072:3136, :].astype(F32), 0)
        fw[...] = jnp.sum(exact * heads_of(), axis=0, keepdims=True)

    def heads_of():
        return jnp.concatenate([head_row(h) for h in range(HEADS)], axis=0).astype(F32)

    def wait_all(*copies):
        for one in copies:
            one.wait()

    small[...] = jnp.zeros(small.shape, F32)

    @pl.when(s == 0)
    def _():
        def forward(m, carry):
            @pl.when(m == 0)
            def _():
                wait_all(load(tok_h.at[first], xin.at[first], 9), load_gains)
                for one in (load_up, load_out, load_down, load(tok_h.at[second], xin.at[second], 10)):
                    one.start()
                load(cot_h, aux, 11).start()

            for k in range(4):
                norm_rows(pl.ds(pl.multiple_of(m * ROWS + k * 64, 64), 64))

            @pl.when(m == 0)
            def _():
                wait_all(load_lens, load_feats, load_cst)
                spread_feats()

            context(m)

            @pl.when(m == 0)
            def _():
                wait_all(*load_qkv, load_up)

            front(m)

            @pl.when(m == 0)
            def _():
                wait_all(load_out, load_down)

            back_out(m)

            @pl.when(m == 0)
            def _():
                pl.semaphore_wait(barrier, len(peers))

            f_swap(m).start()

            @pl.when(m == 0)
            def _():
                wait_all(load(tok_h.at[second], xin.at[second], 10), load(cot_h, aux, 11))

            f_swap(m).wait_recv()
            chip_sum(fpart, frx, fcs, m)
            send_across(fcs, m)
            return carry

        lax.fori_loop(0, MICROS, forward, 0)

        def gradient_in(m):
            for z in range(2):
                send_back(m, z, arrival=True).wait_recv()
            normed, inv = ln_rows(acts[half_rows(m), :].astype(F32))
            nx[m] = normed
            inv_x[m] = jnp.broadcast_to(inv, (HALF, 128))
            f_share(m).start()
            for k in range(2):
                total = arrived(bcs, m, k)
                rows = slice(k * 64, (k + 1) * 64)
                back = ln_back(total, nx[m, rows], inv_x[m, rows, 0:1])
                grad = aux[part_rows(m, c, k), :].astype(F32) + back
                glow[part_rows(m, c, k), :] = grad.astype(BF16)
                x_share(glow, m, k).start()
            for k in range(2):
                x_share(glow, m, k).wait_recv()

        def backward(m, carry):
            last = m == MICROS - 1
            gradient_in(m)

            @pl.when(last)
            def _():
                for n in range(4):
                    grads_down(n)
                grads_out()
                for z in range(2):
                    give(z).start()

            grad_hidden(m, True)

            @pl.when(last)
            def _():
                for n in range(4):
                    grads_up(n)

            grad_mixed(m)
            attend_back(m)

            @pl.when(last)
            def _():
                hop(0, 1)
                for n in range(4):
                    grads_attn(n)

            back_in(m)
            b_swap(m).start()
            return carry

        lax.fori_loop(0, MICROS, backward, 0)
        hop(1, 1)
        for m in range(MICROS):
            for k in range(2):
                x_share(glow, m, k).wait_send()
                for z in range(2):
                    cross(fcs, m, z, k).wait_send()

    @pl.when(s == 1)
    def _():
        wait_all(load(cot_h, glow, 9), load_down)
        for m in range(MICROS):
            grad_hidden(m, False)
        wait_all(load_out, load_lens, load_cst, load_gains, load_feats)
        spread_feats()
        for m in range(MICROS):
            grad_mixed(m)
            context(m)
        wait_all(*load_qkv, load_up, load(tok_h, aux, 11))
        pl.semaphore_wait(barrier, len(peers))

        def cross_over(m):
            b_swap(m).wait_recv()
            chip_sum(bpart, brx, bcs, m)
            send_across(bcs, m)

        def take_in(m, k):
            total = arrived(fcs, m, k)
            own = part_rows(m, c, k)
            xin[own, :] = (aux[own, :].astype(F32) + total).astype(BF16)
            x_share(xin, m, k).start()

        def both(m, carry):
            @pl.when(m == 0)
            def _():
                for k in range(2):
                    take_in(0, k)
                    norm_rows(part_rows(0, c, k))
                for z in range(2):
                    send_back(0, z).start()

            @pl.when(m == 1)
            def _():
                for k in range(2):
                    norm_rows(part_rows(1, c, k))

            for k in range(2):
                x_share(xin, m, k).wait_recv()
                norm_rows(part_rows(m, 1 - c, k))

            @pl.when(m == 1)
            def _():
                cross_over(0)

            front(m)
            attend_back(m)

            @pl.when(m == 0)
            def _():
                for k in range(2):
                    take_in(1, k)
                for z in range(2):
                    send_back(1, z).start()

            back_in(m)
            b_swap(m).start()
            return carry

        lax.fori_loop(0, MICROS, both, 0)
        grads_down(0)
        grads_down(1)
        cross_over(1)
        grads_down(2)
        grads_down(3)
        for n in range(4):
            grads_up(n)
        hop(0, 1)
        for n in range(4):
            grads_attn(n)
        grads_out()
        hop(1, 1)
        for m in range(MICROS):
            for z in range(2):
                for k in range(2):
                    cross(bcs, m, z, k).wait_send()
        for m in range(MICROS):
            for k in range(2):
                x_share(xin, m, k).wait_send()
                send_back(m, k).wait_send()

    small_step(0)
    for part, step in ORDER:
        if part == OUT:

            @pl.when(s == 1)
            def _():
                if step == 0:
                    for m in range(MICROS):
                        back_out(m)
                        f_swap(m).start()
                    for z in range(2):
                        give(z, arrival=True).wait_recv()
                    for q in range(2):
                        sums[OUT].start(q, 0)
                else:
                    hop(OUT, step)
                if step == Sums.LAST:
                    for z in range(2):
                        give_back(z).start()

            continue
        if (part, step) == (UP, 3):

            @pl.when(s == 0)
            def _():
                for m in range(MICROS):
                    b_swap(m).wait_recv()
                    chip_sum(bpart, brx, bcs, m)

            @pl.when(s == 1)
            def _():
                for m in range(MICROS):
                    f_swap(m).wait_recv()
                    chip_sum(fpart, frx, fcs, m)
                    f_spread(m).start()

            for m in range(MICROS):
                b_spread(m).start()

        if part == DOWN and 2 < step < 6:
            small_step(step - 2)
        hop(part, step)
        if part != ATTN:
            continue
        if step == 4:
            for m in range(MICROS):
                finish_backward(m)

            @pl.when(s == 1)
            def _():
                for m in range(MICROS):
                    finish_forward(m)
                    f_spread(m).wait_send()

        if step == 5:
            small_step(4)
            gain_out[...] = small[4, 0:2, :]
            line = jnp.broadcast_to(small[4, 2:3, 0:LOCAL] / fw[...], (HEADS, LOCAL))
            feat_out[...] = dot_exact(line * heads_of(), cst[3072:3136, :].astype(F32), 1)
            small_step(-1)
            for m in range(MICROS):
                f_share(m).wait_recv()
                b_share(m).wait_recv()
                for one in (f_swap(m), f_share(m), b_swap(m), b_spread(m), b_share(m)):
                    one.wait_send()
    for one in sums[:OUT]:
        one.finish(gbuf)

    @pl.when(s == 0)
    def _():
        for z in range(2):
            give(z).wait_send()
            give_back(z, arrival=True).wait_recv()

    @pl.when(s == 1)
    def _():
        sums[OUT].finish(gbuf)
        for z in range(2):
            give_back(z).wait_send()


def layers(lengths, tok, cot, wqkv, wout, wup, wdown, gains, feats):
    vm = pl.BlockSpec(memory_space=pltpu.VMEM)
    far_off = pl.BlockSpec(memory_space=pl.ANY)

    def low(*shape):
        return pltpu.VMEM(shape, BF16)

    def wide(*shape):
        return pltpu.VMEM(shape, F32)

    full = (MICROS, ROWS, WIDTH)
    half = (MICROS, HALF, WIDTH)
    square = (MICROS, ROWS, LOCAL)
    rows = (ALL_ROWS, WIDTH)
    sems = pltpu.SemaphoreType.DMA
    return pl.pallas_call(
        layers_kernel,
        out_shape=(
            low(*rows), wide(*rows), low(2 * WIDTH, WIDTH), low(WIDTH, 768), low(WIDTH, 512),
            wide(2, WIDTH), wide(HEADS, DIM),
        ),
        in_specs=[far_off] * 10,
        out_specs=(vm,) * 7,
        scratch_shapes=[
            pltpu.VMEM((MICROS, 4), jnp.int32), low(*rows), low(*rows), low(*rows),
            low(3, WIDTH, LOCAL), low(LOCAL, WIDTH), low(WIDTH, WIDTH), low(WIDTH, WIDTH),
            wide(2, WIDTH), wide(HEADS, DIM), low(3136, LOCAL),
            low(2 * WIDTH, WIDTH), low(WIDTH, 768), low(WIDTH, 512),
            low(2, 2, 6, 64, WIDTH), low(2, 6, 64, 768), low(2, 6, 64, 512),
            low(2, 2, 3, 32, WIDTH), low(2, 3, 32, 768), low(2, 3, 32, 512),
            wide(1, LOCAL), wide(*square), wide(MICROS, 3, ROWS, LOCAL),
            wide(*rows), low(*rows), low(*rows),
            wide(*square), wide(*square), wide(*square), wide(*square),
            low(*square), low(*square), low(*square),
            low(MICROS, HEADS, ROWS, ROWS), wide(*square), wide(*square),
            low(ALL_ROWS, LOCAL), low(*rows), wide(*rows), low(ALL_ROWS, LOCAL),
            low(3, ALL_ROWS, LOCAL), low(*rows), wide(*half), wide(MICROS, HALF, 128),
            low(*full), low(*half), low(*half), low(*half),
            low(*full), low(*half), low(*half), low(*half),
            low(MICROS, 2, HALF, WIDTH), wide(5, 8, WIDTH), wide(2, 8, WIDTH), wide(2, 4, 8, WIDTH),
            sems((13,)),
            sems((2, MICROS)), sems((2, MICROS)), sems((2, MICROS)),
            sems((2, MICROS)), sems((2, MICROS)), sems((2, MICROS)),
            sems((2, MICROS, 2, 2)), sems((2, MICROS, 2)), sems((2, MICROS, 2)), sems((2, 2)),
            sems((4,)), sems((4, 8)), sems((2, 2)), sems((2, 2)), sems((2, 2)),
        ],
        compiler_params=pltpu.CompilerParams(
            collective_id=0, has_side_effects=True, vmem_limit_bytes=53 * 2**20
        ),
        name="layers",
    )(lengths, tok, cot, wqkv, wout, wup, wdown, gains, feats, jnp.asarray(constants()))


def widen_kernel(
    grads, attn, out_part, acts, in_grads, gains, feats, o_down, o_up, o_qkv, o_out, o_acts, o_in, o_gains, o_feats,
    down, up, qkv, out, sems, more,
):
    def copies(n):
        rows = pl.ds(pl.multiple_of(n * 256, 256), 256)
        tall = pl.ds(pl.multiple_of(lax.rem(n, 2) * 128, 128), 128)
        broad = pl.ds(pl.multiple_of(n // 2 * 512, 512), 512)
        return [
            pltpu.make_async_copy(down.at[rows], o_down.at[rows], sems.at[0, n]),
            pltpu.make_async_copy(up.at[rows], o_up.at[rows], sems.at[1, n]),
            pltpu.make_async_copy(qkv.at[:, rows], o_qkv.at[:, rows], sems.at[2, n]),
            pltpu.make_async_copy(out.at[n], o_out.at[tall, broad], sems.at[3, n]),
        ]

    whole = [
        pltpu.make_async_copy(src, dst, more.at[k])
        for k, (src, dst) in enumerate(
            ((in_grads, o_in), (acts, o_acts), (gains, o_gains), (feats, o_feats))
        )
    ]
    for one in whole:
        one.start()

    def body(n, carry):
        rows = pl.ds(pl.multiple_of(n * 256, 256), 256)
        first, second, third, fourth = copies(n)
        down[rows, :] = grads[rows, :].astype(F32)
        first.start()
        up[rows, :] = grads[pl.ds(pl.multiple_of(WIDTH + n * 256, 256), 256), :].astype(F32)
        second.start()
        for k in range(3):
            qkv[k, rows, :] = attn[rows, k * 256 : (k + 1) * 256].astype(F32)
        third.start()
        out[n] = out_part[pl.ds(pl.multiple_of(512 + n * 128, 128), 128), :].astype(F32)
        fourth.start()
        return carry

    lax.fori_loop(0, 4, body, 0)
    for n in range(4):
        for one in copies(n):
            one.wait()
    for one in whole:
        one.wait()


def widen(grads, attn, out_part, acts, in_grads, gains, feats):
    vm = pl.BlockSpec(memory_space=pltpu.VMEM)
    far_off = pl.BlockSpec(memory_space=pl.ANY)

    def like(*shape):
        return jax.ShapeDtypeStruct(shape, F32)

    def wide(*shape):
        return pltpu.VMEM(shape, F32)

    return pl.pallas_call(
        widen_kernel,
        in_specs=[vm] * 7,
        out_specs=[far_off] * 8,
        out_shape=(
            like(WIDTH, WIDTH), like(WIDTH, WIDTH), like(3, WIDTH, LOCAL), like(LOCAL, WIDTH),
            jax.ShapeDtypeStruct((ALL_ROWS, WIDTH), BF16), like(ALL_ROWS, WIDTH),
            like(2, WIDTH), like(HEADS, DIM),
        ),
        scratch_shapes=[
            wide(WIDTH, WIDTH), wide(WIDTH, WIDTH), wide(3, WIDTH, LOCAL), wide(4, 128, 512),
            pltpu.SemaphoreType.DMA((4, 4)), pltpu.SemaphoreType.DMA((4,)),
        ],
        compiler_params=pltpu.CompilerParams(vmem_limit_bytes=40 * 2**20),
        name="widen",
    )(grads, attn, out_part, acts, in_grads, gains, feats)


def per_device(
    tokens, lengths, cotangent, qkv_weight, out_weight, up_weight, down_weight, norm_gains,
    feat_weights,
):
    acts, in_grads, grads, attn, out_part, gains, feats = layers(
        lengths, tokens, cotangent, jnp.transpose(qkv_weight[0], (1, 0, 2)), out_weight[0],
        up_weight[0], down_weight[0], norm_gains[0], feat_weights[0],
    )
    down, up, qkv, out, acts, in_grads, gains, feats = widen(
        grads, attn, out_part, acts, in_grads, gains, feats
    )
    qkv = jnp.transpose(qkv, (1, 0, 2))
    return tuple(one[None] for one in (acts, in_grads, qkv, out, up, down, gains, feats))


PLACED = (
    P("dp", None),
    P("dp", None),
    P("dp", None),
    P("section", None, None, "tensor"),
    P("section", "tensor", None),
    P("section", None, "tensor"),
    P("section", "tensor", None),
    P("section", None, None),
    P("section", "tensor", None),
)
GIVEN = (
    P("section", "dp", None),
    P("section", "dp", None),
    P("section", None, None, "tensor"),
    P("section", "tensor", None),
    P("section", None, "tensor"),
    P("section", "tensor", None),
    P("section", None, None),
    P("section", "tensor", None),
)


def solution(mesh):
    return jax.shard_map(
        per_device, mesh=mesh, in_specs=PLACED, out_specs=GIVEN, check_vma=False
    )
```
